32 devices in a mesh: dp: 8 (over y, x, core), mp: 4 (over z).
Axes of the slice: x: 2, y: 2, z: 4, core: 2. Of those that a mesh axis runs over, the one named last changes fastest.
Arguments:
- frames: bfloat16 [11008, 768], P(('dp', 'mp')), may hold values from -6 to 6
- span_mask: int32 [16, 688], P('dp'), may hold values from 0 to 1, as said below
- cotangent: bfloat16 [11008, 768], P(('dp', 'mp')), may hold values from -6 to 6
- qkv_weight: float32 [768, 2304], P('dp', 'mp'), may hold values from -0.21875 to 0.21875
- qkv_mean: float32 [768, 2304], P('dp', 'mp'), may hold values from -0.00061035156 to 0.00061035156
- qkv_square: float32 [768, 2304], P('dp', 'mp'), may hold values from 7.064254e-11 to 1.1302806e-09
- out_weight: float32 [768, 768], P('mp', 'dp'), may hold values from -3.5 to 3.5
- out_mean: float32 [768, 768], P('mp', 'dp'), may hold values from -0.00061035156 to 0.00061035156
- out_square: float32 [768, 768], P('mp', 'dp'), may hold values from 2.8257017e-12 to 4.2385526e-11
- up_weight: float32 [768, 3072], P('dp', 'mp'), may hold values from -0.21875 to 0.21875
- up_mean: float32 [768, 3072], P('dp', 'mp'), may hold values from -0.00061035156 to 0.00061035156
- up_square: float32 [768, 3072], P('dp', 'mp'), may hold values from 7.064254e-11 to 1.1302806e-09
- down_weight: float32 [3072, 768], P('mp', 'dp'), may hold values from -0.109375 to 0.109375
- down_mean: float32 [3072, 768], P('mp', 'dp'), may hold values from -0.00061035156 to 0.00061035156
- down_square: float32 [3072, 768], P('mp', 'dp'), may hold values from 7.064254e-11 to 1.1302806e-09
- head_biases: float32 [12, 384], P('mp', 'dp'), may hold values from -4 to 4
- bias_mean: float32 [12, 384], P('mp', 'dp'), may hold values from -0.00061035156 to 0.00061035156
- bias_square: float32 [12, 384], P('mp', 'dp'), may hold values from 7.064254e-11 to 1.1302806e-09
- norm_vectors: float32 [7, 768], P(None, 'dp'), may hold values from -4 to 4
- vector_mean: float32 [7, 768], P(None, 'dp'), may hold values from -0.00061035156 to 0.00061035156
- vector_square: float32 [7, 768], P(None, 'dp'), may hold values from 7.064254e-11 to 1.1302806e-09
Outputs:
- activations: float32 [11008, 768], P(('dp', 'mp'))
- frame_grad: float32 [11008, 768], P(('dp', 'mp'))
- grad_norm: float32 [], replicated
- qkv_master: float32 [768, 2304], P('dp', 'mp')
- qkv_moment: float32 [768, 2304], P('dp', 'mp')
- qkv_variance: float32 [768, 2304], P('dp', 'mp')
- out_master: float32 [768, 768], P('mp', 'dp')
- out_moment: float32 [768, 768], P('mp', 'dp')
- out_variance: float32 [768, 768], P('mp', 'dp')
- up_master: float32 [768, 3072], P('dp', 'mp')
- up_moment: float32 [768, 3072], P('dp', 'mp')
- up_variance: float32 [768, 3072], P('dp', 'mp')
- down_master: float32 [3072, 768], P('mp', 'dp')
- down_moment: float32 [3072, 768], P('mp', 'dp')
- down_variance: float32 [3072, 768], P('mp', 'dp')
- bias_master: float32 [12, 384], P('mp', 'dp')
- bias_moment: float32 [12, 384], P('mp', 'dp')
- bias_variance: float32 [12, 384], P('mp', 'dp')
- vector_master: float32 [7, 768], P(None, 'dp')
- vector_moment: float32 [7, 768], P(None, 'dp')
- vector_variance: float32 [7, 768], P(None, 'dp')
The draws below stay inside these ranges and needn't reach their ends.
Inputs may be any that keep to these rules, and one draw needn't show every extreme that they name: `span_mask`: masked frames come in spans of 10 consecutive frames begun at random frames of a clip (spans may join or be cut by the clip's end); the share of masked frames differs from clip to clip.
All inputs are finite; a program needn't handle non-finite values.
Results may differ from the reference program's by a relative error of at most 0.017.
Values may be sent and summed in bfloat16 or wider, within the bound.
A program may use at most 128 MiB of HBM per device.

```python
import math
import jax
import jax.numpy as jnp
from jax import lax

D = 768
HEADS = 12
FF = 3072
HD = 64
LEN = 688
CLIPS_DP = 2
CLIPS = 16
TOKENS = 11008


def draw_span_mask(key, part):
    first_key, second_key = jax.random.split(key, 2)
    start_rate = jax.random.randint(first_key, (CLIPS, 1), 20, 111)
    starts = (jax.random.randint(second_key, (CLIPS, LEN), 0, 1000) < start_rate).astype(jnp.int32)
    padded = jnp.pad(starts, ((0, 0), (9, 0)))
    covered = jnp.zeros((CLIPS, LEN), jnp.int32)
    for shift_by in range(10):
        covered = covered + padded[:, shift_by:shift_by + LEN]
    return (covered > 0).astype(jnp.int32)


def draw_norm_vectors(key, part):
    first_key, second_key = jax.random.split(key, 2)
    normal_part = jnp.clip(jax.random.normal(first_key, (7, D), jnp.float32), -4.0, 4.0)
    spread = jax.random.uniform(second_key, (7, D), jnp.float32, -1.0, 1.0)
    row_ids = jnp.arange(7)[:, None]
    gain_rows = (row_ids == 1) | (row_ids == 3)
    embed_part = normal_part
    shifted = jnp.where(gain_rows, 1.0 + 0.25 * spread, 0.3 * normal_part)
    return jnp.where(row_ids == 0, embed_part, shifted).astype(jnp.float32)


def block_levels(own_key, dims, cuts, smallest, high):
    def one(axis_at, blocks):
        heights = jax.random.uniform(jax.random.fold_in(jax.random.fold_in(own_key, 6), axis_at), (blocks,), jnp.float32, smallest / len(cuts), high / len(cuts))
        return jnp.repeat(jnp.exp(heights), dims[axis_at] // blocks).reshape((-1,) + (1,) * (len(dims) - axis_at - 1))

    gain = one(*cuts[0])
    for cut in cuts[1:]:
        gain = gain * one(*cut)
    return gain


def bell_draw(key, extent, scale, most, shards=(), dtype=jnp.bfloat16):
    array = scale * jax.random.normal(key, extent, jnp.float32)
    if shards:
        array = array * block_levels(key, extent, shards, -0.22, 0.18)
    return jnp.clip(array, -most, most).astype(dtype)


def setup_inputs(seed: int = 0) -> dict:
    seeds = jax.random.split(jax.random.key(seed), 22)
    return {
        "frames": bell_draw(seeds[0], (TOKENS, D), 1.0, 6.0, ((0, 32),)),
        "span_mask": draw_span_mask(jax.random.fold_in(seeds[21], 71), 0),
        "cotangent": bell_draw(seeds[2], (TOKENS, D), 1.0, 6.0, ((0, 32),)),
        "qkv_weight": bell_draw(seeds[3], (D, 3 * D), D ** -0.5, 0.21875, ((0, 8), (1, 4)), jnp.float32),
        "qkv_mean": bell_draw(seeds[4], (D, 3 * D), (0.11 / (4 * D * D + 2 * D * FF) ** 0.5), 0.00061035156, ((0, 8), (1, 4)), jnp.float32),
        "qkv_square": jnp.clip(jnp.exp(math.log(1.130280646854942e-09) - 2.7725887 * jax.random.uniform(seeds[5], (D, 3 * D), jnp.float32) ** block_levels(seeds[5], (D, 3 * D), ((0, 8), (1, 4)), -0.2, 0.2)), 7.064254042843388e-11, 1.130280646854942e-09),
        "out_weight": bell_draw(seeds[6], (D, D), (max(3 * D // LEN, 1)) ** -0.5, 3.5, ((0, 4), (1, 8)), jnp.float32),
        "out_mean": bell_draw(seeds[7], (D, D), (0.11 / (4 * D * D + 2 * D * FF) ** 0.5), 0.00061035156, ((0, 4), (1, 8)), jnp.float32),
        "out_square": jnp.clip(jnp.exp(math.log(4.2385525644839106e-11) - 2.7080502 * jax.random.uniform(seeds[8], (D, D), jnp.float32) ** block_levels(seeds[8], (D, D), ((0, 4), (1, 8)), -0.2, 0.2)), 2.8257016951999114e-12, 4.2385525644839106e-11),
        "up_weight": bell_draw(seeds[9], (D, FF), D ** -0.5, 0.21875, ((0, 8), (1, 4)), jnp.float32),
        "up_mean": bell_draw(seeds[10], (D, FF), (0.11 / (4 * D * D + 2 * D * FF) ** 0.5), 0.00061035156, ((0, 8), (1, 4)), jnp.float32),
        "up_square": jnp.clip(jnp.exp(math.log(1.130280646854942e-09) - 2.7725887 * jax.random.uniform(seeds[11], (D, FF), jnp.float32) ** block_levels(seeds[11], (D, FF), ((0, 8), (1, 4)), -0.2, 0.2)), 7.064254042843388e-11, 1.130280646854942e-09),
        "down_weight": bell_draw(seeds[12], (FF, D), FF ** -0.5, 0.109375, ((0, 4), (1, 8)), jnp.float32),
        "down_mean": bell_draw(seeds[13], (FF, D), (0.11 / (4 * D * D + 2 * D * FF) ** 0.5), 0.00061035156, ((0, 4), (1, 8)), jnp.float32),
        "down_square": jnp.clip(jnp.exp(math.log(1.130280646854942e-09) - 2.7725887 * jax.random.uniform(seeds[14], (FF, D), jnp.float32) ** block_levels(seeds[14], (FF, D), ((0, 4), (1, 8)), -0.2, 0.2)), 7.064254042843388e-11, 1.130280646854942e-09),
        "head_biases": bell_draw(seeds[15], (HEADS, 2 * HD + FF // HEADS), 0.3, 4.0, ((0, 4), (1, 8)), jnp.float32),
        "bias_mean": bell_draw(seeds[16], (HEADS, 2 * HD + FF // HEADS), (0.11 / (4 * D * D + 2 * D * FF) ** 0.5), 0.00061035156, ((0, 4), (1, 8)), jnp.float32),
        "bias_square": jnp.clip(jnp.exp(math.log(1.130280646854942e-09) - 2.7725887 * jax.random.uniform(seeds[17], (HEADS, 2 * HD + FF // HEADS), jnp.float32) ** block_levels(seeds[17], (HEADS, 2 * HD + FF // HEADS), ((0, 4), (1, 8)), -0.2, 0.2)), 7.064254042843388e-11, 1.130280646854942e-09),
        "norm_vectors": draw_norm_vectors(jax.random.fold_in(seeds[21], 71), 0),
        "vector_mean": bell_draw(seeds[19], (7, D), (0.11 / (4 * D * D + 2 * D * FF) ** 0.5), 0.00061035156, ((1, 8),), jnp.float32),
        "vector_square": jnp.clip(jnp.exp(math.log(1.130280646854942e-09) - 2.7725887 * jax.random.uniform(seeds[20], (7, D), jnp.float32) ** block_levels(seeds[20], (7, D), ((1, 8),), -0.2, 0.2)), 7.064254042843388e-11, 1.130280646854942e-09),
    }


highest = lax.Precision.HIGHEST
norm_eps = 1e-05
adam_eps = 1e-08
beta_one = 0.9
beta_two = 0.999
step_count = 10.0
clip_limit = 1.0
settings = ((0.05, 0.1), (0.3, 0.1), (0.05, 0.1), (0.03, 0.1), (0.3, 0.0), (0.4, 0.0))

@jax.custom_vjp
def low(v):
    return lax.optimization_barrier(v.astype(jnp.bfloat16)).astype(jnp.float32)

@jax.custom_vjp
def low_back(v):
    return v

def low_keep(v):
    return (low(v), None)

def low_pass(kept, grad):
    return (grad,)

def back_keep(v):
    return (v, None)

def back_low(kept, grad):
    return (low(grad),)
low.defvjp(low_keep, low_pass)
low_back.defvjp(back_keep, back_low)

def layer_norm(values, norm_gain, norm_shift):
    centred = values - lax.optimization_barrier(jnp.mean(values, axis=-1, keepdims=True))
    variance = lax.optimization_barrier(jnp.mean(centred * centred, axis=-1, keepdims=True))
    return centred * lax.rsqrt(variance + norm_eps) * norm_gain + norm_shift

def clip_attention(triple):
    queries, key_rows, value_rows = triple
    scores = jnp.einsum('qhe,khe->hqk', queries, key_rows, precision=highest) * HD ** (-0.5)
    scores = low_back(scores)
    attention = jax.nn.softmax(scores, axis=-1)
    return jnp.einsum('hqk,khe->qhe', low(attention), value_rows, precision=highest)

def forward(params, frame_rows, masked):
    qkv_low, out_low, up_low, down_low, bias_low, vector_low = [low(weight) for weight in params]
    inputs = jnp.where(masked, vector_low[0], frame_rows)
    rounded = low(inputs)
    zero_bias = jnp.zeros_like(bias_low[:, :HD])
    qkv_bias = jnp.stack([bias_low[:, :HD], zero_bias, bias_low[:, HD:2 * HD]], axis=1).reshape(-1)
    projected = jnp.dot(rounded, qkv_low, precision=highest) + qkv_bias
    projected = low_back(low(projected))
    split = projected.reshape(-1, LEN, HEADS, 3, HD)
    mixed_rows = lax.map(jax.checkpoint(clip_attention), (split[:, :, :, 0], split[:, :, :, 1], split[:, :, :, 2]))
    mixed_rows = low_back(low(mixed_rows.reshape(-1, D)))
    attended = low_back(jnp.dot(mixed_rows, out_low, precision=highest))
    first_sum = inputs + attended + vector_low[5]
    hidden = layer_norm(first_sum, vector_low[1], vector_low[2])
    pre_act = jnp.dot(low(hidden), up_low, precision=highest) + bias_low[:, 2 * HD:].reshape(-1)
    pre_act = low_back(pre_act)
    activated = low(jax.nn.gelu(pre_act, approximate=False))
    branch = low_back(jnp.dot(activated, down_low, precision=highest))
    second_sum = hidden + branch + vector_low[6]
    return layer_norm(second_sum, vector_low[3], vector_low[4])

def adam_step(weight, mean_old, square_old, gradient, factor, rate, decay):
    clipped = gradient * factor
    mean_new = beta_one * mean_old + (1.0 - beta_one) * clipped
    square_new = beta_two * square_old + (1.0 - beta_two) * clipped * clipped
    mean_hat = mean_new / (1.0 - beta_one ** step_count)
    square_hat = square_new / (1.0 - beta_two ** step_count)
    weight_new = weight - rate * (mean_hat / (jnp.sqrt(square_hat) + adam_eps) + decay * weight)
    return (weight_new, mean_new, square_new)

def reference(frames, span_mask, cotangent, qkv_weight, qkv_mean, qkv_square, out_weight, out_mean, out_square, up_weight, up_mean, up_square, down_weight, down_mean, down_square, head_biases, bias_mean, bias_square, norm_vectors, vector_mean, vector_square):
    params = (qkv_weight, out_weight, up_weight, down_weight, head_biases, norm_vectors)
    means = (qkv_mean, out_mean, up_mean, down_mean, bias_mean, vector_mean)
    squares = (qkv_square, out_square, up_square, down_square, bias_square, vector_square)
    group_rows = CLIPS_DP * LEN
    groups = TOKENS // group_rows
    frame_groups = frames.astype(jnp.float32).reshape(groups, group_rows, D)
    mask_groups = span_mask.reshape(groups, group_rows, 1) == 1
    cot_groups = cotangent.astype(jnp.float32).reshape(groups, group_rows, D)

    def one_group(totals, pieces):
        frame_rows, mask_rows, cot_rows = pieces
        outputs, pullback = jax.vjp(lambda weights, input_rows: forward(weights, input_rows, mask_rows), params, frame_rows)
        weight_grads, frame_grads = pullback(cot_rows)
        totals = tuple((total + grad_part for total, grad_part in zip(totals, weight_grads)))
        return (totals, (outputs, frame_grads))
    zero_grads = tuple((jnp.zeros_like(weight) for weight in params))
    gradients, (outputs, frame_grads) = lax.scan(one_group, zero_grads, (frame_groups, mask_groups, cot_groups))
    total_squares = jnp.float32(0.0)
    for gradient in gradients:
        total_squares = total_squares + jnp.sum(gradient * gradient)
    grad_norm = jnp.sqrt(total_squares)
    factor = jnp.minimum(1.0, clip_limit / (grad_norm + 1e-06))
    updated = []
    for index_at in range(6):
        updated.extend(adam_step(params[index_at], means[index_at], squares[index_at], gradients[index_at], factor, settings[index_at][0], settings[index_at][1]))
    return (outputs.reshape(TOKENS, D), frame_grads.reshape(TOKENS, D), grad_norm, updated[0], updated[1], updated[2], updated[3], updated[4], updated[5], updated[6], updated[7], updated[8], updated[9], updated[10], updated[11], updated[12], updated[13], updated[14], updated[15], updated[16], updated[17])
```

```python
import functools

import jax
import jax.numpy as jnp
from jax import lax
from jax.experimental import pallas as pl
from jax.experimental.pallas import tpu as pltpu
from jax.sharding import PartitionSpec as P

HD = 64
LEN = 688


norm_eps = 1e-05
adam_eps = 1e-08
beta_one = 0.9
beta_two = 0.999
step_count = 10.0
clip_limit = 1.0
settings = ((0.05, 0.1), (0.3, 0.1), (0.05, 0.1), (0.03, 0.1), (0.3, 0.0), (0.4, 0.0))


def norm_rows(values, norm_gain, norm_shift):
    centred = values - jnp.mean(values, axis=-1, keepdims=True)
    variance = jnp.mean(centred * centred, axis=-1, keepdims=True)
    inverse = lax.rsqrt(variance + norm_eps)
    normed = centred * inverse
    return (normed * norm_gain + norm_shift, normed, inverse)


def norm_back(upstream, normed, inverse, norm_gain):
    scaled = upstream * norm_gain
    inner_part = (
        scaled
        - jnp.mean(scaled, axis=-1, keepdims=True)
        - normed * jnp.mean(scaled * normed, axis=-1, keepdims=True)
    )
    return (inverse * inner_part, jnp.sum(upstream * normed, axis=0), jnp.sum(upstream, axis=0))


def gelu_slope(pre_act):
    cumulative = 0.5 * (1.0 + jax.scipy.special.erf(pre_act * 0.7071067811865476))
    return cumulative + pre_act * jnp.exp(-0.5 * pre_act * pre_act) * 0.3989422804014327


def attend_forward(clip_block):
    scaling = HD ** (-0.5)
    queries = clip_block[:, :, 0]
    key_rows = clip_block[:, :, 1]
    value_rows = clip_block[:, :, 2]
    scores = (
        jnp.einsum("qhe,khe->hqk", queries, key_rows, preferred_element_type=jnp.float32) * scaling
    )
    row_peak = jnp.max(scores, axis=-1, keepdims=True)
    log_total = row_peak + jnp.log(jnp.sum(jnp.exp(scores - row_peak), axis=-1, keepdims=True))
    attention = jnp.exp(scores - log_total).astype(jnp.bfloat16)
    mixed_rows = jnp.einsum(
        "hqk,khe->qhe", attention, value_rows, preferred_element_type=jnp.float32
    )
    return (mixed_rows.astype(jnp.bfloat16).reshape(clip_block.shape[0], -1), log_total)


def attend_backward(pieces):
    clip_block, log_total, grad_mixed = pieces
    scaling = HD ** (-0.5)
    queries = clip_block[:, :, 0]
    key_rows = clip_block[:, :, 1]
    value_rows = clip_block[:, :, 2]
    scores = (
        jnp.einsum("qhe,khe->hqk", queries, key_rows, preferred_element_type=jnp.float32) * scaling
    )
    attention = jnp.exp(scores - log_total)
    attention_low = attention.astype(jnp.bfloat16)
    mixed_rows = jnp.einsum(
        "hqk,khe->qhe", attention_low, value_rows, preferred_element_type=jnp.float32
    ).astype(jnp.bfloat16)
    grad_rows = grad_mixed.reshape(queries.shape)
    grad_attention = jnp.einsum(
        "qhe,khe->hqk", grad_rows, value_rows, preferred_element_type=jnp.float32
    )
    grad_values = jnp.einsum(
        "hqk,qhe->khe", attention_low, grad_rows, preferred_element_type=jnp.float32
    )
    row_inner = jnp.sum(attention * grad_attention, axis=-1, keepdims=True)
    grad_scores = (attention * (grad_attention - row_inner)).astype(jnp.bfloat16)
    grad_queries = (
        jnp.einsum("hqk,khe->qhe", grad_scores, key_rows, preferred_element_type=jnp.float32)
        * scaling
    )
    grad_keys = (
        jnp.einsum("hqk,qhe->khe", grad_scores, queries, preferred_element_type=jnp.float32)
        * scaling
    )
    grad_block = jnp.stack([grad_queries, grad_keys, grad_values], axis=2).astype(jnp.bfloat16)
    return (
        mixed_rows.reshape(clip_block.shape[0], -1),
        grad_block.reshape(clip_block.shape[0], -1),
    )


def adam_step(weight, mean_old, square_old, gradient, factor, rate, decay):
    clipped = gradient * factor
    mean_new = beta_one * mean_old + (1.0 - beta_one) * clipped
    square_new = beta_two * square_old + (1.0 - beta_two) * clipped * clipped
    mean_hat = mean_new / (1.0 - beta_one**step_count)
    square_hat = square_new / (1.0 - beta_two**step_count)
    weight_new = weight - rate * (mean_hat / (jnp.sqrt(square_hat) + adam_eps) + decay * weight)
    return (weight_new, mean_new, square_new)


def on_device(
    frames,
    span_mask,
    cotangent,
    qkv_weight,
    qkv_mean,
    qkv_square,
    out_weight,
    out_mean,
    out_square,
    up_weight,
    up_mean,
    up_square,
    down_weight,
    down_mean,
    down_square,
    head_biases,
    bias_mean,
    bias_square,
    norm_vectors,
    vector_mean,
    vector_square,
):
    masters = (qkv_weight, out_weight, up_weight, down_weight, head_biases, norm_vectors)
    lowered = tuple((weight.astype(jnp.bfloat16) for weight in masters))
    qkv_full, out_full, up_full, down_full, bias_full, vector_full = (
        lax.all_gather(lowered[0], "dp", axis=0, tiled=True),
        lax.all_gather(lowered[1], "dp", axis=1, tiled=True),
        lax.all_gather(lowered[2], "dp", axis=0, tiled=True),
        lax.all_gather(lowered[3], "dp", axis=1, tiled=True),
        lax.all_gather(lowered[4], "dp", axis=1, tiled=True),
        lax.all_gather(lowered[5], "dp", axis=1, tiled=True),
    )
    share_rows = frames.shape[0]
    start_row = lax.axis_index("mp") * share_rows
    vectors = vector_full.astype(jnp.float32)
    local_heads = bias_full.shape[0]

    def share_of(array_full):
        return lax.dynamic_slice_in_dim(array_full, start_row, share_rows, 0)

    gathered = lax.all_gather(frames, "mp", axis=0, tiled=True)
    all_rows = gathered.shape[0]
    masked = span_mask.reshape(all_rows, 1) == 1
    inputs = jnp.where(masked, vectors[0], gathered.astype(jnp.float32))
    rounded = inputs.astype(jnp.bfloat16)
    zero_bias = jnp.zeros_like(bias_full[:, :HD])
    qkv_bias = (
        jnp.stack([bias_full[:, :HD], zero_bias, bias_full[:, HD : 2 * HD]], axis=1)
        .reshape(-1)
        .astype(jnp.float32)
    )
    up_bias = bias_full[:, 2 * HD :].reshape(-1).astype(jnp.float32)
    projected = (jnp.dot(rounded, qkv_full, preferred_element_type=jnp.float32) + qkv_bias).astype(
        jnp.bfloat16
    )
    blocks = projected.reshape(-1, LEN, local_heads, 3, HD)
    mixed_rows, log_total = lax.map(attend_forward, blocks)
    mixed_rows = mixed_rows.reshape(all_rows, -1)
    attn_part = jnp.dot(mixed_rows, out_full, preferred_element_type=jnp.float32)
    attended = lax.psum(attn_part, "mp")
    first_sum = inputs + attended + vectors[5]
    hidden, normed_full, inverse_full = norm_rows(first_sum, vectors[1], vectors[2])
    normed_one = share_of(normed_full)
    inverse_one = share_of(inverse_full)
    hidden_low = hidden.astype(jnp.bfloat16)
    pre_act = jnp.dot(hidden_low, up_full, preferred_element_type=jnp.float32) + up_bias
    activated = jax.nn.gelu(pre_act, approximate=False).astype(jnp.bfloat16)
    ffn_part = jnp.dot(activated, down_full, preferred_element_type=jnp.float32)
    second_sum = hidden + lax.psum(ffn_part, "mp") + vectors[6]
    outputs_full, normed_full, inverse_full = norm_rows(second_sum, vectors[3], vectors[4])
    outputs = share_of(outputs_full)
    normed_two = share_of(normed_full)
    inverse_two = share_of(inverse_full)
    qkv_full, out_full, up_full, down_full, bias_full, vector_full = (
        lax.all_gather(lowered[0], "dp", axis=0, tiled=True),
        lax.all_gather(lowered[1], "dp", axis=1, tiled=True),
        lax.all_gather(lowered[2], "dp", axis=0, tiled=True),
        lax.all_gather(lowered[3], "dp", axis=1, tiled=True),
        lax.all_gather(lowered[4], "dp", axis=1, tiled=True),
        lax.all_gather(lowered[5], "dp", axis=1, tiled=True),
    )
    upstream = cotangent.astype(jnp.float32)
    grad_two, grad_gain_two, grad_shift_two = norm_back(
        upstream, normed_two, inverse_two, vectors[3]
    )
    grad_down_bias = jnp.sum(grad_two, axis=0)
    grad_two_full = lax.all_gather(grad_two.astype(jnp.bfloat16), "mp", axis=0, tiled=True)
    pre_again = jnp.dot(hidden_low, up_full, preferred_element_type=jnp.float32) + up_bias
    act_again = jax.nn.gelu(pre_again, approximate=False).astype(jnp.bfloat16)
    grad_down = jnp.einsum(
        "tf,td->fd", act_again, grad_two_full, preferred_element_type=jnp.float32
    )
    grad_act = jnp.einsum("td,fd->tf", grad_two_full, down_full, preferred_element_type=jnp.float32)
    grad_pre = (grad_act * gelu_slope(pre_again)).astype(jnp.bfloat16)
    grad_up = jnp.einsum("td,tf->df", hidden_low, grad_pre, preferred_element_type=jnp.float32)
    grad_up_bias = jnp.sum(grad_pre, axis=0, dtype=jnp.float32)
    hidden_part = jnp.einsum("tf,df->td", grad_pre, up_full, preferred_element_type=jnp.float32)
    grad_hidden = grad_two + lax.psum_scatter(hidden_part, "mp", scatter_dimension=0, tiled=True)
    grad_one, grad_gain_one, grad_shift_one = norm_back(
        grad_hidden, normed_one, inverse_one, vectors[1]
    )
    grad_out_bias = jnp.sum(grad_one, axis=0)
    grad_one_full = lax.all_gather(grad_one.astype(jnp.bfloat16), "mp", axis=0, tiled=True)
    grad_mixed = jnp.einsum(
        "td,cd->tc", grad_one_full, out_full, preferred_element_type=jnp.float32
    ).astype(jnp.bfloat16)
    mixed_again, grad_blocks = lax.map(
        attend_backward, (blocks, log_total, grad_mixed.reshape(-1, LEN, grad_mixed.shape[1]))
    )
    mixed_again = mixed_again.reshape(all_rows, -1)
    grad_blocks = grad_blocks.reshape(all_rows, -1)
    grad_out = jnp.einsum(
        "tc,td->cd", mixed_again, grad_one_full, preferred_element_type=jnp.float32
    )
    grad_qkv = jnp.einsum("td,tc->dc", rounded, grad_blocks, preferred_element_type=jnp.float32)
    bias_sums = jnp.sum(grad_blocks, axis=0, dtype=jnp.float32).reshape(local_heads, 3, HD)
    grad_biases = jnp.concatenate(
        [bias_sums[:, 0], bias_sums[:, 2], grad_up_bias.reshape(local_heads, -1)], axis=1
    )
    input_part = jnp.einsum("tc,dc->td", grad_blocks, qkv_full, preferred_element_type=jnp.float32)
    grad_inputs = grad_one + lax.psum_scatter(
        input_part.astype(jnp.bfloat16), "mp", scatter_dimension=0, tiled=True
    ).astype(jnp.float32)
    masked_share = share_of(masked)
    grad_embed = jnp.sum(jnp.where(masked_share, grad_inputs, 0.0), axis=0)
    frame_grad = jnp.where(masked_share, 0.0, grad_inputs)
    grad_vectors = jnp.stack(
        [
            grad_embed,
            grad_gain_one,
            grad_shift_one,
            grad_gain_two,
            grad_shift_two,
            grad_out_bias,
            grad_down_bias,
        ]
    )
    reduced = (
        lax.psum_scatter(grad_qkv, "dp", scatter_dimension=0, tiled=True),
        lax.psum_scatter(grad_out, "dp", scatter_dimension=1, tiled=True),
        lax.psum_scatter(grad_up, "dp", scatter_dimension=0, tiled=True),
        lax.psum_scatter(grad_down, "dp", scatter_dimension=1, tiled=True),
        lax.psum_scatter(grad_biases, "dp", scatter_dimension=1, tiled=True),
    )
    local_squares = jnp.float32(0.0)
    for portion in reduced:
        local_squares = local_squares + jnp.sum(portion * portion)
    total_squares, vector_total = lax.psum((local_squares, grad_vectors), ("dp", "mp"))
    grad_norm = jnp.sqrt(total_squares + jnp.sum(vector_total * vector_total))
    column_count = norm_vectors.shape[1]
    vector_grad = lax.dynamic_slice_in_dim(
        vector_total, lax.axis_index("dp") * column_count, column_count, 1
    )
    factor = jnp.minimum(1.0, clip_limit / (grad_norm + 1e-06))
    gradients = (reduced[0], reduced[1], reduced[2], reduced[3], reduced[4], vector_grad)
    means = (qkv_mean, out_mean, up_mean, down_mean, bias_mean, vector_mean)
    squares = (qkv_square, out_square, up_square, down_square, bias_square, vector_square)
    updated = []
    for index_at in range(6):
        updated.extend(
            adam_step(
                masters[index_at],
                means[index_at],
                squares[index_at],
                gradients[index_at],
                factor,
                settings[index_at][0],
                settings[index_at][1],
            )
        )
    return (
        outputs,
        frame_grad,
        grad_norm,
        updated[0],
        updated[1],
        updated[2],
        updated[3],
        updated[4],
        updated[5],
        updated[6],
        updated[7],
        updated[8],
        updated[9],
        updated[10],
        updated[11],
        updated[12],
        updated[13],
        updated[14],
        updated[15],
        updated[16],
        updated[17],
    )


MESH = pl.DeviceIdType.MESH
D = 768
ROW = 96


def fast_fits(mesh):
    return mesh.shape["dp"] == 8 and mesh.shape["mp"] == 4


def place():
    return lax.axis_index("dp"), lax.axis_index("mp")


def flip(dp, bit):
    held = lax.rem(lax.div(dp, bit), 2)
    return dp + bit - 2 * bit * held


def rows_of(dp, height):
    return pl.ds(pl.multiple_of(dp * height, height), height)


def greet():
    dp, mp = place()
    bar = pltpu.get_barrier_semaphore()
    for bit in (1, 2, 4):
        pl.semaphore_signal(bar, inc=1, device_id=(flip(dp, bit), mp), device_id_type=MESH)
    for k in range(1, 4):
        pl.semaphore_signal(bar, inc=1, device_id=(dp, lax.rem(mp + k, 4)), device_id_type=MESH)
    pl.semaphore_wait(bar, 6)


class Sender:
    def __init__(self):
        self.sent = []

    def send(self, src, dst, send_sem, recv_sem, device):
        copy = pltpu.make_async_remote_copy(
            src_ref=src,
            dst_ref=dst,
            send_sem=send_sem,
            recv_sem=recv_sem,
            device_id=device,
            device_id_type=MESH,
        )
        copy.start()
        self.sent.append(copy)
        return copy

    def finish(self):
        for copy in self.sent:
            copy.wait_send()


def landed(dst, sem):
    pltpu.make_async_copy(dst, dst, sem).wait()


SEMS = 19


def gather_kernel(count, *refs):
    own = refs[:count]
    full = refs[count : 2 * count]
    ss, rs, ls = refs[2 * count :]
    dp, mp = place()
    dx, dy, dc, dd = flip(dp, 2), flip(dp, 4), flip(dp, 1), flip(flip(dp, 2), 4)
    heights = [ref.shape[0] for ref in own]
    out = Sender()
    keep = []
    for w in range(count):
        copy = pltpu.make_async_copy(own[w], full[w].at[mp, rows_of(dp, heights[w])], ls.at[w])
        copy.start()
        keep.append(copy)
    greet()

    def piece(w, z, d):
        return full[w].at[z, rows_of(d, heights[w])]

    def step_z(w):
        for k in range(3):
            peer = lax.rem(mp + k + 1, 4)
            out.send(own[w], piece(w, mp, dp), ss.at[w, k], rs.at[w, k], (dp, peer))

    def step_xy(w, k):
        z = lax.rem(mp + 4 - k, 4)
        src = own[w] if k == 0 else piece(w, z, dp)
        if k:
            landed(piece(w, z, dp), rs.at[w, k - 1])
        out.send(src, piece(w, z, dp), ss.at[w, 3 + k], rs.at[w, 3 + k], (dx, mp))
        out.send(src, piece(w, z, dp), ss.at[w, 7 + k], rs.at[w, 7 + k], (dy, mp))

    def step_diag(w, k):
        z = lax.rem(mp + 4 - k, 4)
        landed(piece(w, z, dx), rs.at[w, 3 + k])
        if k % 2 == 0:
            out.send(piece(w, z, dx), piece(w, z, dx), ss.at[w, 11 + k], rs.at[w, 11 + k], (dy, mp))
        landed(piece(w, z, dy), rs.at[w, 7 + k])
        if k % 2 == 1:
            out.send(piece(w, z, dy), piece(w, z, dy), ss.at[w, 11 + k], rs.at[w, 11 + k], (dx, mp))

    def group(w, d):
        return full[w].at[:, rows_of(d, heights[w])]

    def step_core(w, which):
        d = (dp, dx, dy, dd)[which]
        if which == 3:
            for k in range(4):
                landed(piece(w, lax.rem(mp + 4 - k, 4), dd), rs.at[w, 11 + k])
        out.send(group(w, d), group(w, d), ss.at[w, 15 + which], rs.at[w, 15 + which], (dc, mp))

    for w in range(count):
        step_z(w)
        step_xy(w, 0)
    for copy in keep:
        copy.wait()
    for w in range(count + 1):
        if w < count:
            for k in range(1, 4):
                step_xy(w, k)
            step_core(w, 0)
        if w >= 1:
            for k in range(4):
                step_diag(w - 1, k)
            step_core(w - 1, 1)
            step_core(w - 1, 2)
            step_core(w - 1, 3)
    for w in range(count):
        for which, d in enumerate((dp, dx, dy, dd)):
            landed(group(w, flip(d, 1)), rs.at[w, 15 + which])
    out.finish()


def gather_all(shards):
    count = len(shards)
    return pl.pallas_call(
        functools.partial(gather_kernel, count),
        out_shape=tuple(
            jax.ShapeDtypeStruct((4, 8 * s.shape[0], s.shape[1]), s.dtype) for s in shards
        ),
        in_specs=[pl.BlockSpec(memory_space=pltpu.VMEM)] * count,
        out_specs=tuple(pl.BlockSpec(memory_space=pl.ANY) for _ in shards),
        scratch_shapes=[
            pltpu.SemaphoreType.DMA((count, SEMS)),
            pltpu.SemaphoreType.DMA((count, SEMS)),
            pltpu.SemaphoreType.DMA((count,)),
        ],
        compiler_params=pltpu.CompilerParams(
            collective_id=0, has_side_effects=True, vmem_limit_bytes=58 * 2**20
        ),
        name="gather_weights",
    )(*shards)


def reduce_kernel(count, *refs):
    local = refs[:count]
    result = refs[count : 2 * count]
    norm_ref, vec_ref = refs[2 * count : 2 * count + 2]
    at = 2 * count + 2
    from_core = refs[at : at + count]
    from_diag = refs[at + count : at + 2 * count]
    from_x = refs[at + 2 * count : at + 3 * count]
    from_y = refs[at + 3 * count : at + 4 * count]
    from_z = refs[at + 4 * count : at + 5 * count]
    tiles, ss, rs, ts, tr = refs[at + 5 * count :]
    dp, mp = place()
    dx, dy, dc, dd = flip(dp, 2), flip(dp, 4), flip(dp, 1), flip(flip(dp, 2), 4)
    heights = [ref.shape[0] for ref in result]
    out = Sender()
    greet()
    owners = (dd, dx, dy, dp)

    def piece(w, z, d):
        return local[w].at[z, rows_of(d, heights[w])]

    def group(w, d):
        return local[w].at[:, rows_of(d, heights[w])]

    def zk(k):
        return lax.rem(mp + k, 4)

    def step_core_send(w):
        for j, d in enumerate(owners):
            out.send(
                group(w, flip(d, 1)), from_core[w].at[j], ss.at[w, j], rs.at[w, j], (dc, mp)
            )

    def add_in(w, z, d, arrived):
        ref = piece(w, z, d)
        ref[...] = (ref[...].astype(jnp.float32) + arrived[...].astype(jnp.float32)).astype(
            ref.dtype
        )

    def step_core(w, j):
        landed(from_core[w].at[j], rs.at[w, j])
        d = owners[j]
        for z in range(4):
            add_in(w, z, d, from_core[w].at[j, z])

    def step_diag_send(w):
        for k in range(4):
            to = dy if k % 2 == 0 else dx
            out.send(
                piece(w, zk(k), dd), from_diag[w].at[k], ss.at[w, 4 + k], rs.at[w, 4 + k], (to, mp)
            )

    def step_direct(w):
        for k in range(4):
            if k % 2 == 1:
                out.send(piece(w, zk(k), dx), from_x[w].at[k], ss.at[w, 8 + k], rs.at[w, 8 + k], (dx, mp))
            else:
                out.send(piece(w, zk(k), dy), from_y[w].at[k], ss.at[w, 12 + k], rs.at[w, 12 + k], (dy, mp))

    def step_diag(w):
        for k in range(4):
            landed(from_diag[w].at[k], rs.at[w, 4 + k])
            if k % 2 == 0:
                add_in(w, zk(k), dx, from_diag[w].at[k])
                out.send(piece(w, zk(k), dx), from_x[w].at[k], ss.at[w, 8 + k], rs.at[w, 8 + k], (dx, mp))
            else:
                add_in(w, zk(k), dy, from_diag[w].at[k])
                out.send(piece(w, zk(k), dy), from_y[w].at[k], ss.at[w, 12 + k], rs.at[w, 12 + k], (dy, mp))

    def step_own(w):
        for k in (1, 2, 3, 0):
            landed(from_x[w].at[k], rs.at[w, 8 + k])
            landed(from_y[w].at[k], rs.at[w, 12 + k])
            ref = piece(w, zk(k), dp)
            total = (
                ref[...].astype(jnp.float32)
                + from_x[w][k].astype(jnp.float32)
                + from_y[w][k].astype(jnp.float32)
            )
            if k:
                ref[...] = total.astype(ref.dtype)
                out.send(
                    ref, from_z[w].at[k - 1], ss.at[w, 15 + k], rs.at[w, 15 + k], (dp, zk(k))
                )
            else:
                result[w][...] = total

    def step_z(w):
        total = result[w][...]
        for k in range(3):
            landed(from_z[w].at[k], rs.at[w, 16 + k])
            total = total + from_z[w][k].astype(jnp.float32)
        result[w][...] = total
        return jnp.sum(total * total)

    for w in range(count):
        step_core_send(w)
    for w in range(count):
        step_core(w, 0)
        step_diag_send(w)
        step_core(w, 1)
        step_core(w, 2)
        step_direct(w)
        step_core(w, 3)
    for w in range(count):
        step_diag(w)
        if w:
            step_own(w - 1)
    step_own(count - 1)
    squares = jnp.float32(0.0)
    for w in range(count):
        squares = squares + step_z(w)
    row_id = lax.broadcasted_iota(jnp.int32, (8, 128), 0)
    tiles[0] = jnp.where(row_id == 7, squares, result[count - 1][0:8, :])
    for k in range(3):
        out.send(tiles.at[0], tiles.at[1 + k], ts.at[k], tr.at[k], (dp, zk(k + 1)))
    for k in range(3):
        landed(tiles.at[1 + k], tr.at[k])
    for k in range(4):
        vec_ref[lax.rem(mp + 4 - k, 4)] = tiles[k]
    total = tiles[0] + tiles[1] + tiles[2] + tiles[3]
    for step, bit in enumerate((1, 2, 4)):
        tiles[4 + 2 * step] = total
        out.send(
            tiles.at[4 + 2 * step],
            tiles.at[5 + 2 * step],
            ts.at[3 + step],
            tr.at[3 + step],
            (flip(dp, bit), mp),
        )
        landed(tiles.at[5 + 2 * step], tr.at[3 + step])
        total = total + tiles[5 + 2 * step]
    norm_ref[...] = total
    out.finish()


def reduce_all(grads):
    count = len(grads)
    shapes = [(g.shape[1] // 8, g.shape[2]) for g in grads]
    scratch = [
        pltpu.VMEM((n, *lead, *s), g.dtype)
        for n, lead in ((4, (4,)), (4, ()), (4, ()), (4, ()), (3, ()))
        for g, s in zip(grads, shapes)
    ]
    vmem = pl.BlockSpec(memory_space=pltpu.VMEM)
    return pl.pallas_call(
        functools.partial(reduce_kernel, count),
        out_shape=tuple(jax.ShapeDtypeStruct(s, jnp.float32) for s in shapes)
        + (
            jax.ShapeDtypeStruct((8, 128), jnp.float32),
            jax.ShapeDtypeStruct((4, 8, 128), jnp.float32),
        ),
        in_specs=[vmem] * count,
        out_specs=(vmem,) * (count + 2),
        scratch_shapes=scratch
        + [
            pltpu.VMEM((10, 8, 128), jnp.float32),
            pltpu.SemaphoreType.DMA((count, SEMS)),
            pltpu.SemaphoreType.DMA((count, SEMS)),
            pltpu.SemaphoreType.DMA((6,)),
            pltpu.SemaphoreType.DMA((6,)),
        ],
        compiler_params=pltpu.CompilerParams(
            collective_id=1, has_side_effects=True, vmem_limit_bytes=60 * 2**20
        ),
        name="reduce_gradients",
    )(*grads)


def on_device_fast(
    frames,
    span_mask,
    cotangent,
    qkv_weight,
    qkv_mean,
    qkv_square,
    out_weight,
    out_mean,
    out_square,
    up_weight,
    up_mean,
    up_square,
    down_weight,
    down_mean,
    down_square,
    head_biases,
    bias_mean,
    bias_square,
    norm_vectors,
    vector_mean,
    vector_square,
):
    f32, bf16 = jnp.float32, jnp.bfloat16
    dp, mp = lax.axis_index("dp"), lax.axis_index("mp")
    share = frames.shape[0]
    local_heads, bias_cut = head_biases.shape
    vec_cut = norm_vectors.shape[1]
    small = jnp.zeros((16, 128), bf16)
    small = small.at[:local_heads, :bias_cut].set(head_biases.astype(bf16))
    small = small.at[4:11, :vec_cut].set(norm_vectors.astype(bf16))
    shards = (
        small,
        qkv_weight.astype(bf16),
        out_weight.T.astype(bf16),
        up_weight.astype(bf16),
        down_weight.T.astype(bf16),
    )
    small_full, qkv_full, out_full, up_full, down_full = gather_all(shards)
    small_full = small_full.reshape(4, 8, 16, 128)
    vectors = small_full[0, :, 4:11, :vec_cut].transpose(1, 0, 2).reshape(7, -1).astype(f32)
    bias_full = (
        small_full[:, :, :local_heads, :bias_cut]
        .transpose(0, 2, 1, 3)
        .reshape(4, local_heads, 8 * bias_cut)
        .astype(f32)
    )
    mask_rows = lax.dynamic_slice_in_dim(span_mask.reshape(-1), mp * share, share, 0)
    masked = mask_rows[:, None] == 1
    inputs = jnp.where(masked, vectors[0], frames.astype(f32))
    rounded = inputs.astype(bf16)
    zero = jnp.zeros((4, local_heads, HD), f32)
    qkv_bias = jnp.stack([bias_full[..., :HD], zero, bias_full[..., HD : 2 * HD]], axis=2)
    up_bias = bias_full[..., 2 * HD :].reshape(4, -1)
    projected = jnp.einsum("td,zdc->ztc", rounded, qkv_full, preferred_element_type=f32)
    projected = (projected + qkv_bias.reshape(4, 1, -1)).astype(bf16)
    split = projected.reshape(4, share, local_heads, 3, HD).transpose(3, 0, 2, 1, 4)
    split = split.reshape(3, 4 * local_heads, share, HD)
    queries = split[0]
    swap = [(0, 1), (1, 0), (2, 3), (3, 2)]
    partner = lax.ppermute(split[1:], "mp", swap)
    key_rows = jnp.concatenate([split[1], partner[0]], axis=1)
    value_rows = jnp.concatenate([split[2], partner[1]], axis=1)
    scaling = HD ** (-0.5)

    def scores_of():
        return jnp.einsum("hqe,hke->hqk", queries, key_rows, preferred_element_type=f32) * scaling

    scores = scores_of()
    peak = jnp.max(scores, axis=-1, keepdims=True)
    log_total = peak + jnp.log(jnp.sum(jnp.exp(scores - peak), axis=-1, keepdims=True))
    attention = jnp.exp(scores - log_total)
    attention_low = attention.astype(bf16)
    mixed = jnp.einsum("hqk,hke->hqe", attention_low, value_rows, preferred_element_type=f32)
    mixed = mixed.astype(bf16)
    mixed = mixed.reshape(4, local_heads, share, HD).transpose(0, 2, 1, 3).reshape(4, share, -1)
    attended = jnp.einsum("ztc,zdc->td", mixed, out_full, preferred_element_type=f32)
    first_sum = inputs + attended + vectors[5]
    hidden, normed_one, inverse_one = norm_rows(first_sum, vectors[1], vectors[2])
    hidden_low = hidden.astype(bf16)
    pre = jnp.einsum("td,zdf->ztf", hidden_low, up_full, preferred_element_type=f32)
    pre = pre + up_bias[:, None]
    act = jax.nn.gelu(pre, approximate=False).astype(bf16)
    slope = gelu_slope(pre)
    branch = jnp.einsum("ztf,zdf->td", act, down_full, preferred_element_type=f32)
    second_sum = hidden + branch + vectors[6]
    outputs, normed_two, inverse_two = norm_rows(second_sum, vectors[3], vectors[4])

    upstream = cotangent.astype(f32)
    grad_two, grad_gain_two, grad_shift_two = norm_back(
        upstream, normed_two, inverse_two, vectors[3]
    )
    grad_down_bias = jnp.sum(grad_two, axis=0)
    two_low = grad_two.astype(bf16)
    grad_down = jnp.einsum("td,ztf->zdf", two_low, act, preferred_element_type=f32).astype(bf16)
    grad_act = jnp.einsum("td,zdf->ztf", two_low, down_full, preferred_element_type=f32)
    grad_pre = (grad_act * slope).astype(bf16)
    grad_up = jnp.einsum("td,ztf->zdf", hidden_low, grad_pre, preferred_element_type=f32)
    grad_up = grad_up.astype(bf16)
    grad_up_bias = jnp.sum(grad_pre, axis=1, dtype=f32)
    hidden_part = jnp.einsum("ztf,zdf->td", grad_pre, up_full, preferred_element_type=f32)
    grad_one, grad_gain_one, grad_shift_one = norm_back(
        grad_two + hidden_part, normed_one, inverse_one, vectors[1]
    )
    grad_out_bias = jnp.sum(grad_one, axis=0)
    one_low = grad_one.astype(bf16)
    grad_out = jnp.einsum("td,ztc->zdc", one_low, mixed, preferred_element_type=f32).astype(bf16)
    grad_mixed = jnp.einsum("td,zdc->ztc", one_low, out_full, preferred_element_type=f32)
    grad_mixed = grad_mixed.astype(bf16).reshape(4, share, local_heads, HD)
    grad_mixed = grad_mixed.transpose(0, 2, 1, 3).reshape(-1, share, HD)
    grad_attn = jnp.einsum("hqe,hke->hqk", grad_mixed, value_rows, preferred_element_type=f32)
    grad_values = jnp.einsum("hqk,hqe->hke", attention_low, grad_mixed, preferred_element_type=f32)
    inner = jnp.sum(attention * grad_attn, axis=-1, keepdims=True)
    grad_scores = (attention * (grad_attn - inner)).astype(bf16)
    grad_queries = scaling * jnp.einsum(
        "hqk,hke->hqe", grad_scores, key_rows, preferred_element_type=f32
    )
    grad_keys = scaling * jnp.einsum(
        "hqk,hqe->hke", grad_scores, queries, preferred_element_type=f32
    )
    other = jnp.stack([grad_keys[:, share:], grad_values[:, share:]]).astype(bf16)
    other = lax.ppermute(other, "mp", swap).astype(f32)
    grad_split = jnp.stack(
        [grad_queries, grad_keys[:, :share] + other[0], grad_values[:, :share] + other[1]]
    ).astype(bf16)
    grad_block = (
        grad_split.reshape(3, 4, local_heads, share, HD)
        .transpose(1, 3, 2, 0, 4)
        .reshape(4, share, -1)
    )
    grad_qkv = jnp.einsum("td,ztc->zdc", rounded, grad_block, preferred_element_type=f32)
    grad_qkv = grad_qkv.astype(bf16)
    bias_sums = jnp.sum(grad_split, axis=2, dtype=f32).reshape(3, 4, local_heads, HD)
    grad_biases = jnp.concatenate(
        [bias_sums[0], bias_sums[2], grad_up_bias.reshape(4, local_heads, -1)], axis=-1
    )
    grad_inputs = grad_one + jnp.einsum(
        "ztc,zdc->td", grad_block, qkv_full, preferred_element_type=f32
    )
    grad_embed = jnp.sum(jnp.where(masked, grad_inputs, 0.0), axis=0)
    frame_grad = jnp.where(masked, 0.0, grad_inputs)
    grad_vectors = jnp.stack(
        [
            grad_embed,
            grad_gain_one,
            grad_shift_one,
            grad_gain_two,
            grad_shift_two,
            grad_out_bias,
            grad_down_bias,
            jnp.zeros_like(grad_embed),
        ]
    )
    bias_rows = grad_biases.reshape(4, local_heads, 8, bias_cut).transpose(0, 2, 1, 3)
    vec_rows = grad_vectors.reshape(4, 2, 8, vec_cut).transpose(0, 2, 1, 3)
    small_grad = jnp.zeros((4, 8, 8, 128), f32)
    small_grad = small_grad.at[:, :, :local_heads, :bias_cut].set(bias_rows)
    small_grad = small_grad.at[:, :, 4:6, :vec_cut].set(vec_rows).reshape(4, 64, 128)
    down_sum, up_sum, out_sum, qkv_sum, small_sum, norm_tile, vec_tiles = reduce_all(
        (grad_down, grad_up, grad_out, grad_qkv, small_grad)
    )
    grad_norm = jnp.sqrt(norm_tile[7, 0])
    vector_grad = vec_tiles[:, 4:6, :vec_cut].reshape(8, vec_cut)[:7]
    bias_grad = small_sum[:local_heads, :bias_cut]
    factor = jnp.minimum(1.0, clip_limit / (grad_norm + 1e-06))
    masters = (qkv_weight, out_weight, up_weight, down_weight, head_biases, norm_vectors)
    gradients = (qkv_sum, out_sum.T, up_sum, down_sum.T, bias_grad, vector_grad)
    means = (qkv_mean, out_mean, up_mean, down_mean, bias_mean, vector_mean)
    squares = (qkv_square, out_square, up_square, down_square, bias_square, vector_square)
    updated = []
    for index_at in range(6):
        updated.extend(
            adam_step(
                masters[index_at],
                means[index_at],
                squares[index_at],
                gradients[index_at],
                factor,
                settings[index_at][0],
                settings[index_at][1],
            )
        )
    return (outputs, frame_grad, grad_norm, *updated)


def solution(mesh):
    return jax.shard_map(
        on_device_fast if fast_fits(mesh) else on_device,
        mesh=mesh,
        in_specs=(
            P(("dp", "mp"), None),
            P("dp", None),
            P(("dp", "mp"), None),
            P("dp", "mp"),
            P("dp", "mp"),
            P("dp", "mp"),
            P("mp", "dp"),
            P("mp", "dp"),
            P("mp", "dp"),
            P("dp", "mp"),
            P("dp", "mp"),
            P("dp", "mp"),
            P("mp", "dp"),
            P("mp", "dp"),
            P("mp", "dp"),
            P("mp", "dp"),
            P("mp", "dp"),
            P("mp", "dp"),
            P(None, "dp"),
            P(None, "dp"),
            P(None, "dp"),
        ),
        out_specs=(
            P(("dp", "mp"), None),
            P(("dp", "mp"), None),
            P(),
            P("dp", "mp"),
            P("dp", "mp"),
            P("dp", "mp"),
            P("mp", "dp"),
            P("mp", "dp"),
            P("mp", "dp"),
            P("dp", "mp"),
            P("dp", "mp"),
            P("dp", "mp"),
            P("mp", "dp"),
            P("mp", "dp"),
            P("mp", "dp"),
            P("mp", "dp"),
            P("mp", "dp"),
            P("mp", "dp"),
            P(None, "dp"),
            P(None, "dp"),
            P(None, "dp"),
        ),
        check_vma=False,
    )
```

```python
import functools

import jax
import jax.numpy as jnp
from jax import lax
from jax.experimental import pallas as pl
from jax.experimental.pallas import tpu as pltpu
from jax.sharding import PartitionSpec as P

HD = 64
LEN = 688


norm_eps = 1e-05
adam_eps = 1e-08
beta_one = 0.9
beta_two = 0.999
step_count = 10.0
clip_limit = 1.0
settings = ((0.05, 0.1), (0.3, 0.1), (0.05, 0.1), (0.03, 0.1), (0.3, 0.0), (0.4, 0.0))


def norm_rows(values, norm_gain, norm_shift):
    centred = values - jnp.mean(values, axis=-1, keepdims=True)
    variance = jnp.mean(centred * centred, axis=-1, keepdims=True)
    inverse = lax.rsqrt(variance + norm_eps)
    normed = centred * inverse
    return (normed * norm_gain + norm_shift, normed, inverse)


def norm_back(upstream, normed, inverse, norm_gain):
    scaled = upstream * norm_gain
    inner_part = (
        scaled
        - jnp.mean(scaled, axis=-1, keepdims=True)
        - normed * jnp.mean(scaled * normed, axis=-1, keepdims=True)
    )
    return (inverse * inner_part, jnp.sum(upstream * normed, axis=0), jnp.sum(upstream, axis=0))


def gelu_slope(pre_act):
    cumulative = 0.5 * (1.0 + jax.scipy.special.erf(pre_act * 0.7071067811865476))
    return cumulative + pre_act * jnp.exp(-0.5 * pre_act * pre_act) * 0.3989422804014327


def attend_forward(clip_block):
    scaling = HD ** (-0.5)
    queries = clip_block[:, :, 0]
    key_rows = clip_block[:, :, 1]
    value_rows = clip_block[:, :, 2]
    scores = (
        jnp.einsum("qhe,khe->hqk", queries, key_rows, preferred_element_type=jnp.float32) * scaling
    )
    row_peak = jnp.max(scores, axis=-1, keepdims=True)
    log_total = row_peak + jnp.log(jnp.sum(jnp.exp(scores - row_peak), axis=-1, keepdims=True))
    attention = jnp.exp(scores - log_total).astype(jnp.bfloat16)
    mixed_rows = jnp.einsum(
        "hqk,khe->qhe", attention, value_rows, preferred_element_type=jnp.float32
    )
    return (mixed_rows.astype(jnp.bfloat16).reshape(clip_block.shape[0], -1), log_total)


def attend_backward(pieces):
    clip_block, log_total, grad_mixed = pieces
    scaling = HD ** (-0.5)
    queries = clip_block[:, :, 0]
    key_rows = clip_block[:, :, 1]
    value_rows = clip_block[:, :, 2]
    scores = (
        jnp.einsum("qhe,khe->hqk", queries, key_rows, preferred_element_type=jnp.float32) * scaling
    )
    attention = jnp.exp(scores - log_total)
    attention_low = attention.astype(jnp.bfloat16)
    mixed_rows = jnp.einsum(
        "hqk,khe->qhe", attention_low, value_rows, preferred_element_type=jnp.float32
    ).astype(jnp.bfloat16)
    grad_rows = grad_mixed.reshape(queries.shape)
    grad_attention = jnp.einsum(
        "qhe,khe->hqk", grad_rows, value_rows, preferred_element_type=jnp.float32
    )
    grad_values = jnp.einsum(
        "hqk,qhe->khe", attention_low, grad_rows, preferred_element_type=jnp.float32
    )
    row_inner = jnp.sum(attention * grad_attention, axis=-1, keepdims=True)
    grad_scores = (attention * (grad_attention - row_inner)).astype(jnp.bfloat16)
    grad_queries = (
        jnp.einsum("hqk,khe->qhe", grad_scores, key_rows, preferred_element_type=jnp.float32)
        * scaling
    )
    grad_keys = (
        jnp.einsum("hqk,qhe->khe", grad_scores, queries, preferred_element_type=jnp.float32)
        * scaling
    )
    grad_block = jnp.stack([grad_queries, grad_keys, grad_values], axis=2).astype(jnp.bfloat16)
    return (
        mixed_rows.reshape(clip_block.shape[0], -1),
        grad_block.reshape(clip_block.shape[0], -1),
    )


def adam_step(weight, mean_old, square_old, gradient, factor, rate, decay):
    clipped = gradient * factor
    mean_new = beta_one * mean_old + (1.0 - beta_one) * clipped
    square_new = beta_two * square_old + (1.0 - beta_two) * clipped * clipped
    mean_hat = mean_new / (1.0 - beta_one**step_count)
    square_hat = square_new / (1.0 - beta_two**step_count)
    weight_new = weight - rate * (mean_hat / (jnp.sqrt(square_hat) + adam_eps) + decay * weight)
    return (weight_new, mean_new, square_new)


def on_device(
    frames,
    span_mask,
    cotangent,
    qkv_weight,
    qkv_mean,
    qkv_square,
    out_weight,
    out_mean,
    out_square,
    up_weight,
    up_mean,
    up_square,
    down_weight,
    down_mean,
    down_square,
    head_biases,
    bias_mean,
    bias_square,
    norm_vectors,
    vector_mean,
    vector_square,
):
    masters = (qkv_weight, out_weight, up_weight, down_weight, head_biases, norm_vectors)
    lowered = tuple((weight.astype(jnp.bfloat16) for weight in masters))
    qkv_full, out_full, up_full, down_full, bias_full, vector_full = (
        lax.all_gather(lowered[0], "dp", axis=0, tiled=True),
        lax.all_gather(lowered[1], "dp", axis=1, tiled=True),
        lax.all_gather(lowered[2], "dp", axis=0, tiled=True),
        lax.all_gather(lowered[3], "dp", axis=1, tiled=True),
        lax.all_gather(lowered[4], "dp", axis=1, tiled=True),
        lax.all_gather(lowered[5], "dp", axis=1, tiled=True),
    )
    share_rows = frames.shape[0]
    start_row = lax.axis_index("mp") * share_rows
    vectors = vector_full.astype(jnp.float32)
    local_heads = bias_full.shape[0]

    def share_of(array_full):
        return lax.dynamic_slice_in_dim(array_full, start_row, share_rows, 0)

    gathered = lax.all_gather(frames, "mp", axis=0, tiled=True)
    all_rows = gathered.shape[0]
    masked = span_mask.reshape(all_rows, 1) == 1
    inputs = jnp.where(masked, vectors[0], gathered.astype(jnp.float32))
    rounded = inputs.astype(jnp.bfloat16)
    zero_bias = jnp.zeros_like(bias_full[:, :HD])
    qkv_bias = (
        jnp.stack([bias_full[:, :HD], zero_bias, bias_full[:, HD : 2 * HD]], axis=1)
        .reshape(-1)
        .astype(jnp.float32)
    )
    up_bias = bias_full[:, 2 * HD :].reshape(-1).astype(jnp.float32)
    projected = (jnp.dot(rounded, qkv_full, preferred_element_type=jnp.float32) + qkv_bias).astype(
        jnp.bfloat16
    )
    blocks = projected.reshape(-1, LEN, local_heads, 3, HD)
    mixed_rows, log_total = lax.map(attend_forward, blocks)
    mixed_rows = mixed_rows.reshape(all_rows, -1)
    attn_part = jnp.dot(mixed_rows, out_full, preferred_element_type=jnp.float32)
    attended = lax.psum(attn_part, "mp")
    first_sum = inputs + attended + vectors[5]
    hidden, normed_full, inverse_full = norm_rows(first_sum, vectors[1], vectors[2])
    normed_one = share_of(normed_full)
    inverse_one = share_of(inverse_full)
    hidden_low = hidden.astype(jnp.bfloat16)
    pre_act = jnp.dot(hidden_low, up_full, preferred_element_type=jnp.float32) + up_bias
    activated = jax.nn.gelu(pre_act, approximate=False).astype(jnp.bfloat16)
    ffn_part = jnp.dot(activated, down_full, preferred_element_type=jnp.float32)
    second_sum = hidden + lax.psum(ffn_part, "mp") + vectors[6]
    outputs_full, normed_full, inverse_full = norm_rows(second_sum, vectors[3], vectors[4])
    outputs = share_of(outputs_full)
    normed_two = share_of(normed_full)
    inverse_two = share_of(inverse_full)
    qkv_full, out_full, up_full, down_full, bias_full, vector_full = (
        lax.all_gather(lowered[0], "dp", axis=0, tiled=True),
        lax.all_gather(lowered[1], "dp", axis=1, tiled=True),
        lax.all_gather(lowered[2], "dp", axis=0, tiled=True),
        lax.all_gather(lowered[3], "dp", axis=1, tiled=True),
        lax.all_gather(lowered[4], "dp", axis=1, tiled=True),
        lax.all_gather(lowered[5], "dp", axis=1, tiled=True),
    )
    upstream = cotangent.astype(jnp.float32)
    grad_two, grad_gain_two, grad_shift_two = norm_back(
        upstream, normed_two, inverse_two, vectors[3]
    )
    grad_down_bias = jnp.sum(grad_two, axis=0)
    grad_two_full = lax.all_gather(grad_two.astype(jnp.bfloat16), "mp", axis=0, tiled=True)
    pre_again = jnp.dot(hidden_low, up_full, preferred_element_type=jnp.float32) + up_bias
    act_again = jax.nn.gelu(pre_again, approximate=False).astype(jnp.bfloat16)
    grad_down = jnp.einsum(
        "tf,td->fd", act_again, grad_two_full, preferred_element_type=jnp.float32
    )
    grad_act = jnp.einsum("td,fd->tf", grad_two_full, down_full, preferred_element_type=jnp.float32)
    grad_pre = (grad_act * gelu_slope(pre_again)).astype(jnp.bfloat16)
    grad_up = jnp.einsum("td,tf->df", hidden_low, grad_pre, preferred_element_type=jnp.float32)
    grad_up_bias = jnp.sum(grad_pre, axis=0, dtype=jnp.float32)
    hidden_part = jnp.einsum("tf,df->td", grad_pre, up_full, preferred_element_type=jnp.float32)
    grad_hidden = grad_two + lax.psum_scatter(hidden_part, "mp", scatter_dimension=0, tiled=True)
    grad_one, grad_gain_one, grad_shift_one = norm_back(
        grad_hidden, normed_one, inverse_one, vectors[1]
    )
    grad_out_bias = jnp.sum(grad_one, axis=0)
    grad_one_full = lax.all_gather(grad_one.astype(jnp.bfloat16), "mp", axis=0, tiled=True)
    grad_mixed = jnp.einsum(
        "td,cd->tc", grad_one_full, out_full, preferred_element_type=jnp.float32
    ).astype(jnp.bfloat16)
    mixed_again, grad_blocks = lax.map(
        attend_backward, (blocks, log_total, grad_mixed.reshape(-1, LEN, grad_mixed.shape[1]))
    )
    mixed_again = mixed_again.reshape(all_rows, -1)
    grad_blocks = grad_blocks.reshape(all_rows, -1)
    grad_out = jnp.einsum(
        "tc,td->cd", mixed_again, grad_one_full, preferred_element_type=jnp.float32
    )
    grad_qkv = jnp.einsum("td,tc->dc", rounded, grad_blocks, preferred_element_type=jnp.float32)
    bias_sums = jnp.sum(grad_blocks, axis=0, dtype=jnp.float32).reshape(local_heads, 3, HD)
    grad_biases = jnp.concatenate(
        [bias_sums[:, 0], bias_sums[:, 2], grad_up_bias.reshape(local_heads, -1)], axis=1
    )
    input_part = jnp.einsum("tc,dc->td", grad_blocks, qkv_full, preferred_element_type=jnp.float32)
    grad_inputs = grad_one + lax.psum_scatter(
        input_part.astype(jnp.bfloat16), "mp", scatter_dimension=0, tiled=True
    ).astype(jnp.float32)
    masked_share = share_of(masked)
    grad_embed = jnp.sum(jnp.where(masked_share, grad_inputs, 0.0), axis=0)
    frame_grad = jnp.where(masked_share, 0.0, grad_inputs)
    grad_vectors = jnp.stack(
        [
            grad_embed,
            grad_gain_one,
            grad_shift_one,
            grad_gain_two,
            grad_shift_two,
            grad_out_bias,
            grad_down_bias,
        ]
    )
    reduced = (
        lax.psum_scatter(grad_qkv, "dp", scatter_dimension=0, tiled=True),
        lax.psum_scatter(grad_out, "dp", scatter_dimension=1, tiled=True),
        lax.psum_scatter(grad_up, "dp", scatter_dimension=0, tiled=True),
        lax.psum_scatter(grad_down, "dp", scatter_dimension=1, tiled=True),
        lax.psum_scatter(grad_biases, "dp", scatter_dimension=1, tiled=True),
    )
    local_squares = jnp.float32(0.0)
    for portion in reduced:
        local_squares = local_squares + jnp.sum(portion * portion)
    total_squares, vector_total = lax.psum((local_squares, grad_vectors), ("dp", "mp"))
    grad_norm = jnp.sqrt(total_squares + jnp.sum(vector_total * vector_total))
    column_count = norm_vectors.shape[1]
    vector_grad = lax.dynamic_slice_in_dim(
        vector_total, lax.axis_index("dp") * column_count, column_count, 1
    )
    factor = jnp.minimum(1.0, clip_limit / (grad_norm + 1e-06))
    gradients = (reduced[0], reduced[1], reduced[2], reduced[3], reduced[4], vector_grad)
    means = (qkv_mean, out_mean, up_mean, down_mean, bias_mean, vector_mean)
    squares = (qkv_square, out_square, up_square, down_square, bias_square, vector_square)
    updated = []
    for index_at in range(6):
        updated.extend(
            adam_step(
                masters[index_at],
                means[index_at],
                squares[index_at],
                gradients[index_at],
                factor,
                settings[index_at][0],
                settings[index_at][1],
            )
        )
    return (
        outputs,
        frame_grad,
        grad_norm,
        updated[0],
        updated[1],
        updated[2],
        updated[3],
        updated[4],
        updated[5],
        updated[6],
        updated[7],
        updated[8],
        updated[9],
        updated[10],
        updated[11],
        updated[12],
        updated[13],
        updated[14],
        updated[15],
        updated[16],
        updated[17],
    )


MESH = pl.DeviceIdType.MESH
SMALL, QKV, OUT, UP, DOWN = range(5)
SEMS = 19
f32, bf16 = jnp.float32, jnp.bfloat16


def fast_fits(mesh):
    return mesh.shape["dp"] == 8 and mesh.shape["mp"] == 4


def flip(dp, bit):
    held = lax.rem(lax.div(dp, bit), 2)
    return dp + bit - 2 * bit * held


def dg(a, b, ca, cb):
    return lax.dot_general(a, b, (((ca,), (cb,)), ((), ())), preferred_element_type=f32)


def landed(dst, sem):
    pltpu.make_async_copy(dst, dst, sem).wait()


def layer_kernel(
    share,
    fm_in,
    cot_in,
    qkv_in,
    out_in,
    up_in,
    down_in,
    bias_in,
    vec_in,
    act_out,
    fg_out,
    qkv_sum,
    out_sum,
    up_sum,
    down_sum,
    small_sum,
    norm_ref,
    vec_tiles,
    ws,
    wq,
    wo,
    wu,
    wd,
    gs,
    rcs,
    rcq,
    rco,
    rcu,
    rcd,
    rds,
    rdq,
    rdo,
    rdu,
    rdd,
    rxs,
    rxq,
    rxo,
    rxu,
    rxd,
    rys,
    ryq,
    ryo,
    ryu,
    ryd,
    rzs,
    rzq,
    rzo,
    rzu,
    rzd,
    fmx,
    cotx,
    x_low,
    q_all,
    kv_own,
    kv_far,
    mixed,
    lse,
    mix_t,
    n_one,
    r_one,
    hid_low,
    act,
    slope,
    acc,
    low,
    dm,
    dproj,
    stage_act,
    stage_fg,
    vec,
    bias,
    gvec,
    gbias,
    tiles,
    gather_s,
    gather_r,
    reduce_s,
    reduce_r,
    kv_s,
    kv_r,
    move_s,
    move_r,
    tile_s,
    tile_r,
):
    T = share
    dp, mp = lax.axis_index("dp"), lax.axis_index("mp")
    core = lax.rem(dp, 2)
    dx, dy, dc = flip(dp, 2), flip(dp, 4), flip(dp, 1)
    dd = flip(dx, 4)
    mover = lax.rem(core + mp, 2) == 1
    stay = lax.rem(core + mp, 2) == 0
    swap_with = (dc, mp + 1 - 2 * lax.rem(mp, 2))
    full = (ws, wq, wo, wu, wd)
    local = (gs, wq, wo, wu, wd)
    from_core = (rcs, rcq, rco, rcu, rcd)
    from_diag = (rds, rdq, rdo, rdu, rdd)
    from_x = (rxs, rxq, rxo, rxu, rxd)
    from_y = (rys, ryq, ryo, ryu, ryd)
    from_z = (rzs, rzq, rzo, rzu, rzd)
    result = (small_sum, qkv_sum, out_sum, up_sum, down_sum)
    heads = q_all.shape[1]
    chunks = [(r, min(88, T - r)) for r in range(0, T, 88)]

    def remote(src, dst, send_sem, recv_sem, device):
        return pltpu.make_async_remote_copy(
            src_ref=src,
            dst_ref=dst,
            send_sem=send_sem,
            recv_sem=recv_sem,
            device_id=device,
            device_id_type=MESH,
        )

    pending = {}

    def send(tag, *args):
        copy = remote(*args)
        copy.start()
        pending.setdefault(tag, []).append(copy)

    def sent(tag):
        for copy in pending.pop(tag, []):
            copy.wait_send()

    def hand_over(slot, src, dst):
        @pl.when(mover)
        def _():
            remote(src, dst, move_s.at[slot], move_r.at[slot], swap_with).start()

        @pl.when(stay)
        def _():
            pltpu.make_async_copy(src, dst, move_r.at[slot]).start()

    def ag_z(k):
        return lax.rem(mp + 4 - k, 4)

    def slot(w, z, d):
        return full[w].at[z, lax.div(d, 2), lax.rem(d, 2)]

    def ag_own(w):
        for k in range(3):
            peer = lax.rem(mp + k + 1, 4)
            send(("ag", w), slot(w, mp, dp), slot(w, mp, dp), gather_s.at[w, k], gather_r.at[w, k], (dp, peer))

    def ag_a(w, k):
        z = ag_z(k)
        ref = slot(w, z, dp)
        if k:
            landed(ref, gather_r.at[w, k - 1])
        send(("ag", w), ref, ref, gather_s.at[w, 3 + k], gather_r.at[w, 3 + k], (dx, mp))
        send(("ag", w), ref, ref, gather_s.at[w, 7 + k], gather_r.at[w, 7 + k], (dy, mp))

    def ag_b(w, k):
        z = ag_z(k)
        at_x, at_y = slot(w, z, dx), slot(w, z, dy)
        landed(at_x, gather_r.at[w, 3 + k])
        if k % 2 == 0:
            send(("ag", w), at_x, at_x, gather_s.at[w, 11 + k], gather_r.at[w, 11 + k], (dy, mp))
        landed(at_y, gather_r.at[w, 7 + k])
        if k % 2 == 1:
            send(("ag", w), at_y, at_y, gather_s.at[w, 11 + k], gather_r.at[w, 11 + k], (dx, mp))

    def ag_c(w, k):
        z = ag_z(k)
        landed(slot(w, z, dd), gather_r.at[w, 11 + k])
        ref = full[w].at[z, :, core]
        send(("ag", w), ref, ref, gather_s.at[w, 15 + k], gather_r.at[w, 15 + k], (dc, mp))

    def ag_d(w, k):
        landed(full[w].at[ag_z(k), :, 1 - core], gather_r.at[w, 15 + k])

    order = (1, 2, 3, 0)

    def rs_z(k):
        return lax.rem(mp + k, 4)

    def part(w, z, d):
        return local[w].at[z, lax.div(d, 2), lax.rem(d, 2)]

    def rs_0(w, k):
        send("rs", local[w].at[rs_z(k), :, 1 - core], from_core[w].at[k], reduce_s.at[w, k], reduce_r.at[w, k], (dc, mp))

    def rs_1(w, k):
        z = rs_z(k)
        landed(from_core[w].at[k], reduce_r.at[w, k])
        ref = local[w].at[z, :, core]
        ref[...] = ref[...] + from_core[w][k]
        far = dy if k % 2 == 0 else dx
        send("rs", part(w, z, dd), from_diag[w].at[k], reduce_s.at[w, 4 + k], reduce_r.at[w, 4 + k], (far, mp))
        if k % 2 == 1:
            send("rs", part(w, z, dx), from_x[w].at[k], reduce_s.at[w, 8 + k], reduce_r.at[w, 8 + k], (dx, mp))
        else:
            send("rs", part(w, z, dy), from_y[w].at[k], reduce_s.at[w, 12 + k], reduce_r.at[w, 12 + k], (dy, mp))

    def rs_2(w, k):
        z = rs_z(k)
        landed(from_diag[w].at[k], reduce_r.at[w, 4 + k])
        d = dx if k % 2 == 0 else dy
        ref = part(w, z, d)
        ref[...] = ref[...] + from_diag[w][k]
        if k % 2 == 0:
            send("rs", ref, from_x[w].at[k], reduce_s.at[w, 8 + k], reduce_r.at[w, 8 + k], (dx, mp))
        else:
            send("rs", ref, from_y[w].at[k], reduce_s.at[w, 12 + k], reduce_r.at[w, 12 + k], (dy, mp))

    def rs_3(w, k):
        landed(from_x[w].at[k], reduce_r.at[w, 8 + k])
        landed(from_y[w].at[k], reduce_r.at[w, 12 + k])
        ref = part(w, rs_z(k), dp)
        total = ref[...].astype(f32) + from_x[w][k].astype(f32) + from_y[w][k].astype(f32)
        if k:
            ref[...] = total.astype(ref.dtype)
            send("rs", ref, from_z[w].at[k - 1], reduce_s.at[w, 15 + k], reduce_r.at[w, 15 + k], (dp, rs_z(k)))
        else:
            result[w][...] = total

    def rs_4(w):
        total = result[w][...]
        for k in range(3):
            landed(from_z[w].at[k], reduce_r.at[w, 16 + k])
            total = total + from_z[w][k].astype(f32)
        result[w][...] = total
        return jnp.sum(total * total)

    own_j = lax.div(dp, 2)
    cut, vec_cut = bias_in.shape[1], vec_in.shape[1]
    ws[mp, own_j, core] = jnp.zeros(ws.shape[3:], f32)
    ws[mp, own_j, core, 0:heads, 0:cut] = bias_in[...].astype(bf16).astype(f32)
    ws[mp, own_j, core, 8:15, 0:vec_cut] = vec_in[...].astype(bf16).astype(f32)
    wq[mp, own_j, core] = qkv_in[...].astype(bf16)
    bar = pltpu.get_barrier_semaphore()
    others = [(dx, mp), (dy, mp), (dc, mp), swap_with]
    others += [(dp, lax.rem(mp + k, 4)) for k in (1, 2, 3)]
    for device in others:
        pl.semaphore_signal(bar, inc=1, device_id=device, device_id_type=MESH)
    pl.semaphore_wait(bar, len(others))
    for w in (SMALL, QKV):
        ag_own(w)
        ag_a(w, 0)
    hand_over(0, fm_in, fmx)
    wo[mp, own_j, core] = out_in[...].T.astype(bf16)
    ag_own(OUT)
    ag_a(OUT, 0)
    wu[mp, own_j, core] = up_in[...].astype(bf16)
    ag_own(UP)
    ag_a(UP, 0)
    wd[mp, own_j, core] = down_in[...].T.astype(bf16)
    ag_own(DOWN)
    for w in (SMALL, QKV):
        for k in (1, 2, 3):
            ag_a(w, k)
    ag_a(DOWN, 0)
    hand_over(1, cot_in, cotx)
    for k in range(4):
        ag_b(SMALL, k)
    for k in range(4):
        ag_c(SMALL, k)
    for k in range(4):
        ag_b(QKV, k)
    for k in (1, 2, 3):
        ag_a(OUT, k)
    for k in range(4):
        ag_d(SMALL, k)
    cells = [(j, c) for j in range(4) for c in range(2)]
    vec[...] = jnp.concatenate([ws[0, j, c, 8:16, 0:vec_cut] for j, c in cells], axis=1)
    for z in range(4):
        bias[z] = jnp.concatenate([ws[z, j, c, 0:8, 0:cut] for j, c in cells], axis=1)
    embed, gain_one, shift_one, gain_two, shift_two, out_add, down_add = (
        vec[i : i + 1, :] for i in range(7)
    )
    width = vec.shape[1]

    def masked_rows(r, n):
        flag = fmx[r : r + n, width:].astype(f32) > 0.5
        return jnp.concatenate([flag.astype(f32)] * (width // 128), axis=1) > 0.5

    def input_rows(r, n):
        return jnp.where(masked_rows(r, n), embed, fmx[r : r + n, 0:width].astype(f32))

    landed(fmx, move_r.at[0])
    for r, n in chunks:
        x_low[r : r + n, :] = input_rows(r, n).astype(bf16)
    for k in (1, 2, 3):
        ag_a(UP, k)
    for k in range(4):
        ag_c(QKV, k)
    for k in range(4):
        ag_b(OUT, k)

    lane = lax.broadcasted_iota(jnp.int32, (1, 128), 1)

    def project(k):
        z = ag_z(k)
        ag_d(QKV, k)
        slab = jnp.dot(x_low[...], wq[z].reshape(width, -1), preferred_element_type=f32)
        for h in range(heads):
            both = bias[z, h : h + 1, 0:128]
            head = slab[:, 192 * h : 192 * h + 128] + both
            head = head.astype(bf16).astype(f32) * HD ** (-0.5)
            q_all[z, h] = jnp.where(lane < HD, head, 0.0).astype(bf16)
            pair = slab[:, 192 * h + 64 : 192 * h + 192] + jnp.where(lane < HD, 0.0, both)
            kv_own[z, h, 0:T, :] = pair.astype(bf16)
        send("kv", kv_own.at[z], kv_far.at[z], kv_s.at[k], kv_r.at[k], (dc, mp))

    for k in range(4):
        project(k)
        if k:
            ag_a(DOWN, k)
    for k in range(4):
        ag_c(OUT, k)

    def attend(k):
        z = ag_z(k)
        landed(kv_far.at[z], kv_r.at[k])

        @pl.loop(0, heads)
        def _(h):
            queries = q_all[z, h]
            own, far = kv_own[z, h, 0:T, :], kv_far[z, h, 0:T, :]
            s_own, s_far = dg(own, queries, 1, 1), dg(far, queries, 1, 1)
            peak = jnp.maximum(
                jnp.max(s_own, axis=0, keepdims=True), jnp.max(s_far, axis=0, keepdims=True)
            )
            e_own, e_far = jnp.exp(s_own - peak), jnp.exp(s_far - peak)
            total = jnp.sum(e_own, axis=0, keepdims=True) + jnp.sum(e_far, axis=0, keepdims=True)
            lse[z, h] = peak + jnp.log(total)
            scale = 1.0 / total
            mix = dg(own, (e_own * scale).astype(bf16), 0, 0)
            mix = mix + dg(far, (e_far * scale).astype(bf16), 0, 0)
            mix_t[h] = mix[HD:, :]

        mixed[z] = mix_t[...].reshape(heads * HD, T).T.astype(bf16)

    for k in range(4):
        attend(k)
        ag_b(UP, k)
    for k in range(4):
        ag_d(OUT, k)
    for k in range(4):
        z = ag_z(k)
        piece = dg(mixed[z], wo[z].reshape(width, -1), 1, 1)
        acc[...] = piece if k == 0 else acc[...] + piece
    for r, n in chunks:
        v = input_rows(r, n) + acc[r : r + n, :] + out_add
        v = v - jnp.mean(v, axis=-1, keepdims=True)
        inverse = lax.rsqrt(jnp.mean(v * v, axis=-1, keepdims=True) + norm_eps)
        normed = v * inverse
        n_one[r : r + n, :] = normed
        r_one[r : r + n, :] = inverse
        hid_low[r : r + n, :] = (normed * gain_one + shift_one).astype(bf16)
    for k in range(4):
        ag_c(UP, k)

    def rise(k):
        z = ag_z(k)
        ag_d(UP, k)
        for h in range(heads):
            cols = slice(256 * h, 256 * h + 256)
            u = jnp.dot(
                hid_low[...], wu[z, :, :, :, cols].reshape(width, 256), preferred_element_type=f32
            )
            u = u + bias[z, h : h + 1, 128:384]
            cumulative = 0.5 * (1.0 + lax.erf(u * 0.7071067811865476))
            act[z, 0:T, cols] = (u * cumulative).astype(bf16)
            bell = jnp.exp(-0.5 * u * u) * 0.3989422804014327
            slope[z, 0:T, cols] = (cumulative + u * bell).astype(bf16)

    for k in range(4):
        rise(k)
        ag_b(DOWN, k)
    for k in range(4):
        z = ag_z(k)
        ag_c(DOWN, k)
        ag_d(DOWN, k)
        piece = dg(act[z, 0:T, :], wd[z].reshape(width, -1), 1, 1)
        acc[...] = piece if k == 0 else acc[...] + piece

    landed(cotx, move_r.at[1])
    sums = [jnp.zeros((1, width), f32) for _ in range(3)]
    for r, n in chunks:
        v = n_one[r : r + n, :] * gain_one + shift_one + acc[r : r + n, :] + down_add
        v = v - jnp.mean(v, axis=-1, keepdims=True)
        inverse = lax.rsqrt(jnp.mean(v * v, axis=-1, keepdims=True) + norm_eps)
        normed = v * inverse
        stage_act[r : r + n, :] = normed * gain_two + shift_two
        up = cotx[r : r + n, :].astype(f32)
        scaled = up * gain_two
        inner = jnp.mean(scaled * normed, axis=-1, keepdims=True)
        grad = inverse * (scaled - jnp.mean(scaled, axis=-1, keepdims=True) - normed * inner)
        acc[r : r + n, :] = grad
        low[r : r + n, :] = grad.astype(bf16)
        for i, term in enumerate((up * normed, up, grad)):
            sums[i] = sums[i] + jnp.sum(term, axis=0, keepdims=True)
    gvec[...] = jnp.zeros(gvec.shape, f32)
    gbias[...] = jnp.zeros(gbias.shape, f32)
    gvec[3:4, :], gvec[4:5, :], gvec[6:7, :] = sums
    hand_over(2, stage_act, act_out)
    for w in range(5):
        sent(("ag", w))

    def tiled(value):
        return value.reshape(4, 2, -1, value.shape[1])

    def fall(k):
        z = rs_z(k)
        grad = dg(low[...], wd[z].reshape(width, -1), 1, 0)
        grad = (grad * slope[z, 0:T, :].astype(f32)).astype(bf16)
        slope[z, 0:T, :] = grad
        total = jnp.sum(grad.astype(f32), axis=0, keepdims=True)
        for h in range(heads):
            gbias[z, h : h + 1, 128:384] = total[:, 256 * h : 256 * h + 256]
        wd[z] = tiled(dg(low[...], act[z, 0:T, :], 0, 0).astype(bf16))
        rs_0(DOWN, k)

    def sink(k):
        z = rs_z(k)
        acc[...] = acc[...] + dg(slope[z, 0:T, :], wu[z].reshape(width, -1), 1, 1)
        wu[z] = tiled(dg(hid_low[...], slope[z, 0:T, :], 0, 0).astype(bf16))
        rs_0(UP, k)

    last = None
    for k in order:
        fall(k)
        if last is not None:
            rs_1(DOWN, last)
        last = k
    for i, k in enumerate(order):
        sink(k)
        if i == 0:
            rs_1(DOWN, last)
        else:
            rs_1(UP, order[i - 1])
        rs_2(DOWN, k)

    sums = [jnp.zeros((1, width), f32) for _ in range(3)]
    for r, n in chunks:
        grad_in = acc[r : r + n, :]
        normed = n_one[r : r + n, :]
        scaled = grad_in * gain_one
        inner = jnp.mean(scaled * normed, axis=-1, keepdims=True)
        grad = r_one[r : r + n, :] * (
            scaled - jnp.mean(scaled, axis=-1, keepdims=True) - normed * inner
        )
        acc[r : r + n, :] = grad
        low[r : r + n, :] = grad.astype(bf16)
        for i, term in enumerate((grad_in * normed, grad_in, grad)):
            sums[i] = sums[i] + jnp.sum(term, axis=0, keepdims=True)
    gvec[1:2, :], gvec[2:3, :], gvec[5:6, :] = sums
    rs_1(UP, order[3])

    def unmix(k):
        z = rs_z(k)
        grad = dg(low[...], wo[z].reshape(width, -1), 1, 0).astype(bf16).astype(f32)
        nothing = jnp.zeros((T, HD), f32)
        for h in range(heads):
            dm[z, h] = jnp.concatenate([nothing, grad[:, HD * h : HD * h + HD]], axis=1).astype(
                bf16
            )
        wo[z] = tiled(dg(low[...], mixed[z], 0, 0).astype(bf16))
        rs_0(OUT, k)

    for i, k in enumerate(order):
        unmix(k)
        rs_3(DOWN, k)
        rs_2(UP, k)

    def attend_back(k):
        z = rs_z(k)

        @pl.loop(0, heads)
        def _(h):
            queries, gm = q_all[z, h], dm[z, h]
            own, far = kv_own[z, h, 0:T, :], kv_far[z, h, 0:T, :]
            level = lse[z, h]
            p_own = jnp.exp(dg(own, queries, 1, 1) - level)
            p_far = jnp.exp(dg(far, queries, 1, 1) - level)
            g_own, g_far = dg(own, gm, 1, 1), dg(far, gm, 1, 1)
            inner = jnp.sum(p_own * g_own, axis=0, keepdims=True)
            inner = inner + jnp.sum(p_far * g_far, axis=0, keepdims=True)
            s_own = (p_own * (g_own - inner)).astype(bf16)
            s_far = (p_far * (g_far - inner)).astype(bf16)
            pair_far = jnp.dot(s_far, queries, preferred_element_type=f32)
            pair_far = pair_far + jnp.dot(p_far.astype(bf16), gm, preferred_element_type=f32)
            pair_own = jnp.dot(s_own, queries, preferred_element_type=f32)
            pair_own = pair_own + jnp.dot(p_own.astype(bf16), gm, preferred_element_type=f32)
            at = pl.multiple_of(128 * h, 128)
            slope[z, 0:T, pl.ds(at, 128)] = pair_far.astype(bf16)
            slope[z, 0:T, pl.ds(pl.multiple_of(128 * heads + at, 128), 128)] = pair_own.astype(bf16)
            grad_q = dg(own, s_own, 0, 0) + dg(far, s_far, 0, 0)
            mix_t[h] = grad_q[0:HD, :] * HD ** (-0.5)

        mixed[z] = mix_t[...].reshape(heads * HD, T).T.astype(bf16)
        send(
            "rs",
            slope.at[z, :, 0 : 128 * heads],
            act.at[z, :, 0 : 128 * heads],
            kv_s.at[4 + k],
            kv_r.at[4 + k],
            (dc, mp),
        )

    for i, k in enumerate(order):
        attend_back(k)
        rs_1(OUT, k)
        if i:
            rs_2(OUT, order[i - 1])
        rs_3(UP, k)
    rs_2(OUT, order[3])

    def project_back(k):
        z = rs_z(k)
        landed(act.at[z, :, 0 : 128 * heads], kv_r.at[4 + k])
        pieces = []
        for h in range(heads):
            pieces.append(mixed[z, :, HD * h : HD * h + HD].astype(f32))
            far = act[z, 0:T, 128 * h : 128 * h + 128].astype(f32)
            at = 128 * (heads + h)
            pieces.append(far + slope[z, 0:T, at : at + 128].astype(f32))
        slab = jnp.concatenate(pieces, axis=1).astype(bf16)
        dproj[...] = slab
        total = jnp.sum(slab.astype(f32), axis=0, keepdims=True)
        for h in range(heads):
            gbias[z, h : h + 1, 0:128] = jnp.concatenate(
                [total[:, 192 * h : 192 * h + 64], total[:, 192 * h + 128 : 192 * h + 192]], axis=1
            )
        acc[...] = acc[...] + dg(dproj[...], wq[z].reshape(width, -1), 1, 1)
        wq[z] = tiled(dg(x_low[...], dproj[...], 0, 0).astype(bf16))
        rs_0(QKV, k)

    for i, k in enumerate(order):
        project_back(k)
        if i:
            rs_1(QKV, order[i - 1])
        rs_3(OUT, k)
    rs_1(QKV, order[3])

    embed_sum = jnp.zeros((1, width), f32)
    for r, n in chunks:
        hidden_rows = masked_rows(r, n)
        grad = acc[r : r + n, :]
        stage_fg[r : r + n, :] = jnp.where(hidden_rows, 0.0, grad)
        embed_sum = embed_sum + jnp.sum(
            jnp.where(hidden_rows, grad, 0.0), axis=0, keepdims=True
        )
    gvec[0:1, :] = embed_sum
    hand_over(3, stage_fg, fg_out)
    gs[...] = jnp.zeros(gs.shape, f32)
    for d, (j, c) in enumerate(cells):
        vectors = gvec[:, vec_cut * d : vec_cut * (d + 1)]
        for z in range(4):
            gs[z, j, c, 0:4, 0:cut] = gbias[z, 0:4, cut * d : cut * (d + 1)]
            gs[z, j, c, 4:6, 0:vec_cut] = vectors[2 * z : 2 * z + 2, :]
    for k in order:
        rs_0(SMALL, k)
    for k in order:
        rs_1(SMALL, k)
    for k in order:
        rs_2(QKV, k)
        rs_2(SMALL, k)
    squares = rs_4(DOWN) + rs_4(UP)
    for k in order:
        rs_3(QKV, k)
        rs_3(SMALL, k)
    squares = squares + rs_4(OUT) + rs_4(QKV) + rs_4(SMALL)

    row_id = lax.broadcasted_iota(jnp.int32, (8, 128), 0)
    tiles[0] = jnp.where(row_id == 7, squares, small_sum[...])
    for k in range(3):
        send("end", tiles.at[0], tiles.at[1 + k], tile_s.at[k], tile_r.at[k], (dp, rs_z(k + 1)))
    for k in range(3):
        landed(tiles.at[1 + k], tile_r.at[k])
    for k in range(4):
        vec_tiles[ag_z(k)] = tiles[k]
    total = tiles[0] + tiles[1] + tiles[2] + tiles[3]
    for step, bit in enumerate((1, 2, 4)):
        mine, theirs = tiles.at[4 + 2 * step], tiles.at[5 + 2 * step]
        mine[...] = total
        send("end", mine, theirs, tile_s.at[3 + step], tile_r.at[3 + step], (flip(dp, bit), mp))
        landed(theirs, tile_r.at[3 + step])
        total = total + theirs[...]
    norm_ref[...] = total
    for tag in ("kv", "rs", "end"):
        sent(tag)
    landed(act_out, move_r.at[2])
    landed(fg_out, move_r.at[3])

    @pl.when(mover)
    def _():
        for slot_at, src, dst in (
            (0, fm_in, fmx),
            (1, cot_in, cotx),
            (2, stage_act, act_out),
            (3, stage_fg, fg_out),
        ):
            remote(src, dst, move_s.at[slot_at], move_r.at[slot_at], swap_with).wait_send()


def run_layer(share, fm, cot, qkv, out, up, down, biases, vectors):
    tall, width = cot.shape
    heads = biases.shape[0]
    rows = qkv.shape[0]
    columns = (128, qkv.shape[1], out.shape[0], up.shape[1], down.shape[0])
    types = (f32, bf16, bf16, bf16, bf16)
    heights = (16, rows, rows, rows, rows)
    weights = [
        pltpu.VMEM((4, 4, 2, n, c), t) for n, c, t in zip(heights, columns, types)
    ] + [pltpu.VMEM((4, 4, 2, 8, 128), f32)]
    pieces = list(zip((8, rows, rows, rows, rows), columns, types))
    arrivals = [
        pltpu.VMEM((*lead, n, c), t)
        for lead in ((4, 4), (4,), (4,), (4,), (3,))
        for n, c, t in pieces
    ]
    activations = [
        pltpu.VMEM(fm.shape, bf16),
        pltpu.VMEM(cot.shape, bf16),
        pltpu.VMEM((share, width), bf16),
        pltpu.VMEM((4, heads, share, 128), bf16),
        pltpu.VMEM((4, heads, tall, 128), bf16),
        pltpu.VMEM((4, heads, tall, 128), bf16),
        pltpu.VMEM((4, share, heads * HD), bf16),
        pltpu.VMEM((4, heads, 1, share), f32),
        pltpu.VMEM((heads, HD, share), f32),
        pltpu.VMEM((share, width), f32),
        pltpu.VMEM((share, 1), f32),
        pltpu.VMEM((share, width), bf16),
        pltpu.VMEM((4, tall, up.shape[1]), bf16),
        pltpu.VMEM((4, tall, up.shape[1]), bf16),
        pltpu.VMEM((share, width), f32),
        pltpu.VMEM((share, width), bf16),
        pltpu.VMEM((4, heads, share, 128), bf16),
        pltpu.VMEM((share, qkv.shape[1]), bf16),
        pltpu.VMEM((share, width), f32),
        pltpu.VMEM((share, width), f32),
        pltpu.VMEM((8, width), f32),
        pltpu.VMEM((4, 8, 384), f32),
        pltpu.VMEM((8, width), f32),
        pltpu.VMEM((4, 8, 384), f32),
        pltpu.VMEM((10, 8, 128), f32),
    ]
    semaphores = [pltpu.SemaphoreType.DMA((5, SEMS)) for _ in range(4)] + [
        pltpu.SemaphoreType.DMA((n,)) for n in (8, 8, 4, 4, 6, 6)
    ]
    anywhere = pl.BlockSpec(memory_space=pl.ANY)
    vmem = pl.BlockSpec(memory_space=pltpu.VMEM)
    shapes = [
        (share, width),
        (share, width),
        (rows, columns[QKV]),
        (rows, columns[OUT]),
        (rows, columns[UP]),
        (rows, columns[DOWN]),
        (8, 128),
        (8, 128),
        (4, 8, 128),
    ]
    return pl.pallas_call(
        functools.partial(layer_kernel, share),
        out_shape=tuple(jax.ShapeDtypeStruct(s, f32) for s in shapes),
        in_specs=[anywhere] * 2 + [vmem] * 6,
        out_specs=(anywhere,) * 2 + (vmem,) * 7,
        scratch_shapes=weights + arrivals + activations + semaphores,
        compiler_params=pltpu.CompilerParams(
            collective_id=0, has_side_effects=True, vmem_limit_bytes=60 * 2**20
        ),
        name="encoder_layer",
    )(fm, cot, qkv, out, up, down, biases, vectors)


def on_device_fast(
    frames,
    span_mask,
    cotangent,
    qkv_weight,
    qkv_mean,
    qkv_square,
    out_weight,
    out_mean,
    out_square,
    up_weight,
    up_mean,
    up_square,
    down_weight,
    down_mean,
    down_square,
    head_biases,
    bias_mean,
    bias_square,
    norm_vectors,
    vector_mean,
    vector_square,
):
    mp = lax.axis_index("mp")
    share = frames.shape[0]
    local_heads, bias_cut = head_biases.shape
    vec_cut = norm_vectors.shape[1]
    mask_rows = lax.dynamic_slice_in_dim(span_mask.reshape(-1), mp * share, share, 0)
    flags = jnp.broadcast_to(mask_rows[:, None].astype(bf16), (share, 128))
    tail = ((0, -share % 16), (0, 0))
    fm = jnp.pad(jnp.concatenate([frames, flags], axis=1), tail)
    cot = jnp.pad(cotangent, tail)
    outputs, frame_grad, qkv_sum, out_sum, up_sum, down_sum, small_sum, norm_tile, vec_tiles = (
        run_layer(
            share, fm, cot, qkv_weight, out_weight, up_weight, down_weight, head_biases, norm_vectors
        )
    )
    grad_norm = jnp.sqrt(norm_tile[7, 0])
    vector_grad = vec_tiles[:, 4:6, :vec_cut].reshape(8, vec_cut)[:7]
    bias_grad = small_sum[:local_heads, :bias_cut]
    factor = jnp.minimum(1.0, clip_limit / (grad_norm + 1e-06))
    masters = (qkv_weight, out_weight, up_weight, down_weight, head_biases, norm_vectors)
    gradients = (qkv_sum, out_sum.T, up_sum, down_sum.T, bias_grad, vector_grad)
    means = (qkv_mean, out_mean, up_mean, down_mean, bias_mean, vector_mean)
    squares = (qkv_square, out_square, up_square, down_square, bias_square, vector_square)
    updated = []
    for index_at in range(6):
        updated.extend(
            adam_step(
                masters[index_at],
                means[index_at],
                squares[index_at],
                gradients[index_at],
                factor,
                settings[index_at][0],
                settings[index_at][1],
            )
        )
    return (outputs, frame_grad, grad_norm, *updated)


def solution(mesh):
    return jax.shard_map(
        on_device_fast if fast_fits(mesh) else on_device,
        mesh=mesh,
        in_specs=(
            P(("dp", "mp"), None),
            P("dp", None),
            P(("dp", "mp"), None),
            P("dp", "mp"),
            P("dp", "mp"),
            P("dp", "mp"),
            P("mp", "dp"),
            P("mp", "dp"),
            P("mp", "dp"),
            P("dp", "mp"),
            P("dp", "mp"),
            P("dp", "mp"),
            P("mp", "dp"),
            P("mp", "dp"),
            P("mp", "dp"),
            P("mp", "dp"),
            P("mp", "dp"),
            P("mp", "dp"),
            P(None, "dp"),
            P(None, "dp"),
            P(None, "dp"),
        ),
        out_specs=(
            P(("dp", "mp"), None),
            P(("dp", "mp"), None),
            P(),
            P("dp", "mp"),
            P("dp", "mp"),
            P("dp", "mp"),
            P("mp", "dp"),
            P("mp", "dp"),
            P("mp", "dp"),
            P("dp", "mp"),
            P("dp", "mp"),
            P("dp", "mp"),
            P("mp", "dp"),
            P("mp", "dp"),
            P("mp", "dp"),
            P("mp", "dp"),
            P("mp", "dp"),
            P("mp", "dp"),
            P(None, "dp"),
            P(None, "dp"),
            P(None, "dp"),
        ),
        check_vma=False,
    )
```

```python
import functools

import jax
import jax.numpy as jnp
from jax import lax
from jax.experimental import pallas as pl
from jax.experimental.pallas import tpu as pltpu
from jax.sharding import PartitionSpec as P

HD = 64
LEN = 688


norm_eps = 1e-05
adam_eps = 1e-08
beta_one = 0.9
beta_two = 0.999
step_count = 10.0
clip_limit = 1.0
settings = ((0.05, 0.1), (0.3, 0.1), (0.05, 0.1), (0.03, 0.1), (0.3, 0.0), (0.4, 0.0))


def norm_rows(values, norm_gain, norm_shift):
    centred = values - jnp.mean(values, axis=-1, keepdims=True)
    variance = jnp.mean(centred * centred, axis=-1, keepdims=True)
    inverse = lax.rsqrt(variance + norm_eps)
    normed = centred * inverse
    return (normed * norm_gain + norm_shift, normed, inverse)


def norm_back(upstream, normed, inverse, norm_gain):
    scaled = upstream * norm_gain
    inner_part = (
        scaled
        - jnp.mean(scaled, axis=-1, keepdims=True)
        - normed * jnp.mean(scaled * normed, axis=-1, keepdims=True)
    )
    return (inverse * inner_part, jnp.sum(upstream * normed, axis=0), jnp.sum(upstream, axis=0))


def gelu_slope(pre_act):
    cumulative = 0.5 * (1.0 + jax.scipy.special.erf(pre_act * 0.7071067811865476))
    return cumulative + pre_act * jnp.exp(-0.5 * pre_act * pre_act) * 0.3989422804014327


def attend_forward(clip_block):
    scaling = HD ** (-0.5)
    queries = clip_block[:, :, 0]
    key_rows = clip_block[:, :, 1]
    value_rows = clip_block[:, :, 2]
    scores = (
        jnp.einsum("qhe,khe->hqk", queries, key_rows, preferred_element_type=jnp.float32) * scaling
    )
    row_peak = jnp.max(scores, axis=-1, keepdims=True)
    log_total = row_peak + jnp.log(jnp.sum(jnp.exp(scores - row_peak), axis=-1, keepdims=True))
    attention = jnp.exp(scores - log_total).astype(jnp.bfloat16)
    mixed_rows = jnp.einsum(
        "hqk,khe->qhe", attention, value_rows, preferred_element_type=jnp.float32
    )
    return (mixed_rows.astype(jnp.bfloat16).reshape(clip_block.shape[0], -1), log_total)


def attend_backward(pieces):
    clip_block, log_total, grad_mixed = pieces
    scaling = HD ** (-0.5)
    queries = clip_block[:, :, 0]
    key_rows = clip_block[:, :, 1]
    value_rows = clip_block[:, :, 2]
    scores = (
        jnp.einsum("qhe,khe->hqk", queries, key_rows, preferred_element_type=jnp.float32) * scaling
    )
    attention = jnp.exp(scores - log_total)
    attention_low = attention.astype(jnp.bfloat16)
    mixed_rows = jnp.einsum(
        "hqk,khe->qhe", attention_low, value_rows, preferred_element_type=jnp.float32
    ).astype(jnp.bfloat16)
    grad_rows = grad_mixed.reshape(queries.shape)
    grad_attention = jnp.einsum(
        "qhe,khe->hqk", grad_rows, value_rows, preferred_element_type=jnp.float32
    )
    grad_values = jnp.einsum(
        "hqk,qhe->khe", attention_low, grad_rows, preferred_element_type=jnp.float32
    )
    row_inner = jnp.sum(attention * grad_attention, axis=-1, keepdims=True)
    grad_scores = (attention * (grad_attention - row_inner)).astype(jnp.bfloat16)
    grad_queries = (
        jnp.einsum("hqk,khe->qhe", grad_scores, key_rows, preferred_element_type=jnp.float32)
        * scaling
    )
    grad_keys = (
        jnp.einsum("hqk,qhe->khe", grad_scores, queries, preferred_element_type=jnp.float32)
        * scaling
    )
    grad_block = jnp.stack([grad_queries, grad_keys, grad_values], axis=2).astype(jnp.bfloat16)
    return (
        mixed_rows.reshape(clip_block.shape[0], -1),
        grad_block.reshape(clip_block.shape[0], -1),
    )


def adam_step(weight, mean_old, square_old, gradient, factor, rate, decay):
    clipped = gradient * factor
    mean_new = beta_one * mean_old + (1.0 - beta_one) * clipped
    square_new = beta_two * square_old + (1.0 - beta_two) * clipped * clipped
    mean_hat = mean_new / (1.0 - beta_one**step_count)
    square_hat = square_new / (1.0 - beta_two**step_count)
    weight_new = weight - rate * (mean_hat / (jnp.sqrt(square_hat) + adam_eps) + decay * weight)
    return (weight_new, mean_new, square_new)


def on_device(
    frames,
    span_mask,
    cotangent,
    qkv_weight,
    qkv_mean,
    qkv_square,
    out_weight,
    out_mean,
    out_square,
    up_weight,
    up_mean,
    up_square,
    down_weight,
    down_mean,
    down_square,
    head_biases,
    bias_mean,
    bias_square,
    norm_vectors,
    vector_mean,
    vector_square,
):
    masters = (qkv_weight, out_weight, up_weight, down_weight, head_biases, norm_vectors)
    lowered = tuple((weight.astype(jnp.bfloat16) for weight in masters))
    qkv_full, out_full, up_full, down_full, bias_full, vector_full = (
        lax.all_gather(lowered[0], "dp", axis=0, tiled=True),
        lax.all_gather(lowered[1], "dp", axis=1, tiled=True),
        lax.all_gather(lowered[2], "dp", axis=0, tiled=True),
        lax.all_gather(lowered[3], "dp", axis=1, tiled=True),
        lax.all_gather(lowered[4], "dp", axis=1, tiled=True),
        lax.all_gather(lowered[5], "dp", axis=1, tiled=True),
    )
    share_rows = frames.shape[0]
    start_row = lax.axis_index("mp") * share_rows
    vectors = vector_full.astype(jnp.float32)
    local_heads = bias_full.shape[0]

    def share_of(array_full):
        return lax.dynamic_slice_in_dim(array_full, start_row, share_rows, 0)

    gathered = lax.all_gather(frames, "mp", axis=0, tiled=True)
    all_rows = gathered.shape[0]
    masked = span_mask.reshape(all_rows, 1) == 1
    inputs = jnp.where(masked, vectors[0], gathered.astype(jnp.float32))
    rounded = inputs.astype(jnp.bfloat16)
    zero_bias = jnp.zeros_like(bias_full[:, :HD])
    qkv_bias = (
        jnp.stack([bias_full[:, :HD], zero_bias, bias_full[:, HD : 2 * HD]], axis=1)
        .reshape(-1)
        .astype(jnp.float32)
    )
    up_bias = bias_full[:, 2 * HD :].reshape(-1).astype(jnp.float32)
    projected = (jnp.dot(rounded, qkv_full, preferred_element_type=jnp.float32) + qkv_bias).astype(
        jnp.bfloat16
    )
    blocks = projected.reshape(-1, LEN, local_heads, 3, HD)
    mixed_rows, log_total = lax.map(attend_forward, blocks)
    mixed_rows = mixed_rows.reshape(all_rows, -1)
    attn_part = jnp.dot(mixed_rows, out_full, preferred_element_type=jnp.float32)
    attended = lax.psum(attn_part, "mp")
    first_sum = inputs + attended + vectors[5]
    hidden, normed_full, inverse_full = norm_rows(first_sum, vectors[1], vectors[2])
    normed_one = share_of(normed_full)
    inverse_one = share_of(inverse_full)
    hidden_low = hidden.astype(jnp.bfloat16)
    pre_act = jnp.dot(hidden_low, up_full, preferred_element_type=jnp.float32) + up_bias
    activated = jax.nn.gelu(pre_act, approximate=False).astype(jnp.bfloat16)
    ffn_part = jnp.dot(activated, down_full, preferred_element_type=jnp.float32)
    second_sum = hidden + lax.psum(ffn_part, "mp") + vectors[6]
    outputs_full, normed_full, inverse_full = norm_rows(second_sum, vectors[3], vectors[4])
    outputs = share_of(outputs_full)
    normed_two = share_of(normed_full)
    inverse_two = share_of(inverse_full)
    qkv_full, out_full, up_full, down_full, bias_full, vector_full = (
        lax.all_gather(lowered[0], "dp", axis=0, tiled=True),
        lax.all_gather(lowered[1], "dp", axis=1, tiled=True),
        lax.all_gather(lowered[2], "dp", axis=0, tiled=True),
        lax.all_gather(lowered[3], "dp", axis=1, tiled=True),
        lax.all_gather(lowered[4], "dp", axis=1, tiled=True),
        lax.all_gather(lowered[5], "dp", axis=1, tiled=True),
    )
    upstream = cotangent.astype(jnp.float32)
    grad_two, grad_gain_two, grad_shift_two = norm_back(
        upstream, normed_two, inverse_two, vectors[3]
    )
    grad_down_bias = jnp.sum(grad_two, axis=0)
    grad_two_full = lax.all_gather(grad_two.astype(jnp.bfloat16), "mp", axis=0, tiled=True)
    pre_again = jnp.dot(hidden_low, up_full, preferred_element_type=jnp.float32) + up_bias
    act_again = jax.nn.gelu(pre_again, approximate=False).astype(jnp.bfloat16)
    grad_down = jnp.einsum(
        "tf,td->fd", act_again, grad_two_full, preferred_element_type=jnp.float32
    )
    grad_act = jnp.einsum("td,fd->tf", grad_two_full, down_full, preferred_element_type=jnp.float32)
    grad_pre = (grad_act * gelu_slope(pre_again)).astype(jnp.bfloat16)
    grad_up = jnp.einsum("td,tf->df", hidden_low, grad_pre, preferred_element_type=jnp.float32)
    grad_up_bias = jnp.sum(grad_pre, axis=0, dtype=jnp.float32)
    hidden_part = jnp.einsum("tf,df->td", grad_pre, up_full, preferred_element_type=jnp.float32)
    grad_hidden = grad_two + lax.psum_scatter(hidden_part, "mp", scatter_dimension=0, tiled=True)
    grad_one, grad_gain_one, grad_shift_one = norm_back(
        grad_hidden, normed_one, inverse_one, vectors[1]
    )
    grad_out_bias = jnp.sum(grad_one, axis=0)
    grad_one_full = lax.all_gather(grad_one.astype(jnp.bfloat16), "mp", axis=0, tiled=True)
    grad_mixed = jnp.einsum(
        "td,cd->tc", grad_one_full, out_full, preferred_element_type=jnp.float32
    ).astype(jnp.bfloat16)
    mixed_again, grad_blocks = lax.map(
        attend_backward, (blocks, log_total, grad_mixed.reshape(-1, LEN, grad_mixed.shape[1]))
    )
    mixed_again = mixed_again.reshape(all_rows, -1)
    grad_blocks = grad_blocks.reshape(all_rows, -1)
    grad_out = jnp.einsum(
        "tc,td->cd", mixed_again, grad_one_full, preferred_element_type=jnp.float32
    )
    grad_qkv = jnp.einsum("td,tc->dc", rounded, grad_blocks, preferred_element_type=jnp.float32)
    bias_sums = jnp.sum(grad_blocks, axis=0, dtype=jnp.float32).reshape(local_heads, 3, HD)
    grad_biases = jnp.concatenate(
        [bias_sums[:, 0], bias_sums[:, 2], grad_up_bias.reshape(local_heads, -1)], axis=1
    )
    input_part = jnp.einsum("tc,dc->td", grad_blocks, qkv_full, preferred_element_type=jnp.float32)
    grad_inputs = grad_one + lax.psum_scatter(
        input_part.astype(jnp.bfloat16), "mp", scatter_dimension=0, tiled=True
    ).astype(jnp.float32)
    masked_share = share_of(masked)
    grad_embed = jnp.sum(jnp.where(masked_share, grad_inputs, 0.0), axis=0)
    frame_grad = jnp.where(masked_share, 0.0, grad_inputs)
    grad_vectors = jnp.stack(
        [
            grad_embed,
            grad_gain_one,
            grad_shift_one,
            grad_gain_two,
            grad_shift_two,
            grad_out_bias,
            grad_down_bias,
        ]
    )
    reduced = (
        lax.psum_scatter(grad_qkv, "dp", scatter_dimension=0, tiled=True),
        lax.psum_scatter(grad_out, "dp", scatter_dimension=1, tiled=True),
        lax.psum_scatter(grad_up, "dp", scatter_dimension=0, tiled=True),
        lax.psum_scatter(grad_down, "dp", scatter_dimension=1, tiled=True),
        lax.psum_scatter(grad_biases, "dp", scatter_dimension=1, tiled=True),
    )
    local_squares = jnp.float32(0.0)
    for portion in reduced:
        local_squares = local_squares + jnp.sum(portion * portion)
    total_squares, vector_total = lax.psum((local_squares, grad_vectors), ("dp", "mp"))
    grad_norm = jnp.sqrt(total_squares + jnp.sum(vector_total * vector_total))
    column_count = norm_vectors.shape[1]
    vector_grad = lax.dynamic_slice_in_dim(
        vector_total, lax.axis_index("dp") * column_count, column_count, 1
    )
    factor = jnp.minimum(1.0, clip_limit / (grad_norm + 1e-06))
    gradients = (reduced[0], reduced[1], reduced[2], reduced[3], reduced[4], vector_grad)
    means = (qkv_mean, out_mean, up_mean, down_mean, bias_mean, vector_mean)
    squares = (qkv_square, out_square, up_square, down_square, bias_square, vector_square)
    updated = []
    for index_at in range(6):
        updated.extend(
            adam_step(
                masters[index_at],
                means[index_at],
                squares[index_at],
                gradients[index_at],
                factor,
                settings[index_at][0],
                settings[index_at][1],
            )
        )
    return (
        outputs,
        frame_grad,
        grad_norm,
        updated[0],
        updated[1],
        updated[2],
        updated[3],
        updated[4],
        updated[5],
        updated[6],
        updated[7],
        updated[8],
        updated[9],
        updated[10],
        updated[11],
        updated[12],
        updated[13],
        updated[14],
        updated[15],
        updated[16],
        updated[17],
    )


MESH = pl.DeviceIdType.MESH
SMALL, MIX, UP, DOWN = range(4)
SEMS = 24
f32, bf16 = jnp.float32, jnp.bfloat16


def fast_fits(mesh):
    return mesh.shape["dp"] == 8 and mesh.shape["mp"] == 4


def flip(dp, bit):
    held = lax.rem(lax.div(dp, bit), 2)
    return dp + bit - 2 * bit * held


def dg(a, b, ca, cb):
    return lax.dot_general(a, b, (((ca,), (cb,)), ((), ())), preferred_element_type=f32)


def landed(dst, sem):
    pltpu.make_async_copy(dst, dst, sem).wait()


def layer_kernel(
    share,
    frames_in,
    mask_in,
    cot_in,
    qkv_in,
    out_in,
    up_in,
    down_in,
    bias_in,
    vec_in,
    act_out,
    fg_out,
    small_sum,
    mix_sum,
    up_sum,
    down_sum,
    norm_ref,
    vec_tiles,
    ws,
    wm,
    wu,
    wd,
    gs,
    rcs,
    rcm,
    rcu,
    rcd,
    rds,
    rdm,
    rdu,
    rdd,
    rxs,
    rxm,
    rxu,
    rxd,
    rys,
    rym,
    ryu,
    ryd,
    rzs,
    rzm,
    rzu,
    rzd,
    fm_own,
    cot_own,
    fmx,
    cotx,
    x_low,
    q_all,
    kv_own,
    kv_far,
    mixed,
    lse,
    mix_t,
    n_one,
    r_one,
    hid_low,
    act,
    slope,
    acc,
    low,
    dm,
    dproj,
    stage_act,
    stage_fg,
    fg_far,
    vec,
    bias,
    gvec,
    gbias,
    tiles,
    gather_s,
    gather_r,
    reduce_s,
    reduce_r,
    kv_s,
    kv_r,
    move_s,
    move_r,
    tile_s,
    tile_r,
):
    T = share
    dp, mp = lax.axis_index("dp"), lax.axis_index("mp")
    core = lax.rem(dp, 2)
    dx, dy, dc = flip(dp, 2), flip(dp, 4), flip(dp, 1)
    dd = flip(dx, 4)
    planes = (mp, flip(mp, 1), flip(mp, 2), flip(flip(mp, 1), 2))
    mover = lax.rem(core + mp, 2) == 1
    stay = lax.rem(core + mp, 2) == 0
    swap_with = (dc, planes[1])
    full = (ws, wm, wu, wd)
    local = (gs, wm, wu, wd)
    from_core = (rcs, rcm, rcu, rcd)
    from_diag = (rds, rdm, rdu, rdd)
    from_x = (rxs, rxm, rxu, rxd)
    from_y = (rys, rym, ryu, ryd)
    from_z = (rzs, rzm, rzu, rzd)
    result = (small_sum, mix_sum, up_sum, down_sum)
    heads = q_all.shape[1]
    chunks = [(r, min(88, T - r)) for r in range(0, T, 88)]

    def remote(src, dst, send_sem, recv_sem, device):
        return pltpu.make_async_remote_copy(
            src_ref=src,
            dst_ref=dst,
            send_sem=send_sem,
            recv_sem=recv_sem,
            device_id=device,
            device_id_type=MESH,
        )

    pending = {}

    def send(tag, src, dst, sems, at, device):
        copy = remote(src, dst, sems[0].at[at], sems[1].at[at], device)
        copy.start()
        pending.setdefault(tag, []).append(copy)

    def sent(tag):
        for copy in pending.pop(tag, []):
            copy.wait_send()

    def hand_over(slot, src, dst):
        @pl.when(mover)
        def _():
            remote(src, dst, move_s.at[slot], move_r.at[slot], swap_with).start()

        @pl.when(stay)
        def _():
            pltpu.make_async_copy(src, dst, move_r.at[slot]).start()

    def halves(ref):
        n = ref.shape[-2]
        if n % 32:
            return ref, None
        return ref.at[pl.ds(0, n // 2)], ref.at[pl.ds(n // 2, n // 2)]

    gather = (gather_s, gather_r)

    def slot(w, k, d):
        return full[w].at[planes[k], lax.div(d, 2), lax.rem(d, 2)]

    def ag_own(w):
        for k in (1, 2, 3):
            send(("ag", w), slot(w, 0, dp), slot(w, 0, dp), gather, (w, k), (dp, planes[k]))

    def ag_a(w, k):
        ref = slot(w, k, dp)
        if k:
            landed(ref, gather_r.at[w, k])
        send(("ag", w), ref, ref, gather, (w, 4 + k), (dx, mp))
        send(("ag", w), ref, ref, gather, (w, 8 + k), (dy, mp))

    def ag_b(w, k):
        at_x, at_y = slot(w, k, dx), slot(w, k, dy)
        landed(at_x, gather_r.at[w, 4 + k])
        if k == 0:
            ref = halves(at_x)[0]
            send(("ag", w), ref, ref, gather, (w, 12), (dy, mp))
        if k == 2:
            send(("ag", w), at_x, at_x, gather, (w, 14), (dy, mp))
        landed(at_y, gather_r.at[w, 8 + k])
        if k == 0 and halves(at_y)[1] is not None:
            ref = halves(at_y)[1]
            send(("ag", w), ref, ref, gather, (w, 13), (dx, mp))
        if k == 3:
            send(("ag", w), at_y, at_y, gather, (w, 15), (dx, mp))

    def ag_c(w, k):
        ref = slot(w, k, dd)
        if k == 0:
            for i, half in enumerate(halves(ref)):
                if half is not None:
                    landed(half, gather_r.at[w, 12 + i])
            send(("ag", w), ref, ref, gather, (w, 16), (dp, planes[1]))
        elif k == 1:
            landed(ref, gather_r.at[w, 16])
        else:
            landed(ref, gather_r.at[w, 12 + k])
        ref = full[w].at[planes[k], :, core]
        send(("ag", w), ref, ref, gather, (w, 17 + k), (dc, mp))

    def ag_d(w, k):
        landed(full[w].at[planes[k], :, 1 - core], gather_r.at[w, 17 + k])

    order = (1, 2, 3, 0)
    reduce = (reduce_s, reduce_r)

    def part(w, k, d):
        return local[w].at[planes[k], lax.div(d, 2), lax.rem(d, 2)]

    def add_to(ref, arrived):
        ref[...] = ref[...] + arrived[...]

    def rs_0(w, k):
        send("rs", local[w].at[planes[k], :, 1 - core], from_core[w].at[k], reduce, (w, k), (dc, mp))

    def rs_1(w, k):
        landed(from_core[w].at[k], reduce_r.at[w, k])
        add_to(local[w].at[planes[k], :, core], from_core[w].at[k])
        at_d, at_x, at_y = part(w, k, dd), part(w, k, dx), part(w, k, dy)
        to_d, to_x, to_y = from_diag[w].at[k], from_x[w].at[k], from_y[w].at[k]
        if k == 1:
            send("rs", at_d, to_d, reduce, (w, 4), (dp, planes[1]))
            send("rs", at_x, to_x, reduce, (w, 10 + k), (dx, mp))
            send("rs", at_y, to_y, reduce, (w, 15 + k), (dy, mp))
        elif k == 2:
            send("rs", at_d, to_d, reduce, (w, 4 + k), (dy, mp))
            send("rs", at_y, to_y, reduce, (w, 15 + k), (dy, mp))
        elif k == 3:
            send("rs", at_d, to_d, reduce, (w, 4 + k), (dx, mp))
            send("rs", at_x, to_x, reduce, (w, 10 + k), (dx, mp))
        else:
            landed(from_diag[w].at[1], reduce_r.at[w, 4])
            add_to(at_d, from_diag[w].at[1])
            first, second = halves(at_d)
            send("rs", first, halves(to_d)[0], reduce, (w, 8), (dx, mp))
            if second is not None:
                send("rs", second, halves(to_d)[1], reduce, (w, 9), (dy, mp))
            send("rs", halves(at_x)[0], halves(to_x)[0], reduce, (w, 10), (dx, mp))
            if second is not None:
                send("rs", halves(at_y)[1], halves(to_y)[1], reduce, (w, 15), (dy, mp))

    def rs_2(w, k):
        at_x, at_y = part(w, k, dx), part(w, k, dy)
        come, to_x, to_y = from_diag[w].at[k], from_x[w].at[k], from_y[w].at[k]
        if k == 2:
            landed(come, reduce_r.at[w, 4 + k])
            add_to(at_x, come)
            send("rs", at_x, to_x, reduce, (w, 10 + k), (dx, mp))
        elif k == 3:
            landed(come, reduce_r.at[w, 4 + k])
            add_to(at_y, come)
            send("rs", at_y, to_y, reduce, (w, 15 + k), (dy, mp))
        elif k == 0:
            first, second = halves(come)
            landed(first, reduce_r.at[w, 8])
            add_to(halves(at_y)[0], first)
            send("rs", halves(at_y)[0], halves(to_y)[0], reduce, (w, 19), (dy, mp))
            if second is not None:
                landed(second, reduce_r.at[w, 9])
                add_to(halves(at_x)[1], second)
                send("rs", halves(at_x)[1], halves(to_x)[1], reduce, (w, 14), (dx, mp))

    def rs_3(w, k):
        if k:
            landed(from_x[w].at[k], reduce_r.at[w, 10 + k])
            landed(from_y[w].at[k], reduce_r.at[w, 15 + k])
        else:
            for i, half in enumerate(halves(from_x[w].at[0])):
                if half is not None:
                    landed(half, reduce_r.at[w, (10, 14)[i]])
            for i, half in enumerate(halves(from_y[w].at[0])):
                if half is not None:
                    landed(half, reduce_r.at[w, (19, 15)[i]])
        ref = part(w, k, dp)
        total = ref[...].astype(f32) + from_x[w][k].astype(f32) + from_y[w][k].astype(f32)
        if k:
            ref[...] = total.astype(ref.dtype)
            send("rs", ref, from_z[w].at[k - 1], reduce, (w, 19 + k), (dp, planes[k]))
        else:
            result[w][...] = total

    def rs_4(w):
        total = result[w][...]
        for k in (1, 2, 3):
            landed(from_z[w].at[k - 1], reduce_r.at[w, 19 + k])
            total = total + from_z[w][k - 1].astype(f32)
        result[w][...] = total
        return jnp.sum(total * total)

    own_j = lax.div(dp, 2)
    cut, vec_cut = bias_in.shape[1], vec_in.shape[1]
    width = frames_in.shape[1]
    ws[mp, own_j, core] = jnp.zeros(ws.shape[3:], f32)
    ws[mp, own_j, core, 0:heads, 0:cut] = bias_in[...].astype(bf16).astype(f32)
    ws[mp, own_j, core, 8:15, 0:vec_cut] = vec_in[...].astype(bf16).astype(f32)
    wm[mp, own_j, core] = jnp.concatenate([qkv_in[...], out_in[...].T], axis=1).astype(bf16)
    bar = pltpu.get_barrier_semaphore()
    group = [dc, dx, dy, dd, flip(dx, 1), flip(dy, 1), flip(dd, 1)]
    others = [(d, mp) for d in group] + [(dp, planes[k]) for k in (1, 2, 3)] + [swap_with]
    for device in others:
        pl.semaphore_signal(bar, inc=1, device_id=device, device_id_type=MESH)
    pl.semaphore_wait(bar, len(others))
    for w in (SMALL, MIX):
        ag_own(w)
        ag_a(w, 0)
    flags = mask_in[...].astype(f32)
    flags = jnp.where(lax.rem(mp, 2) == 0, flags[:, 0:T], flags[:, T : 2 * T])
    flags = jnp.where(lax.div(mp, 2) == 0, flags[0:1, :], flags[1:2, :])
    fm_own[0:T, 0:width] = frames_in[...]
    fm_own[0:T, width:] = jnp.broadcast_to(flags, (128, T)).T.astype(bf16)
    hand_over(0, fm_own, fmx)
    wu[mp, own_j, core] = up_in[...].astype(bf16)
    ag_own(UP)
    ag_a(UP, 0)
    wd[mp, own_j, core] = down_in[...].astype(bf16)
    ag_own(DOWN)
    ag_a(DOWN, 0)
    cot_own[0:T, :] = cot_in[...]
    hand_over(1, cot_own, cotx)
    for k in (1, 2, 3):
        ag_a(SMALL, k)
    ag_b(MIX, 0)
    for k in (1, 2, 3):
        ag_a(MIX, k)
    for k in range(4):
        ag_b(SMALL, k)
    for k in (1, 2, 3):
        ag_b(MIX, k)
    for k in (0, 2, 3, 1):
        ag_c(SMALL, k)
    ag_a(UP, 1)
    ag_b(UP, 0)
    for k in (0, 2, 3):
        ag_c(MIX, k)
    for k in (2, 3):
        ag_a(UP, k)
    ag_c(MIX, 1)
    for k in range(4):
        ag_d(SMALL, k)
    cells = [(j, c) for j in range(4) for c in range(2)]
    vec[...] = jnp.concatenate([ws[0, j, c, 8:16, 0:vec_cut] for j, c in cells], axis=1)
    for z in range(4):
        bias[z] = jnp.concatenate([ws[z, j, c, 0:8, 0:cut] for j, c in cells], axis=1)
    embed, gain_one, shift_one, gain_two, shift_two, out_add, down_add = (
        vec[i : i + 1, :] for i in range(7)
    )

    def masked_rows(r, n):
        flag = fmx[r : r + n, width:].astype(f32)
        return jnp.concatenate([flag] * (width // 128), axis=1) > 0.5

    def input_rows(r, n):
        return jnp.where(masked_rows(r, n), embed, fmx[r : r + n, 0:width].astype(f32))

    landed(fmx, move_r.at[0])
    for r, n in chunks:
        x_low[r : r + n, :] = input_rows(r, n).astype(bf16)

    lane = lax.broadcasted_iota(jnp.int32, (1, 128), 1)
    forth = (0, 2, 3, 1)

    def weight(ref, z, first, last):
        return ref[z, :, :, :, first:last].reshape(width, last - first)

    qkv_wide = 192 * heads + 64
    out_first = 192 * heads - 64

    def project(k):
        z = planes[k]
        ag_d(MIX, k)
        slab = jnp.dot(x_low[...], weight(wm, z, 0, qkv_wide), preferred_element_type=f32)
        for h in range(heads):
            both = bias[z, h : h + 1, 0:128]
            head = slab[:, 192 * h : 192 * h + 128] + both
            head = head.astype(bf16).astype(f32) * HD ** (-0.5)
            q_all[z, h] = jnp.where(lane < HD, head, 0.0).astype(bf16)
            pair = slab[:, 192 * h + 64 : 192 * h + 192] + jnp.where(lane < HD, 0.0, both)
            kv_own[z, h, 0:T, :] = pair.astype(bf16)
        send("kv", kv_own.at[z], kv_far.at[z], (kv_s, kv_r), (k,), (dc, mp))

    project(0)
    ag_a(DOWN, 1)
    project(2)
    ag_b(DOWN, 0)
    ag_b(UP, 1)
    project(3)
    ag_a(DOWN, 2)
    project(1)
    ag_a(DOWN, 3)

    def stand(value):
        flat = value.reshape(heads * HD, T)
        return jnp.concatenate([jnp.zeros((HD, T), f32), flat], axis=0).T.astype(bf16)

    def attend(k):
        z = planes[k]
        landed(kv_far.at[z], kv_r.at[k])

        @pl.loop(0, heads)
        def _(h):
            queries = q_all[z, h]
            own, far = kv_own[z, h, 0:T, :], kv_far[z, h, 0:T, :]
            s_own, s_far = dg(own, queries, 1, 1), dg(far, queries, 1, 1)
            peak = jnp.maximum(
                jnp.max(s_own, axis=0, keepdims=True), jnp.max(s_far, axis=0, keepdims=True)
            )
            e_own, e_far = jnp.exp(s_own - peak), jnp.exp(s_far - peak)
            total = jnp.sum(e_own, axis=0, keepdims=True) + jnp.sum(e_far, axis=0, keepdims=True)
            lse[z, h] = peak + jnp.log(total)
            scale = 1.0 / total
            mix = dg(own, (e_own * scale).astype(bf16), 0, 0)
            mix = mix + dg(far, (e_far * scale).astype(bf16), 0, 0)
            mix_t[h] = mix[HD:, :]

        mixed[z] = stand(mix_t[...])

    attend(0)
    ag_b(UP, 2)
    attend(2)
    ag_b(UP, 3)
    attend(3)
    ag_c(UP, 0)
    attend(1)
    for i, k in enumerate(forth):
        piece = dg(mixed[planes[k]], weight(wm, planes[k], out_first, width), 1, 1)
        acc[...] = piece if i == 0 else acc[...] + piece
    ag_c(UP, 2)
    for r, n in chunks:
        v = input_rows(r, n) + acc[r : r + n, :] + out_add
        v = v - jnp.mean(v, axis=-1, keepdims=True)
        inverse = lax.rsqrt(jnp.mean(v * v, axis=-1, keepdims=True) + norm_eps)
        normed = v * inverse
        n_one[r : r + n, :] = normed
        r_one[r : r + n, :] = inverse
        hid_low[r : r + n, :] = (normed * gain_one + shift_one).astype(bf16)
    ag_c(UP, 3)
    ag_c(UP, 1)

    def rise(k):
        z = planes[k]
        ag_d(UP, k)
        for h in range(heads):
            cols = slice(256 * h, 256 * h + 256)
            u = jnp.dot(
                hid_low[...], weight(wu, z, 256 * h, 256 * h + 256), preferred_element_type=f32
            )
            u = u + bias[z, h : h + 1, 128:384]
            cumulative = 0.5 * (1.0 + lax.erf(u * 0.7071067811865476))
            act[z, 0:T, cols] = (u * cumulative).astype(bf16)
            bell = jnp.exp(-0.5 * u * u) * 0.3989422804014327
            slope[z, 0:T, cols] = (cumulative + u * bell).astype(bf16)

    rise(0)
    ag_b(DOWN, 1)
    rise(2)
    ag_b(DOWN, 2)
    rise(3)
    ag_b(DOWN, 3)
    ag_c(DOWN, 0)
    rise(1)
    for k in (2, 3, 1):
        ag_c(DOWN, k)
    for i, k in enumerate(forth):
        ag_d(DOWN, k)
        piece = dg(act[planes[k], 0:T, :], weight(wd, planes[k], 0, up_in.shape[1]), 1, 1)
        acc[...] = piece if i == 0 else acc[...] + piece

    landed(cotx, move_r.at[1])
    sums = [jnp.zeros((1, width), f32) for _ in range(3)]
    for r, n in chunks:
        v = n_one[r : r + n, :] * gain_one + shift_one + acc[r : r + n, :] + down_add
        v = v - jnp.mean(v, axis=-1, keepdims=True)
        inverse = lax.rsqrt(jnp.mean(v * v, axis=-1, keepdims=True) + norm_eps)
        normed = v * inverse
        stage_act[r : r + n, :] = normed * gain_two + shift_two
        up = cotx[r : r + n, :].astype(f32)
        scaled = up * gain_two
        inner = jnp.mean(scaled * normed, axis=-1, keepdims=True)
        grad = inverse * (scaled - jnp.mean(scaled, axis=-1, keepdims=True) - normed * inner)
        acc[r : r + n, :] = grad
        low[r : r + n, :] = grad.astype(bf16)
        for i, term in enumerate((up * normed, up, grad)):
            sums[i] = sums[i] + jnp.sum(term, axis=0, keepdims=True)
    gvec[...] = jnp.zeros(gvec.shape, f32)
    gbias[...] = jnp.zeros(gbias.shape, f32)
    gvec[3:4, :], gvec[4:5, :], gvec[6:7, :] = sums
    hand_over(2, stage_act, act_out)
    for w in range(4):
        sent(("ag", w))

    def tiled(value):
        return value.reshape(4, 2, -1, value.shape[1])

    def fall(k):
        z = planes[k]
        grad = dg(low[...], weight(wd, z, 0, up_in.shape[1]), 1, 0)
        grad = (grad * slope[z, 0:T, :].astype(f32)).astype(bf16)
        slope[z, 0:T, :] = grad
        total = jnp.sum(grad.astype(f32), axis=0, keepdims=True)
        for h in range(heads):
            gbias[z, h : h + 1, 128:384] = total[:, 256 * h : 256 * h + 256]
        wd[z] = tiled(dg(low[...], act[z, 0:T, :], 0, 0).astype(bf16))
        rs_0(DOWN, k)

    def sink(k):
        z = planes[k]
        acc[...] = acc[...] + dg(slope[z, 0:T, :], weight(wu, z, 0, up_in.shape[1]), 1, 1)
        wu[z] = tiled(dg(hid_low[...], slope[z, 0:T, :], 0, 0).astype(bf16))
        rs_0(UP, k)

    fall(1)
    fall(2)
    rs_1(DOWN, 1)
    fall(3)
    rs_1(DOWN, 2)
    fall(0)
    rs_1(DOWN, 3)
    sink(1)
    rs_1(DOWN, 0)
    sink(2)
    rs_1(UP, 1)
    rs_2(DOWN, 2)
    sink(3)
    rs_1(UP, 2)
    rs_2(DOWN, 3)
    rs_3(DOWN, 1)
    sink(0)
    rs_1(UP, 3)

    sums = [jnp.zeros((1, width), f32) for _ in range(3)]
    for r, n in chunks:
        grad_in = acc[r : r + n, :]
        normed = n_one[r : r + n, :]
        scaled = grad_in * gain_one
        inner = jnp.mean(scaled * normed, axis=-1, keepdims=True)
        grad = r_one[r : r + n, :] * (
            scaled - jnp.mean(scaled, axis=-1, keepdims=True) - normed * inner
        )
        acc[r : r + n, :] = grad
        low[r : r + n, :] = grad.astype(bf16)
        for i, term in enumerate((grad_in * normed, grad_in, grad)):
            sums[i] = sums[i] + jnp.sum(term, axis=0, keepdims=True)
    gvec[1:2, :], gvec[2:3, :], gvec[5:6, :] = sums
    rs_1(UP, 0)
    rs_2(DOWN, 0)

    for k in order:
        z = planes[k]
        grad = dg(low[...], weight(wm, z, out_first, width), 1, 0).astype(bf16).astype(f32)
        for h in range(heads):
            if h % 2 == 0:
                head = grad[:, HD * h : HD * h + 128]
            else:
                piece = grad[:, HD * h + HD : HD * h + 2 * HD]
                head = jnp.concatenate([piece, piece], axis=1)
            dm[z, h] = jnp.where(lane < HD, 0.0, head).astype(bf16)
    rs_3(DOWN, 2)
    rs_2(UP, 2)

    def attend_back(k):
        z = planes[k]

        @pl.loop(0, heads)
        def _(h):
            queries, gm = q_all[z, h], dm[z, h]
            own, far = kv_own[z, h, 0:T, :], kv_far[z, h, 0:T, :]
            level = lse[z, h]
            p_own = jnp.exp(dg(own, queries, 1, 1) - level)
            p_far = jnp.exp(dg(far, queries, 1, 1) - level)
            g_own, g_far = dg(own, gm, 1, 1), dg(far, gm, 1, 1)
            inner = jnp.sum(p_own * g_own, axis=0, keepdims=True)
            inner = inner + jnp.sum(p_far * g_far, axis=0, keepdims=True)
            s_own = (p_own * (g_own - inner)).astype(bf16)
            s_far = (p_far * (g_far - inner)).astype(bf16)
            pair_far = jnp.dot(s_far, queries, preferred_element_type=f32)
            pair_far = pair_far + jnp.dot(p_far.astype(bf16), gm, preferred_element_type=f32)
            pair_own = jnp.dot(s_own, queries, preferred_element_type=f32)
            pair_own = pair_own + jnp.dot(p_own.astype(bf16), gm, preferred_element_type=f32)
            at = pl.multiple_of(128 * h, 128)
            slope[z, 0:T, pl.ds(at, 128)] = pair_far.astype(bf16)
            slope[z, 0:T, pl.ds(pl.multiple_of(128 * heads + at, 128), 128)] = pair_own.astype(bf16)
            grad_q = dg(own, s_own, 0, 0) + dg(far, s_far, 0, 0)
            mix_t[h] = grad_q[0:HD, :] * HD ** (-0.5)

        act[z, 0:T, 128 * heads : 192 * heads] = mix_t[...].reshape(heads * HD, T).T.astype(bf16)
        send(
            "rs",
            slope.at[z, :, 0 : 128 * heads],
            act.at[z, :, 0 : 128 * heads],
            (kv_s, kv_r),
            (4 + k,),
            (dc, mp),
        )

    attend_back(1)
    rs_3(DOWN, 3)
    rs_2(UP, 3)
    attend_back(2)
    rs_3(DOWN, 0)
    rs_3(UP, 1)
    attend_back(3)
    rs_2(UP, 0)
    attend_back(0)
    rs_3(UP, 2)

    def project_back(k):
        z = planes[k]
        landed(act.at[z, :, 0 : 128 * heads], kv_r.at[4 + k])
        pieces = []
        for h in range(heads):
            at = 128 * heads + HD * h
            pieces.append(act[z, 0:T, at : at + HD].astype(f32))
            far = act[z, 0:T, 128 * h : 128 * h + 128].astype(f32)
            at = 128 * (heads + h)
            pieces.append(far + slope[z, 0:T, at : at + 128].astype(f32))
        pieces.append(jnp.zeros((T, HD), f32))
        slab = jnp.concatenate(pieces, axis=1).astype(bf16)
        dproj[...] = slab
        total = jnp.sum(slab.astype(f32), axis=0, keepdims=True)
        for h in range(heads):
            gbias[z, h : h + 1, 0:128] = jnp.concatenate(
                [total[:, 192 * h : 192 * h + 64], total[:, 192 * h + 128 : 192 * h + 192]], axis=1
            )
        acc[...] = acc[...] + dg(dproj[...], weight(wm, z, 0, qkv_wide), 1, 1)
        grad_qkv = dg(x_low[...], dproj[...], 0, 0)
        grad_out = dg(low[...], mixed[z], 0, 0)
        wm[z, :, :, :, 0:out_first] = tiled(grad_qkv[:, 0:out_first].astype(bf16))
        both = grad_qkv[:, out_first:] + grad_out[:, 0:128]
        wm[z, :, :, :, out_first:qkv_wide] = tiled(both.astype(bf16))
        wm[z, :, :, :, qkv_wide:] = tiled(grad_out[:, 128:].astype(bf16))
        rs_0(MIX, k)

    project_back(1)
    project_back(2)
    rs_1(MIX, 1)
    rs_3(UP, 3)
    project_back(3)
    rs_1(MIX, 2)
    project_back(0)
    rs_1(MIX, 3)
    rs_3(UP, 0)

    embed_sum = jnp.zeros((1, width), f32)
    for r, n in chunks:
        hidden_rows = masked_rows(r, n)
        grad = acc[r : r + n, :]
        stage_fg[r : r + n, :] = jnp.where(hidden_rows, 0.0, grad)
        embed_sum = embed_sum + jnp.sum(
            jnp.where(hidden_rows, grad, 0.0), axis=0, keepdims=True
        )
    gvec[0:1, :] = embed_sum

    @pl.when(mover)
    def _():
        remote(cot_own, cotx, move_s.at[1], move_r.at[1], swap_with).wait_send()
        cot_own[0:T, :] = stage_fg[...].astype(bf16)
        remote(cot_own, fg_far, move_s.at[3], move_r.at[4], swap_with).start()

    @pl.when(stay)
    def _():
        pltpu.make_async_copy(stage_fg, fg_out, move_r.at[3]).start()

    gs[...] = jnp.zeros(gs.shape, f32)
    for d, (j, c) in enumerate(cells):
        vectors = gvec[:, vec_cut * d : vec_cut * (d + 1)]
        for z in range(4):
            gs[z, j, c, 0:4, 0:cut] = gbias[z, 0:4, cut * d : cut * (d + 1)]
            gs[z, j, c, 4:6, 0:vec_cut] = vectors[2 * z : 2 * z + 2, :]
    for k in order:
        rs_0(SMALL, k)
    rs_1(MIX, 0)
    for k in order:
        rs_1(SMALL, k)
    rs_2(MIX, 2)
    rs_2(MIX, 3)
    for k in (2, 3, 0):
        rs_2(SMALL, k)
    squares = rs_4(DOWN)
    rs_3(MIX, 1)
    rs_2(MIX, 0)
    squares = squares + rs_4(UP)

    @pl.when(mover)
    def _():
        landed(fg_far, move_r.at[4])
        stage_fg[...] = fg_far[0:T, :].astype(f32)
        pltpu.make_async_copy(stage_fg, fg_out, move_r.at[3]).start()

    for k in order:
        rs_3(SMALL, k)
        if k != 1:
            rs_3(MIX, k)
    squares = squares + rs_4(MIX) + rs_4(SMALL)

    row_id = lax.broadcasted_iota(jnp.int32, (8, 128), 0)
    tiles[0] = jnp.where(row_id == 7, squares, small_sum[...])
    for k in (1, 2, 3):
        send("end", tiles.at[0], tiles.at[k], (tile_s, tile_r), (k,), (dp, planes[k]))
    for k in (1, 2, 3):
        landed(tiles.at[k], tile_r.at[k])
    for k in range(4):
        vec_tiles[planes[k]] = tiles[k]
    tiles[4] = vec_tiles[0] + vec_tiles[1] + vec_tiles[2] + vec_tiles[3]
    for i, d in enumerate(group):
        send("end", tiles.at[4], tiles.at[5 + i], (tile_s, tile_r), (4 + i,), (d, mp))
    for i in range(7):
        landed(tiles.at[5 + i], tile_r.at[4 + i])
    pairs = [tiles[4] + tiles[5], tiles[6] + tiles[9], tiles[7] + tiles[10], tiles[8] + tiles[11]]
    norm_ref[...] = (pairs[0] + pairs[1]) + (pairs[2] + pairs[3])
    for tag in ("kv", "rs", "end"):
        sent(tag)
    landed(act_out, move_r.at[2])
    landed(fg_out, move_r.at[3])

    @pl.when(mover)
    def _():
        remote(fm_own, fmx, move_s.at[0], move_r.at[0], swap_with).wait_send()
        remote(stage_act, act_out, move_s.at[2], move_r.at[2], swap_with).wait_send()
        remote(cot_own, fg_far, move_s.at[3], move_r.at[4], swap_with).wait_send()


def run_layer(share, frames, mask, cot, qkv, out, up, down, biases, vectors):
    width = frames.shape[1]
    tall = share + -share % 16
    heads = biases.shape[0]
    rows = qkv.shape[0]
    wide = up.shape[1]
    columns = (128, width, wide, wide)
    types = (f32, bf16, bf16, bf16)
    heights = (16, rows, rows, rows)
    weights = [
        pltpu.VMEM((4, 4, 2, n, c), t) for n, c, t in zip(heights, columns, types)
    ] + [pltpu.VMEM((4, 4, 2, 8, 128), f32)]
    pieces = list(zip((8, rows, rows, rows), columns, types))
    arrivals = [
        pltpu.VMEM((*lead, n, c), t)
        for lead in ((4, 4), (4,), (4,), (4,), (3,))
        for n, c, t in pieces
    ]
    activations = [
        pltpu.VMEM((tall, width + 128), bf16),
        pltpu.VMEM((tall, width), bf16),
        pltpu.VMEM((tall, width + 128), bf16),
        pltpu.VMEM((tall, width), bf16),
        pltpu.VMEM((share, width), bf16),
        pltpu.VMEM((4, heads, share, 128), bf16),
        pltpu.VMEM((4, heads, tall, 128), bf16),
        pltpu.VMEM((4, heads, tall, 128), bf16),
        pltpu.VMEM((4, share, heads * HD + HD), bf16),
        pltpu.VMEM((4, heads, 1, share), f32),
        pltpu.VMEM((heads, HD, share), f32),
        pltpu.VMEM((share, width), f32),
        pltpu.VMEM((share, 1), f32),
        pltpu.VMEM((share, width), bf16),
        pltpu.VMEM((4, tall, wide), bf16),
        pltpu.VMEM((4, tall, wide), bf16),
        pltpu.VMEM((share, width), f32),
        pltpu.VMEM((share, width), bf16),
        pltpu.VMEM((4, heads, share, 128), bf16),
        pltpu.VMEM((share, qkv.shape[1] + HD), bf16),
        pltpu.VMEM((share, width), f32),
        pltpu.VMEM((share, width), f32),
        pltpu.VMEM((tall, width), bf16),
        pltpu.VMEM((8, width), f32),
        pltpu.VMEM((4, 8, 384), f32),
        pltpu.VMEM((8, width), f32),
        pltpu.VMEM((4, 8, 384), f32),
        pltpu.VMEM((12, 8, 128), f32),
    ]
    semaphores = [pltpu.SemaphoreType.DMA((4, SEMS)) for _ in range(4)] + [
        pltpu.SemaphoreType.DMA((n,)) for n in (8, 8, 5, 5, 12, 12)
    ]
    anywhere = pl.BlockSpec(memory_space=pl.ANY)
    vmem = pl.BlockSpec(memory_space=pltpu.VMEM)
    shapes = [
        (share, width),
        (share, width),
        (8, 128),
        (rows, width),
        (rows, wide),
        (rows, wide),
        (8, 128),
        (4, 8, 128),
    ]
    return pl.pallas_call(
        functools.partial(layer_kernel, share),
        out_shape=tuple(jax.ShapeDtypeStruct(s, f32) for s in shapes),
        in_specs=[vmem] * 9,
        out_specs=(anywhere,) * 2 + (vmem,) * 6,
        scratch_shapes=weights + arrivals + activations + semaphores,
        compiler_params=pltpu.CompilerParams(
            collective_id=0, has_side_effects=True, vmem_limit_bytes=60 * 2**20
        ),
        name="encoder_layer",
    )(frames, mask, cot, qkv, out, up, down, biases, vectors)


def update_kernel(*refs):
    given, made = refs[:26], refs[26:47]
    held, ready = refs[47:73], refs[73:92]
    come, leave = refs[92:]
    arriving = [
        pltpu.make_async_copy(src, dst, come.at[i]) for i, (src, dst) in enumerate(zip(given, held))
    ]
    for copy in arriving:
        copy.start()
    leaving = []

    def out(src, i):
        copy = pltpu.make_async_copy(src, made[i], leave.at[i])
        copy.start()
        leaving.append(copy)

    for copy in arriving[:6]:
        copy.wait()
    small, mix, up, down, norm, vec_tiles = held[:6]
    state = held[8:]
    grad_norm = jnp.sqrt(norm[7:8, 0:1])
    ready[0][...] = grad_norm
    out(ready[0], 0)
    factor = jnp.minimum(1.0, clip_limit / (grad_norm + 1e-06))
    qkv_columns = state[0].shape[1]
    first = mix.shape[1] - state[3].shape[0] - HD
    heads, cut = state[12].shape
    vec_rows, vec_cut = state[15].shape
    gradients = (
        lambda: mix[:, 0:qkv_columns],
        lambda: mix[:, first:].T[HD:, :],
        lambda: up[...],
        lambda: down[...],
        lambda: small[0:heads, 0:cut],
        lambda: jnp.concatenate([vec_tiles[z, 4:6, 0:vec_cut] for z in range(4)], axis=0)[0:vec_rows, :],
    )
    for i in (2, 3, 0, 1, 4, 5):
        old = state[3 * i : 3 * i + 3]
        for copy in arriving[8 + 3 * i : 11 + 3 * i]:
            copy.wait()
        values = adam_step(*(ref[...] for ref in old), gradients[i](), factor, *settings[i])
        for at, value in enumerate(values):
            ready[1 + 3 * i + at][...] = value
            out(ready[1 + 3 * i + at], 3 + 3 * i + at)
    for at in range(2):
        arriving[6 + at].wait()
        out(held[6 + at], 1 + at)
    for copy in leaving:
        copy.wait()


def run_update(sums, norm, vec_tiles, act, fg, state):
    anywhere = pl.BlockSpec(memory_space=pl.ANY)
    given = (*sums, norm, vec_tiles, act, fg, *state)
    shapes = [(1, 1), act.shape, fg.shape] + [a.shape for a in state]
    return pl.pallas_call(
        update_kernel,
        out_shape=tuple(jax.ShapeDtypeStruct(s, f32) for s in shapes),
        in_specs=[anywhere] * len(given),
        out_specs=(anywhere,) * len(shapes),
        scratch_shapes=[pltpu.VMEM(a.shape, f32) for a in given]
        + [pltpu.VMEM(s, f32) for s in shapes[:1] + shapes[3:]]
        + [pltpu.SemaphoreType.DMA((len(given),)), pltpu.SemaphoreType.DMA((len(shapes),))],
        compiler_params=pltpu.CompilerParams(vmem_limit_bytes=60 * 2**20),
        name="update_weights",
    )(*given)


def on_device_fast(
    frames,
    span_mask,
    cotangent,
    qkv_weight,
    qkv_mean,
    qkv_square,
    out_weight,
    out_mean,
    out_square,
    up_weight,
    up_mean,
    up_square,
    down_weight,
    down_mean,
    down_square,
    head_biases,
    bias_mean,
    bias_square,
    norm_vectors,
    vector_mean,
    vector_square,
):
    share = frames.shape[0]
    act, fg, *sums, norm, vec_tiles = run_layer(
        share,
        frames,
        span_mask,
        cotangent,
        qkv_weight,
        out_weight,
        up_weight,
        down_weight.T,
        head_biases,
        norm_vectors,
    )
    down = (down_weight.T, down_mean.T, down_square.T)
    state = (qkv_weight, qkv_mean, qkv_square, out_weight, out_mean, out_square)
    state += (up_weight, up_mean, up_square, *down, head_biases, bias_mean, bias_square)
    state += (norm_vectors, vector_mean, vector_square)
    grad_norm, outputs, frame_grad, *updated = run_update(sums, norm, vec_tiles, act, fg, state)
    updated[9:12] = [value.T for value in updated[9:12]]
    return (outputs, frame_grad, grad_norm.reshape(()), *updated)


def solution(mesh):
    return jax.shard_map(
        on_device_fast if fast_fits(mesh) else on_device,
        mesh=mesh,
        in_specs=(
            P(("dp", "mp"), None),
            P("dp", None),
            P(("dp", "mp"), None),
            P("dp", "mp"),
            P("dp", "mp"),
            P("dp", "mp"),
            P("mp", "dp"),
            P("mp", "dp"),
            P("mp", "dp"),
            P("dp", "mp"),
            P("dp", "mp"),
            P("dp", "mp"),
            P("mp", "dp"),
            P("mp", "dp"),
            P("mp", "dp"),
            P("mp", "dp"),
            P("mp", "dp"),
            P("mp", "dp"),
            P(None, "dp"),
            P(None, "dp"),
            P(None, "dp"),
        ),
        out_specs=(
            P(("dp", "mp"), None),
            P(("dp", "mp"), None),
            P(),
            P("dp", "mp"),
            P("dp", "mp"),
            P("dp", "mp"),
            P("mp", "dp"),
            P("mp", "dp"),
            P("mp", "dp"),
            P("dp", "mp"),
            P("dp", "mp"),
            P("dp", "mp"),
            P("mp", "dp"),
            P("mp", "dp"),
            P("mp", "dp"),
            P("mp", "dp"),
            P("mp", "dp"),
            P("mp", "dp"),
            P(None, "dp"),
            P(None, "dp"),
            P(None, "dp"),
        ),
        check_vma=False,
    )
```

```python
import functools

import jax
import jax.numpy as jnp
from jax import lax
from jax.experimental import pallas as pl
from jax.experimental.pallas import tpu as pltpu
from jax.sharding import PartitionSpec as P

HD = 64
LEN = 688


norm_eps = 1e-05
adam_eps = 1e-08
beta_one = 0.9
beta_two = 0.999
step_count = 10.0
clip_limit = 1.0
settings = ((0.05, 0.1), (0.3, 0.1), (0.05, 0.1), (0.03, 0.1), (0.3, 0.0), (0.4, 0.0))


def norm_rows(values, norm_gain, norm_shift):
    centred = values - jnp.mean(values, axis=-1, keepdims=True)
    variance = jnp.mean(centred * centred, axis=-1, keepdims=True)
    inverse = lax.rsqrt(variance + norm_eps)
    normed = centred * inverse
    return (normed * norm_gain + norm_shift, normed, inverse)


def norm_back(upstream, normed, inverse, norm_gain):
    scaled = upstream * norm_gain
    inner_part = (
        scaled
        - jnp.mean(scaled, axis=-1, keepdims=True)
        - normed * jnp.mean(scaled * normed, axis=-1, keepdims=True)
    )
    return (inverse * inner_part, jnp.sum(upstream * normed, axis=0), jnp.sum(upstream, axis=0))


def gelu_slope(pre_act):
    cumulative = 0.5 * (1.0 + jax.scipy.special.erf(pre_act * 0.7071067811865476))
    return cumulative + pre_act * jnp.exp(-0.5 * pre_act * pre_act) * 0.3989422804014327


def attend_forward(clip_block):
    scaling = HD ** (-0.5)
    queries = clip_block[:, :, 0]
    key_rows = clip_block[:, :, 1]
    value_rows = clip_block[:, :, 2]
    scores = (
        jnp.einsum("qhe,khe->hqk", queries, key_rows, preferred_element_type=jnp.float32) * scaling
    )
    row_peak = jnp.max(scores, axis=-1, keepdims=True)
    log_total = row_peak + jnp.log(jnp.sum(jnp.exp(scores - row_peak), axis=-1, keepdims=True))
    attention = jnp.exp(scores - log_total).astype(jnp.bfloat16)
    mixed_rows = jnp.einsum(
        "hqk,khe->qhe", attention, value_rows, preferred_element_type=jnp.float32
    )
    return (mixed_rows.astype(jnp.bfloat16).reshape(clip_block.shape[0], -1), log_total)


def attend_backward(pieces):
    clip_block, log_total, grad_mixed = pieces
    scaling = HD ** (-0.5)
    queries = clip_block[:, :, 0]
    key_rows = clip_block[:, :, 1]
    value_rows = clip_block[:, :, 2]
    scores = (
        jnp.einsum("qhe,khe->hqk", queries, key_rows, preferred_element_type=jnp.float32) * scaling
    )
    attention = jnp.exp(scores - log_total)
    attention_low = attention.astype(jnp.bfloat16)
    mixed_rows = jnp.einsum(
        "hqk,khe->qhe", attention_low, value_rows, preferred_element_type=jnp.float32
    ).astype(jnp.bfloat16)
    grad_rows = grad_mixed.reshape(queries.shape)
    grad_attention = jnp.einsum(
        "qhe,khe->hqk", grad_rows, value_rows, preferred_element_type=jnp.float32
    )
    grad_values = jnp.einsum(
        "hqk,qhe->khe", attention_low, grad_rows, preferred_element_type=jnp.float32
    )
    row_inner = jnp.sum(attention * grad_attention, axis=-1, keepdims=True)
    grad_scores = (attention * (grad_attention - row_inner)).astype(jnp.bfloat16)
    grad_queries = (
        jnp.einsum("hqk,khe->qhe", grad_scores, key_rows, preferred_element_type=jnp.float32)
        * scaling
    )
    grad_keys = (
        jnp.einsum("hqk,qhe->khe", grad_scores, queries, preferred_element_type=jnp.float32)
        * scaling
    )
    grad_block = jnp.stack([grad_queries, grad_keys, grad_values], axis=2).astype(jnp.bfloat16)
    return (
        mixed_rows.reshape(clip_block.shape[0], -1),
        grad_block.reshape(clip_block.shape[0], -1),
    )


def adam_step(weight, mean_old, square_old, gradient, factor, rate, decay):
    clipped = gradient * factor
    mean_new = beta_one * mean_old + (1.0 - beta_one) * clipped
    square_new = beta_two * square_old + (1.0 - beta_two) * clipped * clipped
    mean_hat = mean_new / (1.0 - beta_one**step_count)
    square_hat = square_new / (1.0 - beta_two**step_count)
    weight_new = weight - rate * (mean_hat / (jnp.sqrt(square_hat) + adam_eps) + decay * weight)
    return (weight_new, mean_new, square_new)


def on_device(
    frames,
    span_mask,
    cotangent,
    qkv_weight,
    qkv_mean,
    qkv_square,
    out_weight,
    out_mean,
    out_square,
    up_weight,
    up_mean,
    up_square,
    down_weight,
    down_mean,
    down_square,
    head_biases,
    bias_mean,
    bias_square,
    norm_vectors,
    vector_mean,
    vector_square,
):
    masters = (qkv_weight, out_weight, up_weight, down_weight, head_biases, norm_vectors)
    lowered = tuple((weight.astype(jnp.bfloat16) for weight in masters))
    qkv_full, out_full, up_full, down_full, bias_full, vector_full = (
        lax.all_gather(lowered[0], "dp", axis=0, tiled=True),
        lax.all_gather(lowered[1], "dp", axis=1, tiled=True),
        lax.all_gather(lowered[2], "dp", axis=0, tiled=True),
        lax.all_gather(lowered[3], "dp", axis=1, tiled=True),
        lax.all_gather(lowered[4], "dp", axis=1, tiled=True),
        lax.all_gather(lowered[5], "dp", axis=1, tiled=True),
    )
    share_rows = frames.shape[0]
    start_row = lax.axis_index("mp") * share_rows
    vectors = vector_full.astype(jnp.float32)
    local_heads = bias_full.shape[0]

    def share_of(array_full):
        return lax.dynamic_slice_in_dim(array_full, start_row, share_rows, 0)

    gathered = lax.all_gather(frames, "mp", axis=0, tiled=True)
    all_rows = gathered.shape[0]
    masked = span_mask.reshape(all_rows, 1) == 1
    inputs = jnp.where(masked, vectors[0], gathered.astype(jnp.float32))
    rounded = inputs.astype(jnp.bfloat16)
    zero_bias = jnp.zeros_like(bias_full[:, :HD])
    qkv_bias = (
        jnp.stack([bias_full[:, :HD], zero_bias, bias_full[:, HD : 2 * HD]], axis=1)
        .reshape(-1)
        .astype(jnp.float32)
    )
    up_bias = bias_full[:, 2 * HD :].reshape(-1).astype(jnp.float32)
    projected = (jnp.dot(rounded, qkv_full, preferred_element_type=jnp.float32) + qkv_bias).astype(
        jnp.bfloat16
    )
    blocks = projected.reshape(-1, LEN, local_heads, 3, HD)
    mixed_rows, log_total = lax.map(attend_forward, blocks)
    mixed_rows = mixed_rows.reshape(all_rows, -1)
    attn_part = jnp.dot(mixed_rows, out_full, preferred_element_type=jnp.float32)
    attended = lax.psum(attn_part, "mp")
    first_sum = inputs + attended + vectors[5]
    hidden, normed_full, inverse_full = norm_rows(first_sum, vectors[1], vectors[2])
    normed_one = share_of(normed_full)
    inverse_one = share_of(inverse_full)
    hidden_low = hidden.astype(jnp.bfloat16)
    pre_act = jnp.dot(hidden_low, up_full, preferred_element_type=jnp.float32) + up_bias
    activated = jax.nn.gelu(pre_act, approximate=False).astype(jnp.bfloat16)
    ffn_part = jnp.dot(activated, down_full, preferred_element_type=jnp.float32)
    second_sum = hidden + lax.psum(ffn_part, "mp") + vectors[6]
    outputs_full, normed_full, inverse_full = norm_rows(second_sum, vectors[3], vectors[4])
    outputs = share_of(outputs_full)
    normed_two = share_of(normed_full)
    inverse_two = share_of(inverse_full)
    qkv_full, out_full, up_full, down_full, bias_full, vector_full = (
        lax.all_gather(lowered[0], "dp", axis=0, tiled=True),
        lax.all_gather(lowered[1], "dp", axis=1, tiled=True),
        lax.all_gather(lowered[2], "dp", axis=0, tiled=True),
        lax.all_gather(lowered[3], "dp", axis=1, tiled=True),
        lax.all_gather(lowered[4], "dp", axis=1, tiled=True),
        lax.all_gather(lowered[5], "dp", axis=1, tiled=True),
    )
    upstream = cotangent.astype(jnp.float32)
    grad_two, grad_gain_two, grad_shift_two = norm_back(
        upstream, normed_two, inverse_two, vectors[3]
    )
    grad_down_bias = jnp.sum(grad_two, axis=0)
    grad_two_full = lax.all_gather(grad_two.astype(jnp.bfloat16), "mp", axis=0, tiled=True)
    pre_again = jnp.dot(hidden_low, up_full, preferred_element_type=jnp.float32) + up_bias
    act_again = jax.nn.gelu(pre_again, approximate=False).astype(jnp.bfloat16)
    grad_down = jnp.einsum(
        "tf,td->fd", act_again, grad_two_full, preferred_element_type=jnp.float32
    )
    grad_act = jnp.einsum("td,fd->tf", grad_two_full, down_full, preferred_element_type=jnp.float32)
    grad_pre = (grad_act * gelu_slope(pre_again)).astype(jnp.bfloat16)
    grad_up = jnp.einsum("td,tf->df", hidden_low, grad_pre, preferred_element_type=jnp.float32)
    grad_up_bias = jnp.sum(grad_pre, axis=0, dtype=jnp.float32)
    hidden_part = jnp.einsum("tf,df->td", grad_pre, up_full, preferred_element_type=jnp.float32)
    grad_hidden = grad_two + lax.psum_scatter(hidden_part, "mp", scatter_dimension=0, tiled=True)
    grad_one, grad_gain_one, grad_shift_one = norm_back(
        grad_hidden, normed_one, inverse_one, vectors[1]
    )
    grad_out_bias = jnp.sum(grad_one, axis=0)
    grad_one_full = lax.all_gather(grad_one.astype(jnp.bfloat16), "mp", axis=0, tiled=True)
    grad_mixed = jnp.einsum(
        "td,cd->tc", grad_one_full, out_full, preferred_element_type=jnp.float32
    ).astype(jnp.bfloat16)
    mixed_again, grad_blocks = lax.map(
        attend_backward, (blocks, log_total, grad_mixed.reshape(-1, LEN, grad_mixed.shape[1]))
    )
    mixed_again = mixed_again.reshape(all_rows, -1)
    grad_blocks = grad_blocks.reshape(all_rows, -1)
    grad_out = jnp.einsum(
        "tc,td->cd", mixed_again, grad_one_full, preferred_element_type=jnp.float32
    )
    grad_qkv = jnp.einsum("td,tc->dc", rounded, grad_blocks, preferred_element_type=jnp.float32)
    bias_sums = jnp.sum(grad_blocks, axis=0, dtype=jnp.float32).reshape(local_heads, 3, HD)
    grad_biases = jnp.concatenate(
        [bias_sums[:, 0], bias_sums[:, 2], grad_up_bias.reshape(local_heads, -1)], axis=1
    )
    input_part = jnp.einsum("tc,dc->td", grad_blocks, qkv_full, preferred_element_type=jnp.float32)
    grad_inputs = grad_one + lax.psum_scatter(
        input_part.astype(jnp.bfloat16), "mp", scatter_dimension=0, tiled=True
    ).astype(jnp.float32)
    masked_share = share_of(masked)
    grad_embed = jnp.sum(jnp.where(masked_share, grad_inputs, 0.0), axis=0)
    frame_grad = jnp.where(masked_share, 0.0, grad_inputs)
    grad_vectors = jnp.stack(
        [
            grad_embed,
            grad_gain_one,
            grad_shift_one,
            grad_gain_two,
            grad_shift_two,
            grad_out_bias,
            grad_down_bias,
        ]
    )
    reduced = (
        lax.psum_scatter(grad_qkv, "dp", scatter_dimension=0, tiled=True),
        lax.psum_scatter(grad_out, "dp", scatter_dimension=1, tiled=True),
        lax.psum_scatter(grad_up, "dp", scatter_dimension=0, tiled=True),
        lax.psum_scatter(grad_down, "dp", scatter_dimension=1, tiled=True),
        lax.psum_scatter(grad_biases, "dp", scatter_dimension=1, tiled=True),
    )
    local_squares = jnp.float32(0.0)
    for portion in reduced:
        local_squares = local_squares + jnp.sum(portion * portion)
    total_squares, vector_total = lax.psum((local_squares, grad_vectors), ("dp", "mp"))
    grad_norm = jnp.sqrt(total_squares + jnp.sum(vector_total * vector_total))
    column_count = norm_vectors.shape[1]
    vector_grad = lax.dynamic_slice_in_dim(
        vector_total, lax.axis_index("dp") * column_count, column_count, 1
    )
    factor = jnp.minimum(1.0, clip_limit / (grad_norm + 1e-06))
    gradients = (reduced[0], reduced[1], reduced[2], reduced[3], reduced[4], vector_grad)
    means = (qkv_mean, out_mean, up_mean, down_mean, bias_mean, vector_mean)
    squares = (qkv_square, out_square, up_square, down_square, bias_square, vector_square)
    updated = []
    for index_at in range(6):
        updated.extend(
            adam_step(
                masters[index_at],
                means[index_at],
                squares[index_at],
                gradients[index_at],
                factor,
                settings[index_at][0],
                settings[index_at][1],
            )
        )
    return (
        outputs,
        frame_grad,
        grad_norm,
        updated[0],
        updated[1],
        updated[2],
        updated[3],
        updated[4],
        updated[5],
        updated[6],
        updated[7],
        updated[8],
        updated[9],
        updated[10],
        updated[11],
        updated[12],
        updated[13],
        updated[14],
        updated[15],
        updated[16],
        updated[17],
    )


MESH = pl.DeviceIdType.MESH
SMALL, MIX, UP, DOWN = range(4)
SEMS = 24
f32, bf16 = jnp.float32, jnp.bfloat16


def fast_fits(mesh):
    return mesh.shape["dp"] == 8 and mesh.shape["mp"] == 4


def flip(dp, bit):
    held = lax.rem(lax.div(dp, bit), 2)
    return dp + bit - 2 * bit * held


def dg(a, b, ca, cb):
    return lax.dot_general(a, b, (((ca,), (cb,)), ((), ())), preferred_element_type=f32)


def landed(dst, sem):
    pltpu.make_async_copy(dst, dst, sem).wait()


def layer_kernel(
    share,
    frames_in,
    mask_in,
    cot_in,
    qkv_in,
    out_in,
    up_in,
    down_in,
    bias_in,
    vec_in,
    act_out,
    fg_out,
    small_sum,
    mix_sum,
    up_sum,
    down_sum,
    norm_ref,
    vec_tiles,
    ws,
    wm,
    wu,
    wd,
    gs,
    rcs,
    rcm,
    rcu,
    rcd,
    rds,
    rdm,
    rdu,
    rdd,
    rxs,
    rxm,
    rxu,
    rxd,
    rys,
    rym,
    ryu,
    ryd,
    rzs,
    rzm,
    rzu,
    rzd,
    fm_own,
    cot_own,
    fmx,
    cotx,
    x_low,
    q_all,
    kv_own,
    kv_far,
    mixed,
    lse,
    mix_t,
    n_one,
    r_one,
    hid_low,
    act,
    slope,
    acc,
    low,
    dm,
    dproj,
    stage_act,
    stage_fg,
    fg_far,
    vec,
    bias,
    gvec,
    gbias,
    tiles,
    gather_s,
    gather_r,
    reduce_s,
    reduce_r,
    kv_s,
    kv_r,
    move_s,
    move_r,
    tile_s,
    tile_r,
):
    T = share
    dp, mp = lax.axis_index("dp"), lax.axis_index("mp")
    core = lax.rem(dp, 2)
    dx, dy, dc = flip(dp, 2), flip(dp, 4), flip(dp, 1)
    dd = flip(dx, 4)
    planes = (mp, flip(mp, 1), flip(mp, 2), flip(flip(mp, 1), 2))
    mover = lax.rem(core + mp, 2) == 1
    stay = lax.rem(core + mp, 2) == 0
    swap_with = (dc, planes[1])
    full = (ws, wm, wu, wd)
    local = (gs, wm, wu, wd)
    from_core = (rcs, rcm, rcu, rcd)
    from_diag = (rds, rdm, rdu, rdd)
    from_x = (rxs, rxm, rxu, rxd)
    from_y = (rys, rym, ryu, ryd)
    from_z = (rzs, rzm, rzu, rzd)
    result = (small_sum, mix_sum, up_sum, down_sum)
    heads = q_all.shape[1]
    chunks = [(r, min(88, T - r)) for r in range(0, T, 88)]

    def remote(src, dst, send_sem, recv_sem, device):
        return pltpu.make_async_remote_copy(
            src_ref=src,
            dst_ref=dst,
            send_sem=send_sem,
            recv_sem=recv_sem,
            device_id=device,
            device_id_type=MESH,
        )

    pending = {}

    def send(tag, src, dst, sems, at, device):
        copy = remote(src, dst, sems[0].at[at], sems[1].at[at], device)
        copy.start()
        pending.setdefault(tag, []).append(copy)

    def sent(tag):
        for copy in pending.pop(tag, []):
            copy.wait_send()

    def hand_over(slot, src, dst):
        @pl.when(mover)
        def _():
            remote(src, dst, move_s.at[slot], move_r.at[slot], swap_with).start()

        @pl.when(stay)
        def _():
            pltpu.make_async_copy(src, dst, move_r.at[slot]).start()

    def halves(ref):
        n = ref.shape[-2] // 2
        return ref.at[pl.ds(0, n)], ref.at[pl.ds(n, n)]

    gather = (gather_s, gather_r)

    def slot(w, k, d):
        return full[w].at[planes[k], lax.div(d, 2), lax.rem(d, 2)]

    def ag_own(w):
        for k in (1, 2, 3):
            send(("ag", w), slot(w, 0, dp), slot(w, 0, dp), gather, (w, k), (dp, planes[k]))

    def ag_a(w, k):
        ref = slot(w, k, dp)
        if k:
            landed(ref, gather_r.at[w, k])
        send(("ag", w), ref, ref, gather, (w, 4 + k), (dx, mp))
        send(("ag", w), ref, ref, gather, (w, 8 + k), (dy, mp))

    def ag_b(w, k):
        at_x, at_y = slot(w, k, dx), slot(w, k, dy)
        landed(at_x, gather_r.at[w, 4 + k])
        if w == SMALL or k == 2:
            send(("ag", w), at_x, at_x, gather, (w, 12 + k), (dy, mp))
        elif k == 0:
            ref = halves(at_x)[0]
            send(("ag", w), ref, ref, gather, (w, 12), (dy, mp))
        landed(at_y, gather_r.at[w, 8 + k])
        if w == SMALL:
            return
        if k == 0:
            ref = halves(at_y)[1]
            send(("ag", w), ref, ref, gather, (w, 13), (dx, mp))
        if k == 3:
            send(("ag", w), at_y, at_y, gather, (w, 15), (dx, mp))

    def ag_c(w, k):
        ref = slot(w, k, dd)
        if w == SMALL or k > 1:
            landed(ref, gather_r.at[w, 12 + k])
        elif k == 0:
            for i, half in enumerate(halves(ref)):
                landed(half, gather_r.at[w, 12 + i])
            send(("ag", w), ref, ref, gather, (w, 16), (dp, planes[1]))
        else:
            landed(ref, gather_r.at[w, 16])
        ref = full[w].at[planes[k], :, core]
        send(("ag", w), ref, ref, gather, (w, 17 + k), (dc, mp))

    def ag_d(w, k):
        landed(full[w].at[planes[k], :, 1 - core], gather_r.at[w, 17 + k])

    squares = []
    reduce = (reduce_s, reduce_r)

    def part(w, k, d):
        return local[w].at[planes[k], lax.div(d, 2), lax.rem(d, 2)]

    def add_to(ref, arrived):
        ref[...] = ref[...] + arrived[...]

    def rs_0(w, k):
        send("rs", local[w].at[planes[k], :, 1 - core], from_core[w].at[k], reduce, (w, k), (dc, mp))

    def rs_1(w, k):
        landed(from_core[w].at[k], reduce_r.at[w, k])
        add_to(local[w].at[planes[k], :, core], from_core[w].at[k])
        at_d, at_x, at_y = part(w, k, dd), part(w, k, dx), part(w, k, dy)
        to_d, to_x, to_y = from_diag[w].at[k], from_x[w].at[k], from_y[w].at[k]
        if w == SMALL or k > 1:
            if k % 2:
                send("rs", at_d, to_d, reduce, (w, 4 + k), (dx, mp))
                send("rs", at_x, to_x, reduce, (w, 10 + k), (dx, mp))
            else:
                send("rs", at_d, to_d, reduce, (w, 4 + k), (dy, mp))
                send("rs", at_y, to_y, reduce, (w, 15 + k), (dy, mp))
        elif k == 1:
            send("rs", at_d, to_d, reduce, (w, 4), (dp, planes[1]))
            send("rs", at_x, to_x, reduce, (w, 10 + k), (dx, mp))
            send("rs", at_y, to_y, reduce, (w, 15 + k), (dy, mp))
        else:
            landed(from_diag[w].at[1], reduce_r.at[w, 4])
            add_to(at_d, from_diag[w].at[1])
            send("rs", halves(at_d)[0], halves(to_d)[0], reduce, (w, 8), (dx, mp))
            send("rs", halves(at_d)[1], halves(to_d)[1], reduce, (w, 9), (dy, mp))
            send("rs", halves(at_x)[0], halves(to_x)[0], reduce, (w, 10), (dx, mp))
            send("rs", halves(at_y)[1], halves(to_y)[1], reduce, (w, 15), (dy, mp))

    def rs_2(w, k):
        at_x, at_y = part(w, k, dx), part(w, k, dy)
        come, to_x, to_y = from_diag[w].at[k], from_x[w].at[k], from_y[w].at[k]
        if w == SMALL or k > 1:
            landed(come, reduce_r.at[w, 4 + k])
            if k % 2:
                add_to(at_y, come)
                send("rs", at_y, to_y, reduce, (w, 15 + k), (dy, mp))
            else:
                add_to(at_x, come)
                send("rs", at_x, to_x, reduce, (w, 10 + k), (dx, mp))
        else:
            first, second = halves(come)
            landed(first, reduce_r.at[w, 8])
            add_to(halves(at_y)[0], first)
            send("rs", halves(at_y)[0], halves(to_y)[0], reduce, (w, 19), (dy, mp))
            landed(second, reduce_r.at[w, 9])
            add_to(halves(at_x)[1], second)
            send("rs", halves(at_x)[1], halves(to_x)[1], reduce, (w, 14), (dx, mp))

    def rs_3(w, k):
        if w == SMALL or k:
            landed(from_x[w].at[k], reduce_r.at[w, 10 + k])
            landed(from_y[w].at[k], reduce_r.at[w, 15 + k])
        else:
            for half, at in zip(halves(from_x[w].at[0]), (10, 14)):
                landed(half, reduce_r.at[w, at])
            for half, at in zip(halves(from_y[w].at[0]), (19, 15)):
                landed(half, reduce_r.at[w, at])
        ref = part(w, k, dp)
        total = ref[...].astype(f32) + from_x[w][k].astype(f32) + from_y[w][k].astype(f32)
        if k:
            ref[...] = total.astype(ref.dtype)
            send("rs", ref, from_z[w].at[k - 1], reduce, (w, 19 + k), (dp, planes[k]))
        else:
            result[w][...] = total

    def rs_4(w):
        total = result[w][...]
        for k in (1, 2, 3):
            landed(from_z[w].at[k - 1], reduce_r.at[w, 19 + k])
            total = total + from_z[w][k - 1].astype(f32)
        result[w][...] = total
        squares.append(jnp.sum(total * total))

    own_j = lax.div(dp, 2)
    cut, vec_cut = bias_in.shape[1], vec_in.shape[1]
    width, wide = frames_in.shape[1], up_in.shape[1]
    qkv_wide = 192 * heads + 64
    out_first = 192 * heads - 64
    lane = lax.broadcasted_iota(jnp.int32, (1, 128), 1)
    cells = [(j, c) for j in range(4) for c in range(2)]
    group = [dc, dx, dy, dd, flip(dx, 1), flip(dy, 1), flip(dd, 1)]
    others = [(d, mp) for d in group] + [(dp, planes[k]) for k in (1, 2, 3)] + [swap_with]
    bar = pltpu.get_barrier_semaphore()
    for device in others:
        pl.semaphore_signal(bar, inc=1, device_id=device, device_id_type=MESH)
    ws[mp, own_j, core] = jnp.zeros(ws.shape[3:], f32)
    ws[mp, own_j, core, 0:heads, 0:cut] = bias_in[...].astype(bf16).astype(f32)
    ws[mp, own_j, core, 8:15, 0:vec_cut] = vec_in[...].astype(bf16).astype(f32)

    def prep_mix():
        wm[mp, own_j, core] = jnp.concatenate([qkv_in[...], out_in[...].T], axis=1).astype(bf16)

    def prep_up():
        wu[mp, own_j, core] = up_in[...].astype(bf16)

    def prep_down():
        wd[mp, own_j, core] = down_in[...].astype(bf16)

    def prep_flags():
        flags = mask_in[...].astype(f32)
        flags = jnp.where(lax.rem(mp, 2) == 0, flags[:, 0:T], flags[:, T : 2 * T])
        flags = jnp.where(lax.div(mp, 2) == 0, flags[0:1, :], flags[1:2, :])
        fm_own[0:T, 0:width] = frames_in[...]
        fm_own[0:T, width:] = jnp.broadcast_to(flags, (128, T)).T.astype(bf16)

    def move_frames():
        hand_over(0, fm_own, fmx)

    def move_cot():
        cot_own[0:T, :] = cot_in[...]
        hand_over(1, cot_own, cotx)

    def unpack():
        for k in range(4):
            ag_d(SMALL, k)
        vec[...] = jnp.concatenate([ws[0, j, c, 8:16, 0:vec_cut] for j, c in cells], axis=1)
        for z in range(4):
            bias[z] = jnp.concatenate([ws[z, j, c, 0:8, 0:cut] for j, c in cells], axis=1)

    def vector(i):
        return vec[i : i + 1, :]

    embed, gain_one, shift_one, gain_two, shift_two, out_add, down_add = (
        functools.partial(vector, i) for i in range(7)
    )

    def masked_rows(r, n):
        flag = fmx[r : r + n, width:].astype(f32)
        return jnp.concatenate([flag] * (width // 128), axis=1) > 0.5

    def input_rows(r, n):
        return jnp.where(masked_rows(r, n), embed(), fmx[r : r + n, 0:width].astype(f32))

    def round_inputs():
        landed(fmx, move_r.at[0])
        for r, n in chunks:
            x_low[r : r + n, :] = input_rows(r, n).astype(bf16)

    def weight(ref, z, first, last):
        return ref[z, :, :, :, first:last].reshape(width, last - first)

    def add_up(piece, first):
        acc[...] = piece if first else acc[...] + piece

    def project(k):
        z = planes[k]
        ag_d(MIX, k)
        slab = jnp.dot(x_low[...], weight(wm, z, 0, qkv_wide), preferred_element_type=f32)
        for h in range(heads):
            both = bias[z, h : h + 1, 0:128]
            head = slab[:, 192 * h : 192 * h + 128] + both
            head = head.astype(bf16).astype(f32) * HD ** (-0.5)
            q_all[z, h] = jnp.where(lane < HD, head, 0.0).astype(bf16)
            pair = slab[:, 192 * h + 64 : 192 * h + 192] + jnp.where(lane < HD, 0.0, both)
            kv_own[z, h, 0:T, :] = pair.astype(bf16)
        send("kv", kv_own.at[z], kv_far.at[z], (kv_s, kv_r), (k,), (dc, mp))

    def stand(value):
        flat = value.reshape(heads * HD, T)
        return jnp.concatenate([jnp.zeros((HD, T), f32), flat], axis=0).T.astype(bf16)

    def attend(k):
        z = planes[k]
        landed(kv_far.at[z], kv_r.at[k])

        @pl.loop(0, heads)
        def _(h):
            queries = q_all[z, h]
            own, far = kv_own[z, h, 0:T, :], kv_far[z, h, 0:T, :]
            s_own, s_far = dg(own, queries, 1, 1), dg(far, queries, 1, 1)
            peak = jnp.maximum(
                jnp.max(s_own, axis=0, keepdims=True), jnp.max(s_far, axis=0, keepdims=True)
            )
            e_own, e_far = jnp.exp(s_own - peak), jnp.exp(s_far - peak)
            total = jnp.sum(e_own, axis=0, keepdims=True) + jnp.sum(e_far, axis=0, keepdims=True)
            lse[z, h] = peak + jnp.log(total)
            scale = 1.0 / total
            mix = dg(own, (e_own * scale).astype(bf16), 0, 0)
            mix = mix + dg(far, (e_far * scale).astype(bf16), 0, 0)
            mix_t[h] = mix[HD:, :]

        mixed[z] = stand(mix_t[...])

    def norm_one():
        for k in range(4):
            add_up(dg(mixed[planes[k]], weight(wm, planes[k], out_first, width), 1, 1), k == 0)
        for r, n in chunks:
            v = input_rows(r, n) + acc[r : r + n, :] + out_add()
            v = v - jnp.mean(v, axis=-1, keepdims=True)
            inverse = lax.rsqrt(jnp.mean(v * v, axis=-1, keepdims=True) + norm_eps)
            normed = v * inverse
            n_one[r : r + n, :] = normed
            r_one[r : r + n, :] = inverse
            hid_low[r : r + n, :] = (normed * gain_one() + shift_one()).astype(bf16)

    def rise(k):
        z = planes[k]
        ag_d(UP, k)
        for h in range(heads):
            cols = slice(256 * h, 256 * h + 256)
            u = jnp.dot(
                hid_low[...], weight(wu, z, 256 * h, 256 * h + 256), preferred_element_type=f32
            )
            u = u + bias[z, h : h + 1, 128:384]
            cumulative = 0.5 * (1.0 + lax.erf(u * 0.7071067811865476))
            act[z, 0:T, cols] = (u * cumulative).astype(bf16)
            bell = jnp.exp(-0.5 * u * u) * 0.3989422804014327
            slope[z, 0:T, cols] = (cumulative + u * bell).astype(bf16)

    def drop(k):
        ag_d(DOWN, k)
        add_up(dg(act[planes[k], 0:T, :], weight(wd, planes[k], 0, wide), 1, 1), k == 0)

    def norm_two():
        landed(cotx, move_r.at[1])
        sums = [jnp.zeros((1, width), f32) for _ in range(3)]
        for r, n in chunks:
            v = n_one[r : r + n, :] * gain_one() + shift_one() + acc[r : r + n, :] + down_add()
            v = v - jnp.mean(v, axis=-1, keepdims=True)
            inverse = lax.rsqrt(jnp.mean(v * v, axis=-1, keepdims=True) + norm_eps)
            normed = v * inverse
            stage_act[r : r + n, :] = normed * gain_two() + shift_two()
            up = cotx[r : r + n, :].astype(f32)
            scaled = up * gain_two()
            inner = jnp.mean(scaled * normed, axis=-1, keepdims=True)
            grad = inverse * (scaled - jnp.mean(scaled, axis=-1, keepdims=True) - normed * inner)
            acc[r : r + n, :] = grad
            low[r : r + n, :] = grad.astype(bf16)
            for i, term in enumerate((up * normed, up, grad)):
                sums[i] = sums[i] + jnp.sum(term, axis=0, keepdims=True)
        gvec[...] = jnp.zeros(gvec.shape, f32)
        gbias[...] = jnp.zeros(gbias.shape, f32)
        gvec[3:4, :], gvec[4:5, :], gvec[6:7, :] = sums

    pl.semaphore_wait(bar, len(others))
    for step, *given in (
        (prep_mix,),
        (ag_a, MIX, 0),
        (ag_own, SMALL),
        (ag_own, MIX),
        (prep_flags,),
        (prep_up,),
        (prep_down,),
        (ag_a, DOWN, 0),
        (ag_b, MIX, 0),
        (ag_a, MIX, 1),
        (ag_a, SMALL, 1),
        (ag_a, SMALL, 2),
        (ag_a, UP, 0),
        (ag_c, MIX, 0),
        (ag_own, UP),
        (ag_b, SMALL, 2),
        (ag_b, MIX, 1),
        (ag_b, SMALL, 1),
        (ag_a, MIX, 2),
        (ag_a, SMALL, 0),
        (move_frames,),
        (ag_b, UP, 0),
        (ag_a, SMALL, 3),
        (ag_b, DOWN, 0),
        (ag_b, SMALL, 0),
        (ag_b, SMALL, 3),
        (ag_a, MIX, 3),
        (ag_own, DOWN),
        (ag_b, MIX, 2),
        (ag_c, UP, 0),
        (ag_a, UP, 2),
        (ag_b, MIX, 3),
        (ag_c, DOWN, 0),
        (ag_a, UP, 3),
        (ag_c, MIX, 1),
        (ag_a, UP, 1),
        (ag_c, SMALL, 1),
        (ag_c, SMALL, 0),
        (ag_c, SMALL, 3),
        (ag_c, SMALL, 2),
        (ag_c, MIX, 3),
        (ag_c, MIX, 2),
        (ag_b, UP, 2),
        (unpack,),
        (ag_b, UP, 3),
        (round_inputs,),
        (project, 0),
        (project, 1),
        (move_cot,),
        (ag_a, DOWN, 1),
        (project, 2),
        (project, 3),
        (attend, 0),
        (attend, 1),
        (ag_a, DOWN, 2),
        (ag_b, UP, 1),
        (attend, 2),
        (ag_c, UP, 3),
        (ag_a, DOWN, 3),
        (ag_b, DOWN, 1),
        (attend, 3),
        (ag_c, UP, 2),
        (ag_c, UP, 1),
        (ag_b, DOWN, 2),
        (norm_one,),
        (ag_b, DOWN, 3),
        (rise, 0),
        (rise, 1),
        (ag_c, DOWN, 1),
        (rise, 2),
        (ag_c, DOWN, 2),
        (rise, 3),
        (ag_c, DOWN, 3),
        (drop, 0),
        (drop, 1),
        (drop, 2),
        (drop, 3),
        (norm_two,),
    ):
        step(*given)
    for w in range(4):
        sent(("ag", w))

    def tiled(value):
        return value.reshape(4, 2, -1, value.shape[1])

    def move_act():
        hand_over(2, stage_act, act_out)

    def fall(k):
        z = planes[k]
        grad = dg(low[...], weight(wd, z, 0, wide), 1, 0)
        grad = (grad * slope[z, 0:T, :].astype(f32)).astype(bf16)
        slope[z, 0:T, :] = grad
        total = jnp.sum(grad.astype(f32), axis=0, keepdims=True)
        for h in range(heads):
            gbias[z, h : h + 1, 128:384] = total[:, 256 * h : 256 * h + 256]
        wd[z] = tiled(dg(low[...], act[z, 0:T, :], 0, 0).astype(bf16))
        rs_0(DOWN, k)

    def sink(k):
        z = planes[k]
        acc[...] = acc[...] + dg(slope[z, 0:T, :], weight(wu, z, 0, wide), 1, 1)
        wu[z] = tiled(dg(hid_low[...], slope[z, 0:T, :], 0, 0).astype(bf16))
        rs_0(UP, k)

    def norm_back_one():
        sums = [jnp.zeros((1, width), f32) for _ in range(3)]
        for r, n in chunks:
            grad_in = acc[r : r + n, :]
            normed = n_one[r : r + n, :]
            scaled = grad_in * gain_one()
            inner = jnp.mean(scaled * normed, axis=-1, keepdims=True)
            grad = r_one[r : r + n, :] * (
                scaled - jnp.mean(scaled, axis=-1, keepdims=True) - normed * inner
            )
            acc[r : r + n, :] = grad
            low[r : r + n, :] = grad.astype(bf16)
            for i, term in enumerate((grad_in * normed, grad_in, grad)):
                sums[i] = sums[i] + jnp.sum(term, axis=0, keepdims=True)
        gvec[1:2, :], gvec[2:3, :], gvec[5:6, :] = sums

    def unmix():
        for z in planes:
            grad = dg(low[...], weight(wm, z, out_first, width), 1, 0).astype(bf16).astype(f32)
            for h in range(heads):
                if h % 2 == 0:
                    head = grad[:, HD * h : HD * h + 128]
                else:
                    piece = grad[:, HD * h + HD : HD * h + 2 * HD]
                    head = jnp.concatenate([piece, piece], axis=1)
                dm[z, h] = jnp.where(lane < HD, 0.0, head).astype(bf16)

    def attend_back(k):
        z = planes[k]

        @pl.loop(0, heads)
        def _(h):
            queries, gm = q_all[z, h], dm[z, h]
            own, far = kv_own[z, h, 0:T, :], kv_far[z, h, 0:T, :]
            level = lse[z, h]
            p_own = jnp.exp(dg(own, queries, 1, 1) - level)
            p_far = jnp.exp(dg(far, queries, 1, 1) - level)
            g_own, g_far = dg(own, gm, 1, 1), dg(far, gm, 1, 1)
            inner = jnp.sum(p_own * g_own, axis=0, keepdims=True)
            inner = inner + jnp.sum(p_far * g_far, axis=0, keepdims=True)
            s_own = (p_own * (g_own - inner)).astype(bf16)
            s_far = (p_far * (g_far - inner)).astype(bf16)
            pair_far = jnp.dot(s_far, queries, preferred_element_type=f32)
            pair_far = pair_far + jnp.dot(p_far.astype(bf16), gm, preferred_element_type=f32)
            pair_own = jnp.dot(s_own, queries, preferred_element_type=f32)
            pair_own = pair_own + jnp.dot(p_own.astype(bf16), gm, preferred_element_type=f32)
            at = pl.multiple_of(128 * h, 128)
            slope[z, 0:T, pl.ds(at, 128)] = pair_far.astype(bf16)
            slope[z, 0:T, pl.ds(pl.multiple_of(128 * heads + at, 128), 128)] = pair_own.astype(bf16)
            grad_q = dg(own, s_own, 0, 0) + dg(far, s_far, 0, 0)
            mix_t[h] = grad_q[0:HD, :] * HD ** (-0.5)

        act[z, 0:T, 128 * heads : 192 * heads] = mix_t[...].reshape(heads * HD, T).T.astype(bf16)
        send(
            "rs",
            slope.at[z, :, 0 : 128 * heads],
            act.at[z, :, 0 : 128 * heads],
            (kv_s, kv_r),
            (4 + k,),
            (dc, mp),
        )

    def project_back(k):
        z = planes[k]
        landed(act.at[z, :, 0 : 128 * heads], kv_r.at[4 + k])
        pieces = []
        for h in range(heads):
            at = 128 * heads + HD * h
            pieces.append(act[z, 0:T, at : at + HD].astype(f32))
            far = act[z, 0:T, 128 * h : 128 * h + 128].astype(f32)
            at = 128 * (heads + h)
            pieces.append(far + slope[z, 0:T, at : at + 128].astype(f32))
        pieces.append(jnp.zeros((T, HD), f32))
        slab = jnp.concatenate(pieces, axis=1).astype(bf16)
        dproj[...] = slab
        total = jnp.sum(slab.astype(f32), axis=0, keepdims=True)
        for h in range(heads):
            gbias[z, h : h + 1, 0:128] = jnp.concatenate(
                [total[:, 192 * h : 192 * h + 64], total[:, 192 * h + 128 : 192 * h + 192]], axis=1
            )
        acc[...] = acc[...] + dg(dproj[...], weight(wm, z, 0, qkv_wide), 1, 1)
        grad_qkv = dg(x_low[...], dproj[...], 0, 0)
        grad_out = dg(low[...], mixed[z], 0, 0)
        wm[z, :, :, :, 0:out_first] = tiled(grad_qkv[:, 0:out_first].astype(bf16))
        both = grad_qkv[:, out_first:] + grad_out[:, 0:128]
        wm[z, :, :, :, out_first:qkv_wide] = tiled(both.astype(bf16))
        wm[z, :, :, :, qkv_wide:] = tiled(grad_out[:, 128:].astype(bf16))
        rs_0(MIX, k)

    def finish():
        embed_sum = jnp.zeros((1, width), f32)
        for r, n in chunks:
            hidden_rows = masked_rows(r, n)
            grad = acc[r : r + n, :]
            stage_fg[r : r + n, :] = jnp.where(hidden_rows, 0.0, grad)
            embed_sum = embed_sum + jnp.sum(
                jnp.where(hidden_rows, grad, 0.0), axis=0, keepdims=True
            )
        gvec[0:1, :] = embed_sum

        @pl.when(mover)
        def _():
            remote(cot_own, cotx, move_s.at[1], move_r.at[1], swap_with).wait_send()
            cot_own[0:T, :] = stage_fg[...].astype(bf16)
            remote(cot_own, fg_far, move_s.at[3], move_r.at[4], swap_with).start()

        @pl.when(stay)
        def _():
            pltpu.make_async_copy(stage_fg, fg_out, move_r.at[3]).start()

        gs[...] = jnp.zeros(gs.shape, f32)
        for d, (j, c) in enumerate(cells):
            vectors = gvec[:, vec_cut * d : vec_cut * (d + 1)]
            for z in range(4):
                gs[z, j, c, 0:4, 0:cut] = gbias[z, 0:4, cut * d : cut * (d + 1)]
                gs[z, j, c, 4:6, 0:vec_cut] = vectors[2 * z : 2 * z + 2, :]
        for k in (1, 2, 3, 0):
            rs_0(SMALL, k)

    def take_fg():
        @pl.when(mover)
        def _():
            landed(fg_far, move_r.at[4])
            stage_fg[...] = fg_far[0:T, :].astype(f32)
            pltpu.make_async_copy(stage_fg, fg_out, move_r.at[3]).start()

    for step, *given in (
        (fall, 2),
        (fall, 3),
        (fall, 1),
        (rs_1, DOWN, 2),
        (move_act,),
        (rs_1, DOWN, 3),
        (fall, 0),
        (sink, 2),
        (sink, 3),
        (rs_2, DOWN, 2),
        (sink, 1),
        (rs_2, DOWN, 3),
        (sink, 0),
        (rs_1, DOWN, 1),
        (norm_back_one,),
        (unmix,),
        (rs_1, UP, 2),
        (attend_back, 2),
        (rs_3, DOWN, 3),
        (rs_1, UP, 1),
        (attend_back, 3),
        (rs_3, DOWN, 2),
        (rs_3, DOWN, 1),
        (rs_2, UP, 2),
        (attend_back, 1),
        (rs_1, UP, 3),
        (attend_back, 0),
        (rs_3, UP, 2),
        (project_back, 2),
        (rs_2, UP, 3),
        (rs_3, UP, 1),
        (project_back, 3),
        (rs_1, MIX, 2),
        (rs_1, UP, 0),
        (project_back, 1),
        (rs_3, UP, 3),
        (rs_1, MIX, 3),
        (project_back, 0),
        (rs_2, MIX, 2),
        (rs_1, MIX, 1),
        (finish,),
        (rs_1, SMALL, 1),
        (rs_1, SMALL, 3),
        (rs_1, SMALL, 2),
        (rs_2, MIX, 3),
        (rs_3, MIX, 2),
        (rs_1, DOWN, 0),
        (rs_2, UP, 0),
        (rs_3, MIX, 1),
        (rs_3, MIX, 3),
        (rs_1, SMALL, 0),
        (rs_2, SMALL, 3),
        (rs_2, SMALL, 1),
        (rs_1, MIX, 0),
        (rs_2, SMALL, 2),
        (rs_2, DOWN, 0),
        (rs_3, SMALL, 3),
        (rs_2, SMALL, 0),
        (rs_2, MIX, 0),
        (rs_3, SMALL, 1),
        (rs_3, SMALL, 2),
        (rs_3, DOWN, 0),
        (rs_3, UP, 0),
        (take_fg,),
        (rs_4, UP),
        (rs_4, DOWN),
        (rs_3, MIX, 0),
        (rs_3, SMALL, 0),
        (rs_4, MIX),
        (rs_4, SMALL),
    ):
        step(*given)
    row_id = lax.broadcasted_iota(jnp.int32, (8, 128), 0)
    tiles[0] = jnp.where(row_id == 7, sum(squares), small_sum[...])
    for k in (1, 2, 3):
        send("end", tiles.at[0], tiles.at[k], (tile_s, tile_r), (k,), (dp, planes[k]))
    for k in (1, 2, 3):
        landed(tiles.at[k], tile_r.at[k])
    for k in range(4):
        vec_tiles[planes[k]] = tiles[k]
    tiles[4] = vec_tiles[0] + vec_tiles[1] + vec_tiles[2] + vec_tiles[3]
    for i, d in enumerate(group):
        send("end", tiles.at[4], tiles.at[5 + i], (tile_s, tile_r), (4 + i,), (d, mp))
    for i in range(7):
        landed(tiles.at[5 + i], tile_r.at[4 + i])
    pairs = [tiles[4] + tiles[5], tiles[6] + tiles[9], tiles[7] + tiles[10], tiles[8] + tiles[11]]
    norm_ref[...] = (pairs[0] + pairs[1]) + (pairs[2] + pairs[3])
    for tag in ("kv", "rs", "end"):
        sent(tag)
    landed(act_out, move_r.at[2])
    landed(fg_out, move_r.at[3])

    @pl.when(mover)
    def _():
        remote(fm_own, fmx, move_s.at[0], move_r.at[0], swap_with).wait_send()
        remote(stage_act, act_out, move_s.at[2], move_r.at[2], swap_with).wait_send()
        remote(cot_own, fg_far, move_s.at[3], move_r.at[4], swap_with).wait_send()


def run_layer(share, frames, mask, cot, qkv, out, up, down, biases, vectors):
    width = frames.shape[1]
    tall = share + -share % 16
    heads = biases.shape[0]
    rows = qkv.shape[0]
    wide = up.shape[1]
    columns = (128, width, wide, wide)
    types = (f32, bf16, bf16, bf16)
    heights = (16, rows, rows, rows)
    weights = [
        pltpu.VMEM((4, 4, 2, n, c), t) for n, c, t in zip(heights, columns, types)
    ] + [pltpu.VMEM((4, 4, 2, 8, 128), f32)]
    pieces = list(zip((8, rows, rows, rows), columns, types))
    arrivals = [
        pltpu.VMEM((*lead, n, c), t)
        for lead in ((4, 4), (4,), (4,), (4,), (3,))
        for n, c, t in pieces
    ]
    activations = [
        pltpu.VMEM((tall, width + 128), bf16),
        pltpu.VMEM((tall, width), bf16),
        pltpu.VMEM((tall, width + 128), bf16),
        pltpu.VMEM((tall, width), bf16),
        pltpu.VMEM((share, width), bf16),
        pltpu.VMEM((4, heads, share, 128), bf16),
        pltpu.VMEM((4, heads, tall, 128), bf16),
        pltpu.VMEM((4, heads, tall, 128), bf16),
        pltpu.VMEM((4, share, heads * HD + HD), bf16),
        pltpu.VMEM((4, heads, 1, share), f32),
        pltpu.VMEM((heads, HD, share), f32),
        pltpu.VMEM((share, width), f32),
        pltpu.VMEM((share, 1), f32),
        pltpu.VMEM((share, width), bf16),
        pltpu.VMEM((4, tall, wide), bf16),
        pltpu.VMEM((4, tall, wide), bf16),
        pltpu.VMEM((share, width), f32),
        pltpu.VMEM((share, width), bf16),
        pltpu.VMEM((4, heads, share, 128), bf16),
        pltpu.VMEM((share, qkv.shape[1] + HD), bf16),
        pltpu.VMEM((share, width), f32),
        pltpu.VMEM((share, width), f32),
        pltpu.VMEM((tall, width), bf16),
        pltpu.VMEM((8, width), f32),
        pltpu.VMEM((4, 8, 384), f32),
        pltpu.VMEM((8, width), f32),
        pltpu.VMEM((4, 8, 384), f32),
        pltpu.VMEM((12, 8, 128), f32),
    ]
    semaphores = [pltpu.SemaphoreType.DMA((4, SEMS)) for _ in range(4)] + [
        pltpu.SemaphoreType.DMA((n,)) for n in (8, 8, 5, 5, 12, 12)
    ]
    anywhere = pl.BlockSpec(memory_space=pl.ANY)
    vmem = pl.BlockSpec(memory_space=pltpu.VMEM)
    shapes = [
        (share, width),
        (share, width),
        (8, 128),
        (rows, width),
        (rows, wide),
        (rows, wide),
        (8, 128),
        (4, 8, 128),
    ]
    return pl.pallas_call(
        functools.partial(layer_kernel, share),
        out_shape=tuple(jax.ShapeDtypeStruct(s, f32) for s in shapes),
        in_specs=[vmem] * 9,
        out_specs=(anywhere,) * 2 + (vmem,) * 6,
        scratch_shapes=weights + arrivals + activations + semaphores,
        compiler_params=pltpu.CompilerParams(
            collective_id=0, has_side_effects=True, vmem_limit_bytes=60 * 2**20
        ),
        name="encoder_layer",
    )(frames, mask, cot, qkv, out, up, down, biases, vectors)


def update_kernel(*refs):
    given, made = refs[:26], refs[26:47]
    held, ready = refs[47:73], refs[73:92]
    come, leave = refs[92:]
    arriving = [
        pltpu.make_async_copy(src, dst, come.at[i]) for i, (src, dst) in enumerate(zip(given, held))
    ]
    for copy in arriving:
        copy.start()
    leaving = []

    def out(src, i):
        copy = pltpu.make_async_copy(src, made[i], leave.at[i])
        copy.start()
        leaving.append(copy)

    for copy in arriving[:6]:
        copy.wait()
    small, mix, up, down, norm, vec_tiles = held[:6]
    state = held[8:]
    grad_norm = jnp.sqrt(norm[7:8, 0:1])
    ready[0][...] = grad_norm
    out(ready[0], 0)
    factor = jnp.minimum(1.0, clip_limit / (grad_norm + 1e-06))
    qkv_columns = state[0].shape[1]
    first = mix.shape[1] - state[3].shape[0] - HD
    heads, cut = state[12].shape
    vec_rows, vec_cut = state[15].shape
    gradients = (
        lambda: mix[:, 0:qkv_columns],
        lambda: mix[:, first:].T[HD:, :],
        lambda: up[...],
        lambda: down[...],
        lambda: small[0:heads, 0:cut],
        lambda: jnp.concatenate([vec_tiles[z, 4:6, 0:vec_cut] for z in range(4)], axis=0)[0:vec_rows, :],
    )
    for i in (2, 3, 0, 1, 4, 5):
        old = state[3 * i : 3 * i + 3]
        for copy in arriving[8 + 3 * i : 11 + 3 * i]:
            copy.wait()
        values = adam_step(*(ref[...] for ref in old), gradients[i](), factor, *settings[i])
        for at, value in enumerate(values):
            ready[1 + 3 * i + at][...] = value
            out(ready[1 + 3 * i + at], 3 + 3 * i + at)
    for at in range(2):
        arriving[6 + at].wait()
        out(held[6 + at], 1 + at)
    for copy in leaving:
        copy.wait()


def run_update(sums, norm, vec_tiles, act, fg, state):
    anywhere = pl.BlockSpec(memory_space=pl.ANY)
    given = (*sums, norm, vec_tiles, act, fg, *state)
    shapes = [(1, 1), act.shape, fg.shape] + [a.shape for a in state]
    return pl.pallas_call(
        update_kernel,
        out_shape=tuple(jax.ShapeDtypeStruct(s, f32) for s in shapes),
        in_specs=[anywhere] * len(given),
        out_specs=(anywhere,) * len(shapes),
        scratch_shapes=[pltpu.VMEM(a.shape, f32) for a in given]
        + [pltpu.VMEM(s, f32) for s in shapes[:1] + shapes[3:]]
        + [pltpu.SemaphoreType.DMA((len(given),)), pltpu.SemaphoreType.DMA((len(shapes),))],
        compiler_params=pltpu.CompilerParams(vmem_limit_bytes=60 * 2**20),
        name="update_weights",
    )(*given)


def on_device_fast(
    frames,
    span_mask,
    cotangent,
    qkv_weight,
    qkv_mean,
    qkv_square,
    out_weight,
    out_mean,
    out_square,
    up_weight,
    up_mean,
    up_square,
    down_weight,
    down_mean,
    down_square,
    head_biases,
    bias_mean,
    bias_square,
    norm_vectors,
    vector_mean,
    vector_square,
):
    share = frames.shape[0]
    act, fg, *sums, norm, vec_tiles = run_layer(
        share,
        frames,
        span_mask,
        cotangent,
        qkv_weight,
        out_weight,
        up_weight,
        down_weight.T,
        head_biases,
        norm_vectors,
    )
    down = (down_weight.T, down_mean.T, down_square.T)
    state = (qkv_weight, qkv_mean, qkv_square, out_weight, out_mean, out_square)
    state += (up_weight, up_mean, up_square, *down, head_biases, bias_mean, bias_square)
    state += (norm_vectors, vector_mean, vector_square)
    grad_norm, outputs, frame_grad, *updated = run_update(sums, norm, vec_tiles, act, fg, state)
    updated[9:12] = [value.T for value in updated[9:12]]
    return (outputs, frame_grad, grad_norm.reshape(()), *updated)


def solution(mesh):
    return jax.shard_map(
        on_device_fast if fast_fits(mesh) else on_device,
        mesh=mesh,
        in_specs=(
            P(("dp", "mp"), None),
            P("dp", None),
            P(("dp", "mp"), None),
            P("dp", "mp"),
            P("dp", "mp"),
            P("dp", "mp"),
            P("mp", "dp"),
            P("mp", "dp"),
            P("mp", "dp"),
            P("dp", "mp"),
            P("dp", "mp"),
            P("dp", "mp"),
            P("mp", "dp"),
            P("mp", "dp"),
            P("mp", "dp"),
            P("mp", "dp"),
            P("mp", "dp"),
            P("mp", "dp"),
            P(None, "dp"),
            P(None, "dp"),
            P(None, "dp"),
        ),
        out_specs=(
            P(("dp", "mp"), None),
            P(("dp", "mp"), None),
            P(),
            P("dp", "mp"),
            P("dp", "mp"),
            P("dp", "mp"),
            P("mp", "dp"),
            P("mp", "dp"),
            P("mp", "dp"),
            P("dp", "mp"),
            P("dp", "mp"),
            P("dp", "mp"),
            P("mp", "dp"),
            P("mp", "dp"),
            P("mp", "dp"),
            P("mp", "dp"),
            P("mp", "dp"),
            P("mp", "dp"),
            P(None, "dp"),
            P(None, "dp"),
            P(None, "dp"),
        ),
        check_vma=False,
    )
```

```python
import functools

import jax
import jax.numpy as jnp
from jax import lax
from jax.experimental import pallas as pl
from jax.experimental.pallas import tpu as pltpu
from jax.sharding import PartitionSpec as P

HD = 64
LEN = 688


norm_eps = 1e-05
adam_eps = 1e-08
beta_one = 0.9
beta_two = 0.999
step_count = 10.0
clip_limit = 1.0
settings = ((0.05, 0.1), (0.3, 0.1), (0.05, 0.1), (0.03, 0.1), (0.3, 0.0), (0.4, 0.0))


def norm_rows(values, norm_gain, norm_shift):
    centred = values - jnp.mean(values, axis=-1, keepdims=True)
    variance = jnp.mean(centred * centred, axis=-1, keepdims=True)
    inverse = lax.rsqrt(variance + norm_eps)
    normed = centred * inverse
    return (normed * norm_gain + norm_shift, normed, inverse)


def norm_back(upstream, normed, inverse, norm_gain):
    scaled = upstream * norm_gain
    inner_part = (
        scaled
        - jnp.mean(scaled, axis=-1, keepdims=True)
        - normed * jnp.mean(scaled * normed, axis=-1, keepdims=True)
    )
    return (inverse * inner_part, jnp.sum(upstream * normed, axis=0), jnp.sum(upstream, axis=0))


def gelu_slope(pre_act):
    cumulative = 0.5 * (1.0 + jax.scipy.special.erf(pre_act * 0.7071067811865476))
    return cumulative + pre_act * jnp.exp(-0.5 * pre_act * pre_act) * 0.3989422804014327


def attend_forward(clip_block):
    scaling = HD ** (-0.5)
    queries = clip_block[:, :, 0]
    key_rows = clip_block[:, :, 1]
    value_rows = clip_block[:, :, 2]
    scores = (
        jnp.einsum("qhe,khe->hqk", queries, key_rows, preferred_element_type=jnp.float32) * scaling
    )
    row_peak = jnp.max(scores, axis=-1, keepdims=True)
    log_total = row_peak + jnp.log(jnp.sum(jnp.exp(scores - row_peak), axis=-1, keepdims=True))
    attention = jnp.exp(scores - log_total).astype(jnp.bfloat16)
    mixed_rows = jnp.einsum(
        "hqk,khe->qhe", attention, value_rows, preferred_element_type=jnp.float32
    )
    return (mixed_rows.astype(jnp.bfloat16).reshape(clip_block.shape[0], -1), log_total)


def attend_backward(pieces):
    clip_block, log_total, grad_mixed = pieces
    scaling = HD ** (-0.5)
    queries = clip_block[:, :, 0]
    key_rows = clip_block[:, :, 1]
    value_rows = clip_block[:, :, 2]
    scores = (
        jnp.einsum("qhe,khe->hqk", queries, key_rows, preferred_element_type=jnp.float32) * scaling
    )
    attention = jnp.exp(scores - log_total)
    attention_low = attention.astype(jnp.bfloat16)
    mixed_rows = jnp.einsum(
        "hqk,khe->qhe", attention_low, value_rows, preferred_element_type=jnp.float32
    ).astype(jnp.bfloat16)
    grad_rows = grad_mixed.reshape(queries.shape)
    grad_attention = jnp.einsum(
        "qhe,khe->hqk", grad_rows, value_rows, preferred_element_type=jnp.float32
    )
    grad_values = jnp.einsum(
        "hqk,qhe->khe", attention_low, grad_rows, preferred_element_type=jnp.float32
    )
    row_inner = jnp.sum(attention * grad_attention, axis=-1, keepdims=True)
    grad_scores = (attention * (grad_attention - row_inner)).astype(jnp.bfloat16)
    grad_queries = (
        jnp.einsum("hqk,khe->qhe", grad_scores, key_rows, preferred_element_type=jnp.float32)
        * scaling
    )
    grad_keys = (
        jnp.einsum("hqk,qhe->khe", grad_scores, queries, preferred_element_type=jnp.float32)
        * scaling
    )
    grad_block = jnp.stack([grad_queries, grad_keys, grad_values], axis=2).astype(jnp.bfloat16)
    return (
        mixed_rows.reshape(clip_block.shape[0], -1),
        grad_block.reshape(clip_block.shape[0], -1),
    )


def adam_step(weight, mean_old, square_old, gradient, factor, rate, decay):
    clipped = gradient * factor
    mean_new = beta_one * mean_old + (1.0 - beta_one) * clipped
    square_new = beta_two * square_old + (1.0 - beta_two) * clipped * clipped
    mean_hat = mean_new / (1.0 - beta_one**step_count)
    square_hat = square_new / (1.0 - beta_two**step_count)
    weight_new = weight - rate * (mean_hat / (jnp.sqrt(square_hat) + adam_eps) + decay * weight)
    return (weight_new, mean_new, square_new)


def on_device(
    frames,
    span_mask,
    cotangent,
    qkv_weight,
    qkv_mean,
    qkv_square,
    out_weight,
    out_mean,
    out_square,
    up_weight,
    up_mean,
    up_square,
    down_weight,
    down_mean,
    down_square,
    head_biases,
    bias_mean,
    bias_square,
    norm_vectors,
    vector_mean,
    vector_square,
):
    masters = (qkv_weight, out_weight, up_weight, down_weight, head_biases, norm_vectors)
    lowered = tuple((weight.astype(jnp.bfloat16) for weight in masters))
    qkv_full, out_full, up_full, down_full, bias_full, vector_full = (
        lax.all_gather(lowered[0], "dp", axis=0, tiled=True),
        lax.all_gather(lowered[1], "dp", axis=1, tiled=True),
        lax.all_gather(lowered[2], "dp", axis=0, tiled=True),
        lax.all_gather(lowered[3], "dp", axis=1, tiled=True),
        lax.all_gather(lowered[4], "dp", axis=1, tiled=True),
        lax.all_gather(lowered[5], "dp", axis=1, tiled=True),
    )
    share_rows = frames.shape[0]
    start_row = lax.axis_index("mp") * share_rows
    vectors = vector_full.astype(jnp.float32)
    local_heads = bias_full.shape[0]

    def share_of(array_full):
        return lax.dynamic_slice_in_dim(array_full, start_row, share_rows, 0)

    gathered = lax.all_gather(frames, "mp", axis=0, tiled=True)
    all_rows = gathered.shape[0]
    masked = span_mask.reshape(all_rows, 1) == 1
    inputs = jnp.where(masked, vectors[0], gathered.astype(jnp.float32))
    rounded = inputs.astype(jnp.bfloat16)
    zero_bias = jnp.zeros_like(bias_full[:, :HD])
    qkv_bias = (
        jnp.stack([bias_full[:, :HD], zero_bias, bias_full[:, HD : 2 * HD]], axis=1)
        .reshape(-1)
        .astype(jnp.float32)
    )
    up_bias = bias_full[:, 2 * HD :].reshape(-1).astype(jnp.float32)
    projected = (jnp.dot(rounded, qkv_full, preferred_element_type=jnp.float32) + qkv_bias).astype(
        jnp.bfloat16
    )
    blocks = projected.reshape(-1, LEN, local_heads, 3, HD)
    mixed_rows, log_total = lax.map(attend_forward, blocks)
    mixed_rows = mixed_rows.reshape(all_rows, -1)
    attn_part = jnp.dot(mixed_rows, out_full, preferred_element_type=jnp.float32)
    attended = lax.psum(attn_part, "mp")
    first_sum = inputs + attended + vectors[5]
    hidden, normed_full, inverse_full = norm_rows(first_sum, vectors[1], vectors[2])
    normed_one = share_of(normed_full)
    inverse_one = share_of(inverse_full)
    hidden_low = hidden.astype(jnp.bfloat16)
    pre_act = jnp.dot(hidden_low, up_full, preferred_element_type=jnp.float32) + up_bias
    activated = jax.nn.gelu(pre_act, approximate=False).astype(jnp.bfloat16)
    ffn_part = jnp.dot(activated, down_full, preferred_element_type=jnp.float32)
    second_sum = hidden + lax.psum(ffn_part, "mp") + vectors[6]
    outputs_full, normed_full, inverse_full = norm_rows(second_sum, vectors[3], vectors[4])
    outputs = share_of(outputs_full)
    normed_two = share_of(normed_full)
    inverse_two = share_of(inverse_full)
    qkv_full, out_full, up_full, down_full, bias_full, vector_full = (
        lax.all_gather(lowered[0], "dp", axis=0, tiled=True),
        lax.all_gather(lowered[1], "dp", axis=1, tiled=True),
        lax.all_gather(lowered[2], "dp", axis=0, tiled=True),
        lax.all_gather(lowered[3], "dp", axis=1, tiled=True),
        lax.all_gather(lowered[4], "dp", axis=1, tiled=True),
        lax.all_gather(lowered[5], "dp", axis=1, tiled=True),
    )
    upstream = cotangent.astype(jnp.float32)
    grad_two, grad_gain_two, grad_shift_two = norm_back(
        upstream, normed_two, inverse_two, vectors[3]
    )
    grad_down_bias = jnp.sum(grad_two, axis=0)
    grad_two_full = lax.all_gather(grad_two.astype(jnp.bfloat16), "mp", axis=0, tiled=True)
    pre_again = jnp.dot(hidden_low, up_full, preferred_element_type=jnp.float32) + up_bias
    act_again = jax.nn.gelu(pre_again, approximate=False).astype(jnp.bfloat16)
    grad_down = jnp.einsum(
        "tf,td->fd", act_again, grad_two_full, preferred_element_type=jnp.float32
    )
    grad_act = jnp.einsum("td,fd->tf", grad_two_full, down_full, preferred_element_type=jnp.float32)
    grad_pre = (grad_act * gelu_slope(pre_again)).astype(jnp.bfloat16)
    grad_up = jnp.einsum("td,tf->df", hidden_low, grad_pre, preferred_element_type=jnp.float32)
    grad_up_bias = jnp.sum(grad_pre, axis=0, dtype=jnp.float32)
    hidden_part = jnp.einsum("tf,df->td", grad_pre, up_full, preferred_element_type=jnp.float32)
    grad_hidden = grad_two + lax.psum_scatter(hidden_part, "mp", scatter_dimension=0, tiled=True)
    grad_one, grad_gain_one, grad_shift_one = norm_back(
        grad_hidden, normed_one, inverse_one, vectors[1]
    )
    grad_out_bias = jnp.sum(grad_one, axis=0)
    grad_one_full = lax.all_gather(grad_one.astype(jnp.bfloat16), "mp", axis=0, tiled=True)
    grad_mixed = jnp.einsum(
        "td,cd->tc", grad_one_full, out_full, preferred_element_type=jnp.float32
    ).astype(jnp.bfloat16)
    mixed_again, grad_blocks = lax.map(
        attend_backward, (blocks, log_total, grad_mixed.reshape(-1, LEN, grad_mixed.shape[1]))
    )
    mixed_again = mixed_again.reshape(all_rows, -1)
    grad_blocks = grad_blocks.reshape(all_rows, -1)
    grad_out = jnp.einsum(
        "tc,td->cd", mixed_again, grad_one_full, preferred_element_type=jnp.float32
    )
    grad_qkv = jnp.einsum("td,tc->dc", rounded, grad_blocks, preferred_element_type=jnp.float32)
    bias_sums = jnp.sum(grad_blocks, axis=0, dtype=jnp.float32).reshape(local_heads, 3, HD)
    grad_biases = jnp.concatenate(
        [bias_sums[:, 0], bias_sums[:, 2], grad_up_bias.reshape(local_heads, -1)], axis=1
    )
    input_part = jnp.einsum("tc,dc->td", grad_blocks, qkv_full, preferred_element_type=jnp.float32)
    grad_inputs = grad_one + lax.psum_scatter(
        input_part.astype(jnp.bfloat16), "mp", scatter_dimension=0, tiled=True
    ).astype(jnp.float32)
    masked_share = share_of(masked)
    grad_embed = jnp.sum(jnp.where(masked_share, grad_inputs, 0.0), axis=0)
    frame_grad = jnp.where(masked_share, 0.0, grad_inputs)
    grad_vectors = jnp.stack(
        [
            grad_embed,
            grad_gain_one,
            grad_shift_one,
            grad_gain_two,
            grad_shift_two,
            grad_out_bias,
            grad_down_bias,
        ]
    )
    reduced = (
        lax.psum_scatter(grad_qkv, "dp", scatter_dimension=0, tiled=True),
        lax.psum_scatter(grad_out, "dp", scatter_dimension=1, tiled=True),
        lax.psum_scatter(grad_up, "dp", scatter_dimension=0, tiled=True),
        lax.psum_scatter(grad_down, "dp", scatter_dimension=1, tiled=True),
        lax.psum_scatter(grad_biases, "dp", scatter_dimension=1, tiled=True),
    )
    local_squares = jnp.float32(0.0)
    for portion in reduced:
        local_squares = local_squares + jnp.sum(portion * portion)
    total_squares, vector_total = lax.psum((local_squares, grad_vectors), ("dp", "mp"))
    grad_norm = jnp.sqrt(total_squares + jnp.sum(vector_total * vector_total))
    column_count = norm_vectors.shape[1]
    vector_grad = lax.dynamic_slice_in_dim(
        vector_total, lax.axis_index("dp") * column_count, column_count, 1
    )
    factor = jnp.minimum(1.0, clip_limit / (grad_norm + 1e-06))
    gradients = (reduced[0], reduced[1], reduced[2], reduced[3], reduced[4], vector_grad)
    means = (qkv_mean, out_mean, up_mean, down_mean, bias_mean, vector_mean)
    squares = (qkv_square, out_square, up_square, down_square, bias_square, vector_square)
    updated = []
    for index_at in range(6):
        updated.extend(
            adam_step(
                masters[index_at],
                means[index_at],
                squares[index_at],
                gradients[index_at],
                factor,
                settings[index_at][0],
                settings[index_at][1],
            )
        )
    return (
        outputs,
        frame_grad,
        grad_norm,
        updated[0],
        updated[1],
        updated[2],
        updated[3],
        updated[4],
        updated[5],
        updated[6],
        updated[7],
        updated[8],
        updated[9],
        updated[10],
        updated[11],
        updated[12],
        updated[13],
        updated[14],
        updated[15],
        updated[16],
        updated[17],
    )


MESH = pl.DeviceIdType.MESH
SMALL, MIX, UP, DOWN = range(4)
SEMS = 32
f32, bf16 = jnp.float32, jnp.bfloat16


def fast_fits(mesh):
    return mesh.shape["dp"] == 8 and mesh.shape["mp"] == 4


def flip(dp, bit):
    held = lax.rem(lax.div(dp, bit), 2)
    return dp + bit - 2 * bit * held


def dg(a, b, ca, cb):
    return lax.dot_general(a, b, (((ca,), (cb,)), ((), ())), preferred_element_type=f32)


def landed(dst, sem):
    pltpu.make_async_copy(dst, dst, sem).wait()


def layer_kernel(
    share,
    frames_in,
    mask_in,
    cot_in,
    qkv_in,
    out_in,
    up_in,
    down_in,
    bias_in,
    vec_in,
    act_out,
    fg_out,
    small_sum,
    mix_sum,
    up_sum,
    down_sum,
    norm_ref,
    vec_tiles,
    ws,
    wm,
    wu,
    wd,
    gs,
    gd,
    rcs,
    rcm,
    rcu,
    rcd,
    rds,
    rdm,
    rdu,
    rdd,
    rxs,
    rxm,
    rxu,
    rxd,
    rys,
    rym,
    ryu,
    ryd,
    rzs,
    rzm,
    rzu,
    rzd,
    fm_own,
    cot_own,
    fmx,
    cotx,
    x_low,
    q_all,
    kv_own,
    kv_far,
    mixed,
    lse,
    mix_t,
    n_one,
    r_one,
    hid_low,
    act,
    slope,
    acc,
    low,
    dm,
    dproj,
    far_pair,
    frames_at,
    cot_at,
    up_at,
    down_at,
    small_at,
    stage_act,
    stage_fg,
    fg_far,
    vec,
    bias,
    gvec,
    gbias,
    tiles,
    gather_s,
    gather_r,
    reduce_s,
    reduce_r,
    kv_s,
    kv_r,
    move_s,
    move_r,
    tile_s,
    tile_r,
    load_s,
):
    T = share
    dp, mp = lax.axis_index("dp"), lax.axis_index("mp")
    core = lax.rem(dp, 2)
    dx, dy, dc = flip(dp, 2), flip(dp, 4), flip(dp, 1)
    dd = flip(dx, 4)
    planes = (mp, flip(mp, 1), flip(mp, 2), flip(flip(mp, 1), 2))
    mover = lax.rem(core + mp, 2) == 1
    stay = lax.rem(core + mp, 2) == 0
    swap_with = (dc, planes[1])
    full = (ws, wm, wu, wd)
    local = (gs, wm, wu, gd)
    from_core = (rcs, rcm, rcu, rcd)
    from_diag = (rds, rdm, rdu, rdd)
    from_x = (rxs, rxm, rxu, rxd)
    from_y = (rys, rym, ryu, ryd)
    from_z = (rzs, rzm, rzu, rzd)
    result = (small_sum, mix_sum, up_sum, down_sum)
    heads = q_all.shape[1]
    chunks = [(r, min(88, T - r)) for r in range(0, T, 88)]

    def remote(src, dst, send_sem, recv_sem, device):
        return pltpu.make_async_remote_copy(
            src_ref=src,
            dst_ref=dst,
            send_sem=send_sem,
            recv_sem=recv_sem,
            device_id=device,
            device_id_type=MESH,
        )

    pending = {}

    def send(tag, src, dst, sems, at, device):
        copy = remote(src, dst, sems[0].at[at], sems[1].at[at], device)
        copy.start()
        pending.setdefault(tag, []).append(copy)

    def sent(tag):
        for copy in pending.pop(tag, []):
            copy.wait_send()

    def hand_over(slot, src, dst):
        @pl.when(mover)
        def _():
            remote(src, dst, move_s.at[slot], move_r.at[slot], swap_with).start()

        @pl.when(stay)
        def _():
            pltpu.make_async_copy(src, dst, move_r.at[slot]).start()

    def halves(ref):
        n = ref.shape[-2] // 2
        return ref.at[pl.ds(0, n)], ref.at[pl.ds(n, n)]

    gather = (gather_s, gather_r)

    def slot(w, k, d):
        return full[w].at[planes[k], lax.div(d, 2), lax.rem(d, 2)]

    def ag_own(w):
        for k in (1, 2, 3):
            send(("ag", w), slot(w, 0, dp), slot(w, 0, dp), gather, (w, k), (dp, planes[k]))

    def ag_a(w, k):
        ref = slot(w, k, dp)
        if k:
            landed(ref, gather_r.at[w, k])
        send(("ag", w), ref, ref, gather, (w, 4 + k), (dx, mp))
        send(("ag", w), ref, ref, gather, (w, 8 + k), (dy, mp))

    own_j, x_j, y_j, d_j = (lax.div(d, 2) for d in (dp, dx, dy, dd))
    row_j = 2 * lax.div(own_j, 2)

    def to_core(w, k, cells, at):
        ref = full[w].at[planes[k], cells, core]
        send(("ag", w), ref, ref, gather, (w, at), (dc, mp))

    def ag_b(w, k):
        at_x, at_y = slot(w, k, dx), slot(w, k, dy)
        landed(at_x, gather_r.at[w, 4 + k])
        if k == 2 or (w == SMALL and k == 0):
            send(("ag", w), at_x, at_x, gather, (w, 12 + k), (dy, mp))
        elif k == 0:
            ref = halves(at_x)[0]
            send(("ag", w), ref, ref, gather, (w, 12), (dy, mp))
        if w == DOWN:
            to_core(w, k, pl.ds(row_j, 2), 17 + k)
        landed(at_y, gather_r.at[w, 8 + k])
        if k == 3 or (w == SMALL and k == 1):
            send(("ag", w), at_y, at_y, gather, (w, 12 + k), (dx, mp))
        elif k == 0 and w != SMALL:
            ref = halves(at_y)[1]
            send(("ag", w), ref, ref, gather, (w, 13), (dx, mp))
        if w == DOWN:
            to_core(w, k, y_j, 21 + k)

    def ag_c(w, k):
        ref = slot(w, k, dd)
        if w == SMALL or k > 1:
            landed(ref, gather_r.at[w, 12 + k])
        elif k == 0:
            for i, half in enumerate(halves(ref)):
                landed(half, gather_r.at[w, 12 + i])
            send(("ag", w), ref, ref, gather, (w, 16), (dp, planes[1]))
        else:
            landed(ref, gather_r.at[w, 16])
        if w == DOWN:
            to_core(w, k, d_j, 25 + k)
        else:
            to_core(w, k, slice(None), 17 + k)

    def ag_d(w, k):
        if w == DOWN:
            for cells, at in ((pl.ds(row_j, 2), 17), (y_j, 21), (d_j, 25)):
                landed(full[w].at[planes[k], cells, 1 - core], gather_r.at[w, at + k])
        else:
            landed(full[w].at[planes[k], :, 1 - core], gather_r.at[w, 17 + k])

    squares = []
    reduce = (reduce_s, reduce_r)

    def part(w, k, d):
        return local[w].at[planes[k], lax.div(d, 2), lax.rem(d, 2)]

    def add_to(ref, arrived):
        ref[...] = ref[...] + arrived[...]

    def rs_0(w, k):
        send("rs", local[w].at[planes[k], :, 1 - core], from_core[w].at[k], reduce, (w, k), (dc, mp))

    def rs_1(w, k):
        landed(from_core[w].at[k], reduce_r.at[w, k])
        add_to(local[w].at[planes[k], :, core], from_core[w].at[k])
        at_d, at_x, at_y = part(w, k, dd), part(w, k, dx), part(w, k, dy)
        to_d, to_x, to_y = from_diag[w].at[k], from_x[w].at[k], from_y[w].at[k]
        if w == SMALL or k > 1:
            if k % 2:
                send("rs", at_d, to_d, reduce, (w, 4 + k), (dx, mp))
                send("rs", at_x, to_x, reduce, (w, 10 + k), (dx, mp))
            else:
                send("rs", at_d, to_d, reduce, (w, 4 + k), (dy, mp))
                send("rs", at_y, to_y, reduce, (w, 15 + k), (dy, mp))
        elif k == 1:
            send("rs", at_d, to_d, reduce, (w, 4), (dp, planes[1]))
            send("rs", at_x, to_x, reduce, (w, 10 + k), (dx, mp))
            send("rs", at_y, to_y, reduce, (w, 15 + k), (dy, mp))
        else:
            landed(from_diag[w].at[1], reduce_r.at[w, 4])
            add_to(at_d, from_diag[w].at[1])
            send("rs", halves(at_d)[0], halves(to_d)[0], reduce, (w, 8), (dx, mp))
            send("rs", halves(at_d)[1], halves(to_d)[1], reduce, (w, 9), (dy, mp))
            send("rs", halves(at_x)[0], halves(to_x)[0], reduce, (w, 10), (dx, mp))
            send("rs", halves(at_y)[1], halves(to_y)[1], reduce, (w, 15), (dy, mp))

    def rs_2(w, k):
        at_x, at_y = part(w, k, dx), part(w, k, dy)
        come, to_x, to_y = from_diag[w].at[k], from_x[w].at[k], from_y[w].at[k]
        if w == SMALL or k > 1:
            landed(come, reduce_r.at[w, 4 + k])
            if k % 2:
                add_to(at_y, come)
                send("rs", at_y, to_y, reduce, (w, 15 + k), (dy, mp))
            else:
                add_to(at_x, come)
                send("rs", at_x, to_x, reduce, (w, 10 + k), (dx, mp))
        else:
            first, second = halves(come)
            landed(first, reduce_r.at[w, 8])
            add_to(halves(at_y)[0], first)
            send("rs", halves(at_y)[0], halves(to_y)[0], reduce, (w, 19), (dy, mp))
            landed(second, reduce_r.at[w, 9])
            add_to(halves(at_x)[1], second)
            send("rs", halves(at_x)[1], halves(to_x)[1], reduce, (w, 14), (dx, mp))

    def rs_3(w, k):
        if w == SMALL or k:
            landed(from_x[w].at[k], reduce_r.at[w, 10 + k])
            landed(from_y[w].at[k], reduce_r.at[w, 15 + k])
        else:
            for half, at in zip(halves(from_x[w].at[0]), (10, 14)):
                landed(half, reduce_r.at[w, at])
            for half, at in zip(halves(from_y[w].at[0]), (19, 15)):
                landed(half, reduce_r.at[w, at])
        ref = part(w, k, dp)
        total = ref[...].astype(f32) + from_x[w][k].astype(f32) + from_y[w][k].astype(f32)
        if k:
            ref[...] = total.astype(ref.dtype)
            send("rs", ref, from_z[w].at[k - 1], reduce, (w, 19 + k), (dp, planes[k]))
        else:
            result[w][...] = total

    def rs_4(w):
        total = result[w][...]
        for k in (1, 2, 3):
            landed(from_z[w].at[k - 1], reduce_r.at[w, 19 + k])
            total = total + from_z[w][k - 1].astype(f32)
        result[w][...] = total
        squares.append(jnp.sum(total * total))

    loads = [
        pltpu.make_async_copy(src, dst, load_s.at[i])
        for i, (src, dst) in enumerate(
            ((up_in, up_at), (frames_in, frames_at), (down_in, down_at), (cot_in, cot_at))
        )
    ]
    for copy in loads:
        copy.start()
    cut, vec_cut = bias_in.shape[1], vec_in.shape[1]
    width, wide = frames_in.shape[1], up_in.shape[1]
    qkv_wide = 192 * heads + 64
    out_first = 192 * heads - 64
    lane = lax.broadcasted_iota(jnp.int32, (1, 128), 1)
    cells = [(j, c) for j in range(4) for c in range(2)]
    group = [dc, dx, dy, dd, flip(dx, 1), flip(dy, 1), flip(dd, 1)]
    others = [(d, mp) for d in group] + [(dp, planes[k]) for k in (1, 2, 3)] + [swap_with]
    bar = pltpu.get_barrier_semaphore()
    for device in others:
        pl.semaphore_signal(bar, inc=1, device_id=device, device_id_type=MESH)
    small_at[...] = jnp.zeros(small_at.shape, f32)
    small_at[0:heads, 0:cut] = bias_in[...]
    small_at[8:15, 0:vec_cut] = vec_in[...]
    ws[mp, own_j, core] = small_at[...].astype(bf16)

    def prep_mix():
        wm[mp, own_j, core] = jnp.concatenate([qkv_in[...], out_in[...].T], axis=1).astype(bf16)

    def prep_up():
        loads[0].wait()
        wu[mp, own_j, core] = up_at[...].astype(bf16)

    def prep_down():
        loads[2].wait()
        wd[mp, own_j, core] = down_at[...].astype(bf16)

    def prep_flags():
        flags = mask_in[...].astype(f32)
        flags = jnp.where(lax.rem(mp, 2) == 0, flags[:, 0:T], flags[:, T : 2 * T])
        flags = jnp.where(lax.div(mp, 2) == 0, flags[0:1, :], flags[1:2, :])
        loads[1].wait()
        fm_own[0:T, 0:width] = frames_at[...]
        fm_own[0:T, width:] = jnp.broadcast_to(flags, (128, T)).T.astype(bf16)

    def move_frames():
        hand_over(0, fm_own, fmx)

    def move_cot():
        loads[3].wait()
        cot_own[0:T, :] = cot_at[...]
        hand_over(1, cot_own, cotx)

    def unpack():
        for k in range(4):
            ag_d(SMALL, k)
        for z in range(4):
            held = [ws[z, j, c].astype(f32) for j, c in cells]
            bias[z] = jnp.concatenate([piece[0:8, 0:cut] for piece in held], axis=1)
            if z == 0:
                vec[...] = jnp.concatenate([piece[8:16, 0:vec_cut] for piece in held], axis=1)

    def vector(i):
        return vec[i : i + 1, :]

    embed, gain_one, shift_one, gain_two, shift_two, out_add, down_add = (
        functools.partial(vector, i) for i in range(7)
    )

    def masked_rows(r, n):
        flag = fmx[r : r + n, width:].astype(f32)
        return jnp.concatenate([flag] * (width // 128), axis=1) > 0.5

    def input_rows(r, n):
        return jnp.where(masked_rows(r, n), embed(), fmx[r : r + n, 0:width].astype(f32))

    def round_inputs():
        landed(fmx, move_r.at[0])
        for r, n in chunks:
            x_low[r : r + n, :] = input_rows(r, n).astype(bf16)

    def weight(ref, z, first, last):
        return ref[z, :, :, :, first:last].reshape(width, last - first)

    def add_up(piece, first):
        acc[...] = piece if first else acc[...] + piece

    def project(k):
        z = planes[k]
        ag_d(MIX, k)
        slab = jnp.dot(x_low[...], weight(wm, z, 0, qkv_wide), preferred_element_type=f32)
        for h in range(heads):
            both = bias[z, h : h + 1, 0:128]
            head = slab[:, 192 * h : 192 * h + 128] + both
            head = head.astype(bf16).astype(f32) * HD ** (-0.5)
            q_all[z, h] = jnp.where(lane < HD, head, 0.0).astype(bf16)
            pair = slab[:, 192 * h + 64 : 192 * h + 192] + jnp.where(lane < HD, 0.0, both)
            kv_own[z, h, 0:T, :] = pair.astype(bf16)
        send("kv", kv_own.at[z], kv_far.at[z], (kv_s, kv_r), (k,), (dc, mp))

    def stand(value):
        flat = value.reshape(heads * HD, T)
        return jnp.concatenate([jnp.zeros((HD, T), f32), flat], axis=0).T.astype(bf16)

    def attend(k, h):
        z = planes[k]
        if h == 0:
            landed(kv_far.at[z], kv_r.at[k])

        queries = q_all[z, h]
        own, far = kv_own[z, h, 0:T, :], kv_far[z, h, 0:T, :]
        s_own, s_far = dg(own, queries, 1, 1), dg(far, queries, 1, 1)
        peak = jnp.maximum(
            jnp.max(s_own, axis=0, keepdims=True), jnp.max(s_far, axis=0, keepdims=True)
        )
        e_own, e_far = jnp.exp(s_own - peak), jnp.exp(s_far - peak)
        total = jnp.sum(e_own, axis=0, keepdims=True) + jnp.sum(e_far, axis=0, keepdims=True)
        lse[z, h] = peak + jnp.log(total)
        scale = 1.0 / total
        mix = dg(own, (e_own * scale).astype(bf16), 0, 0)
        mix = mix + dg(far, (e_far * scale).astype(bf16), 0, 0)
        mix_t[h] = mix[HD:, :]

        if h == heads - 1:
            mixed[z] = stand(mix_t[...])

    def norm_one():
        for k in range(4):
            add_up(dg(mixed[planes[k]], weight(wm, planes[k], out_first, width), 1, 1), k == 0)
        for r, n in chunks:
            v = input_rows(r, n) + acc[r : r + n, :] + out_add()
            v = v - jnp.mean(v, axis=-1, keepdims=True)
            inverse = lax.rsqrt(jnp.mean(v * v, axis=-1, keepdims=True) + norm_eps)
            normed = v * inverse
            n_one[r : r + n, :] = normed
            r_one[r : r + n, :] = inverse
            hid_low[r : r + n, :] = (normed * gain_one() + shift_one()).astype(bf16)

    def rise(k):
        z = planes[k]
        ag_d(UP, k)
        for h in range(heads):
            cols = slice(256 * h, 256 * h + 256)
            u = jnp.dot(
                hid_low[...], weight(wu, z, 256 * h, 256 * h + 256), preferred_element_type=f32
            )
            u = u + bias[z, h : h + 1, 128:384]
            cumulative = 0.5 * (1.0 + lax.erf(u * 0.7071067811865476))
            act[z, 0:T, cols] = (u * cumulative).astype(bf16)
            bell = jnp.exp(-0.5 * u * u) * 0.3989422804014327
            slope[z, 0:T, cols] = (cumulative + u * bell).astype(bf16)

    def drop(k):
        ag_d(DOWN, k)
        add_up(dg(act[planes[k], 0:T, :], weight(wd, planes[k], 0, wide), 1, 1), k == 0)

    def norm_two():
        landed(cotx, move_r.at[1])
        sums = [jnp.zeros((1, width), f32) for _ in range(3)]
        for r, n in chunks:
            v = n_one[r : r + n, :] * gain_one() + shift_one() + acc[r : r + n, :] + down_add()
            v = v - jnp.mean(v, axis=-1, keepdims=True)
            inverse = lax.rsqrt(jnp.mean(v * v, axis=-1, keepdims=True) + norm_eps)
            normed = v * inverse
            stage_act[r : r + n, :] = normed * gain_two() + shift_two()
            up = cotx[r : r + n, :].astype(f32)
            scaled = up * gain_two()
            inner = jnp.mean(scaled * normed, axis=-1, keepdims=True)
            grad = inverse * (scaled - jnp.mean(scaled, axis=-1, keepdims=True) - normed * inner)
            acc[r : r + n, :] = grad
            low[r : r + n, :] = grad.astype(bf16)
            for i, term in enumerate((up * normed, up, grad)):
                sums[i] = sums[i] + jnp.sum(term, axis=0, keepdims=True)
        gvec[...] = jnp.zeros(gvec.shape, f32)
        gbias[...] = jnp.zeros(gbias.shape, f32)
        gvec[3:4, :], gvec[4:5, :], gvec[6:7, :] = sums

    pl.semaphore_wait(bar, len(others))
    for step, *given in (
        (ag_own, SMALL),
        (prep_mix,),
        (ag_own, MIX),
        (ag_a, MIX, 0),
        (ag_a, SMALL, 2),
        (prep_flags,),
        (prep_down,),
        (ag_a, SMALL, 0),
        (ag_a, SMALL, 1),
        (prep_up,),
        (ag_a, DOWN, 0),
        (ag_b, SMALL, 0),
        (ag_a, UP, 0),
        (ag_a, MIX, 1),
        (move_frames,),
        (ag_own, UP),
        (ag_a, SMALL, 3),
        (ag_a, MIX, 2),
        (ag_b, MIX, 0),
        (ag_b, SMALL, 1),
        (ag_a, MIX, 3),
        (ag_c, SMALL, 0),
        (ag_b, SMALL, 3),
        (ag_b, DOWN, 0),
        (ag_b, MIX, 2),
        (ag_c, MIX, 0),
        (ag_b, MIX, 1),
        (ag_b, UP, 0),
        (ag_b, SMALL, 2),
        (ag_a, UP, 1),
        (ag_own, DOWN),
        (ag_c, SMALL, 1),
        (ag_a, UP, 2),
        (ag_b, MIX, 3),
        (ag_c, DOWN, 0),
        (ag_c, SMALL, 3),
        (ag_c, SMALL, 2),
        (unpack,),
        (round_inputs,),
        (project, 0),
        (ag_a, UP, 3),
        (attend, 0, 0),
        (ag_c, MIX, 1),
        (ag_c, UP, 0),
        (ag_c, MIX, 2),
        (ag_b, UP, 2),
        (attend, 0, 1),
        (project, 1),
        (ag_c, MIX, 3),
        (ag_a, DOWN, 1),
        (ag_b, UP, 3),
        (move_cot,),
        (attend, 0, 2),
        (attend, 1, 0),
        (project, 3),
        (attend, 1, 1),
        (project, 2),
        (ag_a, DOWN, 2),
        (attend, 1, 2),
        (attend, 2, 0),
        (attend, 2, 1),
        (attend, 2, 2),
        (ag_a, DOWN, 3),
        (attend, 3, 0),
        (attend, 3, 1),
        (ag_c, UP, 3),
        (ag_b, UP, 1),
        (ag_b, DOWN, 1),
        (attend, 3, 2),
        (ag_c, UP, 2),
        (ag_b, DOWN, 2),
        (norm_one,),
        (ag_c, UP, 1),
        (ag_b, DOWN, 3),
        (rise, 2),
        (ag_c, DOWN, 1),
        (rise, 0),
        (drop, 0),
        (ag_c, DOWN, 2),
        (rise, 1),
        (drop, 1),
        (drop, 2),
        (ag_c, DOWN, 3),
        (rise, 3),
        (drop, 3),
        (norm_two,),
    ):
        step(*given)

    def tiled(value):
        return value.reshape(4, 2, -1, value.shape[1])

    def move_act():
        hand_over(2, stage_act, act_out)

    def gain_down(k):
        z = planes[k]
        gd[z] = tiled(dg(low[...], act[z, 0:T, :], 0, 0).astype(bf16))
        rs_0(DOWN, k)

    def fall(k):
        z = planes[k]
        grad = dg(low[...], weight(wd, z, 0, wide), 1, 0)
        grad = (grad * slope[z, 0:T, :].astype(f32)).astype(bf16)
        slope[z, 0:T, :] = grad
        total = jnp.sum(grad.astype(f32), axis=0, keepdims=True)
        for h in range(heads):
            gbias[z, h : h + 1, 128:384] = total[:, 256 * h : 256 * h + 256]

    def flow(k):
        z = planes[k]
        acc[...] = acc[...] + dg(slope[z, 0:T, :], weight(wu, z, 0, wide), 1, 1)

    def gain_up(k):
        sent(("ag", UP))
        z = planes[k]
        wu[z] = tiled(dg(hid_low[...], slope[z, 0:T, :], 0, 0).astype(bf16))
        rs_0(UP, k)

    def norm_back_one():
        sums = [jnp.zeros((1, width), f32) for _ in range(3)]
        for r, n in chunks:
            grad_in = acc[r : r + n, :]
            normed = n_one[r : r + n, :]
            scaled = grad_in * gain_one()
            inner = jnp.mean(scaled * normed, axis=-1, keepdims=True)
            grad = r_one[r : r + n, :] * (
                scaled - jnp.mean(scaled, axis=-1, keepdims=True) - normed * inner
            )
            acc[r : r + n, :] = grad
            low[r : r + n, :] = grad.astype(bf16)
            for i, term in enumerate((grad_in * normed, grad_in, grad)):
                sums[i] = sums[i] + jnp.sum(term, axis=0, keepdims=True)
        gvec[1:2, :], gvec[2:3, :], gvec[5:6, :] = sums

    def unmix():
        for z in planes:
            grad = dg(low[...], weight(wm, z, out_first, width), 1, 0).astype(bf16).astype(f32)
            for h in range(heads):
                if h % 2 == 0:
                    head = grad[:, HD * h : HD * h + 128]
                else:
                    piece = grad[:, HD * h + HD : HD * h + 2 * HD]
                    head = jnp.concatenate([piece, piece], axis=1)
                dm[z, h] = jnp.where(lane < HD, 0.0, head).astype(bf16)

    def attend_back(k, h):
        z = planes[k]

        queries, gm = q_all[z, h], dm[z, h]
        own, far = kv_own[z, h, 0:T, :], kv_far[z, h, 0:T, :]
        level = lse[z, h]
        p_own = jnp.exp(dg(own, queries, 1, 1) - level)
        p_far = jnp.exp(dg(far, queries, 1, 1) - level)
        g_own, g_far = dg(own, gm, 1, 1), dg(far, gm, 1, 1)
        inner = jnp.sum(p_own * g_own, axis=0, keepdims=True)
        inner = inner + jnp.sum(p_far * g_far, axis=0, keepdims=True)
        s_own = (p_own * (g_own - inner)).astype(bf16)
        s_far = (p_far * (g_far - inner)).astype(bf16)
        pair_far = jnp.dot(s_far, queries, preferred_element_type=f32)
        pair_far = pair_far + jnp.dot(p_far.astype(bf16), gm, preferred_element_type=f32)
        pair_own = jnp.dot(s_own, queries, preferred_element_type=f32)
        pair_own = pair_own + jnp.dot(p_own.astype(bf16), gm, preferred_element_type=f32)
        slope[z, 0:T, 128 * h : 128 * h + 128] = pair_far.astype(bf16)
        at = 128 * (heads + h)
        slope[z, 0:T, at : at + 128] = pair_own.astype(bf16)
        grad_q = dg(own, s_own, 0, 0) + dg(far, s_far, 0, 0)
        mix_t[h] = grad_q[0:HD, :] * HD ** (-0.5)

        if h < heads - 1:
            return
        act[z, 0:T, 0 : HD * heads] = mix_t[...].reshape(heads * HD, T).T.astype(bf16)
        send(
            "rs",
            slope.at[z, :, 0 : 128 * heads],
            far_pair.at[z],
            (kv_s, kv_r),
            (4 + k,),
            (dc, mp),
        )

    def project_back(k):
        sent(("ag", MIX))
        z = planes[k]
        landed(far_pair.at[z], kv_r.at[4 + k])
        pieces = []
        for h in range(heads):
            pieces.append(act[z, 0:T, HD * h : HD * h + HD].astype(f32))
            far = far_pair[z, 0:T, 128 * h : 128 * h + 128].astype(f32)
            at = 128 * (heads + h)
            pieces.append(far + slope[z, 0:T, at : at + 128].astype(f32))
        pieces.append(jnp.zeros((T, HD), f32))
        slab = jnp.concatenate(pieces, axis=1).astype(bf16)
        dproj[...] = slab
        total = jnp.sum(slab.astype(f32), axis=0, keepdims=True)
        for h in range(heads):
            gbias[z, h : h + 1, 0:128] = jnp.concatenate(
                [total[:, 192 * h : 192 * h + 64], total[:, 192 * h + 128 : 192 * h + 192]], axis=1
            )
        acc[...] = acc[...] + dg(dproj[...], weight(wm, z, 0, qkv_wide), 1, 1)
        grad_qkv = dg(x_low[...], dproj[...], 0, 0)
        grad_out = dg(low[...], mixed[z], 0, 0)
        wm[z, :, :, :, 0:out_first] = tiled(grad_qkv[:, 0:out_first].astype(bf16))
        both = grad_qkv[:, out_first:] + grad_out[:, 0:128]
        wm[z, :, :, :, out_first:qkv_wide] = tiled(both.astype(bf16))
        wm[z, :, :, :, qkv_wide:] = tiled(grad_out[:, 128:].astype(bf16))
        rs_0(MIX, k)

    def finish():
        embed_sum = jnp.zeros((1, width), f32)
        for r, n in chunks:
            hidden_rows = masked_rows(r, n)
            grad = acc[r : r + n, :]
            stage_fg[r : r + n, :] = jnp.where(hidden_rows, 0.0, grad)
            embed_sum = embed_sum + jnp.sum(
                jnp.where(hidden_rows, grad, 0.0), axis=0, keepdims=True
            )
        gvec[0:1, :] = embed_sum

        @pl.when(mover)
        def _():
            remote(cot_own, cotx, move_s.at[1], move_r.at[1], swap_with).wait_send()
            cot_own[0:T, :] = stage_fg[...].astype(bf16)
            remote(cot_own, fg_far, move_s.at[3], move_r.at[4], swap_with).start()

        @pl.when(stay)
        def _():
            pltpu.make_async_copy(stage_fg, fg_out, move_r.at[3]).start()

        gs[...] = jnp.zeros(gs.shape, f32)
        for d, (j, c) in enumerate(cells):
            vectors = gvec[:, vec_cut * d : vec_cut * (d + 1)]
            for z in range(4):
                gs[z, j, c, 0:4, 0:cut] = gbias[z, 0:4, cut * d : cut * (d + 1)]
                gs[z, j, c, 4:6, 0:vec_cut] = vectors[2 * z : 2 * z + 2, :]
        for k in (1, 2, 3, 0):
            rs_0(SMALL, k)

    def take_fg():
        @pl.when(mover)
        def _():
            landed(fg_far, move_r.at[4])
            stage_fg[...] = fg_far[0:T, :].astype(f32)
            pltpu.make_async_copy(stage_fg, fg_out, move_r.at[3]).start()

    for step, *given in (
        (move_act,),
        (gain_down, 3),
        (gain_down, 2),
        (fall, 2),
        (flow, 2),
        (rs_1, DOWN, 3),
        (gain_down, 1),
        (rs_1, DOWN, 2),
        (fall, 3),
        (flow, 3),
        (gain_up, 3),
        (fall, 0),
        (rs_1, DOWN, 1),
        (flow, 0),
        (fall, 1),
        (flow, 1),
        (gain_up, 1),
        (rs_2, DOWN, 2),
        (gain_down, 0),
        (rs_1, UP, 3),
        (norm_back_one,),
        (unmix,),
        (rs_1, UP, 1),
        (attend_back, 3, 0),
        (attend_back, 3, 1),
        (attend_back, 3, 2),
        (rs_3, DOWN, 2),
        (rs_2, DOWN, 3),
        (gain_up, 2),
        (rs_3, DOWN, 1),
        (project_back, 3),
        (rs_2, UP, 3),
        (attend_back, 1, 0),
        (attend_back, 1, 1),
        (rs_3, DOWN, 3),
        (rs_1, UP, 2),
        (rs_1, MIX, 3),
        (attend_back, 1, 2),
        (gain_up, 0),
        (rs_3, UP, 1),
        (attend_back, 2, 0),
        (rs_3, UP, 3),
        (project_back, 1),
        (rs_2, MIX, 3),
        (attend_back, 2, 1),
        (attend_back, 2, 2),
        (rs_1, MIX, 1),
        (rs_2, UP, 2),
        (rs_1, UP, 0),
        (project_back, 2),
        (rs_3, MIX, 3),
        (attend_back, 0, 0),
        (attend_back, 0, 1),
        (rs_1, MIX, 2),
        (rs_3, MIX, 1),
        (attend_back, 0, 2),
        (rs_1, DOWN, 0),
        (rs_3, UP, 2),
        (project_back, 0),
        (finish,),
        (rs_2, MIX, 2),
        (rs_1, SMALL, 1),
        (rs_1, SMALL, 3),
        (rs_1, SMALL, 0),
        (rs_1, SMALL, 2),
        (rs_1, MIX, 0),
        (rs_3, MIX, 2),
        (rs_2, SMALL, 3),
        (rs_2, SMALL, 1),
        (rs_2, SMALL, 2),
        (rs_2, UP, 0),
        (rs_2, DOWN, 0),
        (rs_2, MIX, 0),
        (rs_2, SMALL, 0),
        (rs_3, SMALL, 1),
        (rs_3, SMALL, 2),
        (rs_3, SMALL, 3),
        (rs_3, UP, 0),
        (rs_3, DOWN, 0),
        (rs_4, UP),
        (rs_4, DOWN),
        (rs_3, SMALL, 0),
        (take_fg,),
        (rs_3, MIX, 0),
        (rs_4, MIX),
        (rs_4, SMALL),
    ):
        step(*given)
    row_id = lax.broadcasted_iota(jnp.int32, (8, 128), 0)
    tiles[0] = jnp.where(row_id == 7, sum(squares), small_sum[...])
    for k in (1, 2, 3):
        send("end", tiles.at[0], tiles.at[k], (tile_s, tile_r), (k,), (dp, planes[k]))
    for k in (1, 2, 3):
        landed(tiles.at[k], tile_r.at[k])
    for k in range(4):
        vec_tiles[planes[k]] = tiles[k]
    tiles[4] = vec_tiles[0] + vec_tiles[1] + vec_tiles[2] + vec_tiles[3]
    for i, d in enumerate(group):
        send("end", tiles.at[4], tiles.at[5 + i], (tile_s, tile_r), (4 + i,), (d, mp))
    for i in range(7):
        landed(tiles.at[5 + i], tile_r.at[4 + i])
    pairs = [tiles[4] + tiles[5], tiles[6] + tiles[9], tiles[7] + tiles[10], tiles[8] + tiles[11]]
    norm_ref[...] = (pairs[0] + pairs[1]) + (pairs[2] + pairs[3])
    for tag in ("kv", "rs", "end", ("ag", SMALL), ("ag", DOWN)):
        sent(tag)
    landed(act_out, move_r.at[2])
    landed(fg_out, move_r.at[3])

    @pl.when(mover)
    def _():
        remote(fm_own, fmx, move_s.at[0], move_r.at[0], swap_with).wait_send()
        remote(stage_act, act_out, move_s.at[2], move_r.at[2], swap_with).wait_send()
        remote(cot_own, fg_far, move_s.at[3], move_r.at[4], swap_with).wait_send()


def run_layer(share, frames, mask, cot, qkv, out, up, down, biases, vectors):
    width = frames.shape[1]
    tall = share + -share % 16
    heads = biases.shape[0]
    rows = qkv.shape[0]
    wide = up.shape[1]
    columns = (128, width, wide, wide)
    types = (bf16,) * 4
    heights = (16, rows, rows, rows)
    weights = [
        pltpu.VMEM((4, 4, 2, n, c), t) for n, c, t in zip(heights, columns, types)
    ] + [pltpu.VMEM((4, 4, 2, 8, 128), f32), pltpu.VMEM((4, 4, 2, rows, wide), bf16)]
    pieces = list(zip((8, rows, rows, rows), columns, (f32, bf16, bf16, bf16)))
    arrivals = [
        pltpu.VMEM((*lead, n, c), t)
        for lead in ((4, 4), (4,), (4,), (4,), (3,))
        for n, c, t in pieces
    ]
    activations = [
        pltpu.VMEM((tall, width + 128), bf16),
        pltpu.VMEM((tall, width), bf16),
        pltpu.VMEM((tall, width + 128), bf16),
        pltpu.VMEM((tall, width), bf16),
        pltpu.VMEM((share, width), bf16),
        pltpu.VMEM((4, heads, share, 128), bf16),
        pltpu.VMEM((4, heads, tall, 128), bf16),
        pltpu.VMEM((4, heads, tall, 128), bf16),
        pltpu.VMEM((4, share, heads * HD + HD), bf16),
        pltpu.VMEM((4, heads, 1, share), f32),
        pltpu.VMEM((heads, HD, share), f32),
        pltpu.VMEM((share, width), f32),
        pltpu.VMEM((share, 1), f32),
        pltpu.VMEM((share, width), bf16),
        pltpu.VMEM((4, tall, wide), bf16),
        pltpu.VMEM((4, tall, wide), bf16),
        pltpu.VMEM((share, width), f32),
        pltpu.VMEM((share, width), bf16),
        pltpu.VMEM((4, heads, share, 128), bf16),
        pltpu.VMEM((share, qkv.shape[1] + HD), bf16),
        pltpu.VMEM((4, tall, 128 * heads), bf16),
        pltpu.VMEM((share, width), bf16),
        pltpu.VMEM((share, width), bf16),
        pltpu.VMEM((rows, wide), f32),
        pltpu.VMEM((rows, wide), f32),
        pltpu.VMEM((16, 128), f32),
        pltpu.VMEM((share, width), f32),
        pltpu.VMEM((share, width), f32),
        pltpu.VMEM((tall, width), bf16),
        pltpu.VMEM((8, width), f32),
        pltpu.VMEM((4, 8, 384), f32),
        pltpu.VMEM((8, width), f32),
        pltpu.VMEM((4, 8, 384), f32),
        pltpu.VMEM((12, 8, 128), f32),
    ]
    semaphores = [pltpu.SemaphoreType.DMA((4, SEMS)) for _ in range(4)] + [
        pltpu.SemaphoreType.DMA((n,)) for n in (8, 8, 5, 5, 12, 12, 4)
    ]
    anywhere = pl.BlockSpec(memory_space=pl.ANY)
    vmem = pl.BlockSpec(memory_space=pltpu.VMEM)
    shapes = [
        (share, width),
        (share, width),
        (8, 128),
        (rows, width),
        (rows, wide),
        (rows, wide),
        (8, 128),
        (4, 8, 128),
    ]
    return pl.pallas_call(
        functools.partial(layer_kernel, share),
        out_shape=tuple(jax.ShapeDtypeStruct(s, f32) for s in shapes),
        in_specs=[anywhere, vmem, anywhere, vmem, vmem, anywhere, anywhere, vmem, vmem],
        out_specs=(anywhere,) * 2 + (vmem,) * 6,
        scratch_shapes=weights + arrivals + activations + semaphores,
        compiler_params=pltpu.CompilerParams(
            collective_id=0, has_side_effects=True, vmem_limit_bytes=60 * 2**20
        ),
        name="encoder_layer",
    )(frames, mask, cot, qkv, out, up, down, biases, vectors)


def update_kernel(*refs):
    given, made = refs[:26], refs[26:47]
    held, ready = refs[47:73], refs[73:92]
    come, leave = refs[92:]
    arriving = [
        pltpu.make_async_copy(src, dst, come.at[i]) for i, (src, dst) in enumerate(zip(given, held))
    ]
    for copy in arriving:
        copy.start()
    leaving = []

    def out(src, i):
        copy = pltpu.make_async_copy(src, made[i], leave.at[i])
        copy.start()
        leaving.append(copy)

    for copy in arriving[:6]:
        copy.wait()
    small, mix, up, down, norm, vec_tiles = held[:6]
    state = held[8:]
    grad_norm = jnp.sqrt(norm[7:8, 0:1])
    ready[0][...] = grad_norm
    out(ready[0], 0)
    factor = jnp.minimum(1.0, clip_limit / (grad_norm + 1e-06))
    qkv_columns = state[0].shape[1]
    first = mix.shape[1] - state[3].shape[0] - HD
    heads, cut = state[12].shape
    vec_rows, vec_cut = state[15].shape
    gradients = (
        lambda: mix[:, 0:qkv_columns],
        lambda: mix[:, first:].T[HD:, :],
        lambda: up[...],
        lambda: down[...],
        lambda: small[0:heads, 0:cut],
        lambda: jnp.concatenate([vec_tiles[z, 4:6, 0:vec_cut] for z in range(4)], axis=0)[0:vec_rows, :],
    )
    for i in (2, 3, 0, 1, 4, 5):
        old = state[3 * i : 3 * i + 3]
        for copy in arriving[8 + 3 * i : 11 + 3 * i]:
            copy.wait()
        values = adam_step(*(ref[...] for ref in old), gradients[i](), factor, *settings[i])
        for at, value in enumerate(values):
            ready[1 + 3 * i + at][...] = value
            out(ready[1 + 3 * i + at], 3 + 3 * i + at)
    for at in range(2):
        arriving[6 + at].wait()
        out(held[6 + at], 1 + at)
    for copy in leaving:
        copy.wait()


def run_update(sums, norm, vec_tiles, act, fg, state):
    anywhere = pl.BlockSpec(memory_space=pl.ANY)
    given = (*sums, norm, vec_tiles, act, fg, *state)
    shapes = [(1, 1), act.shape, fg.shape] + [a.shape for a in state]
    return pl.pallas_call(
        update_kernel,
        out_shape=tuple(jax.ShapeDtypeStruct(s, f32) for s in shapes),
        in_specs=[anywhere] * len(given),
        out_specs=(anywhere,) * len(shapes),
        scratch_shapes=[pltpu.VMEM(a.shape, f32) for a in given]
        + [pltpu.VMEM(s, f32) for s in shapes[:1] + shapes[3:]]
        + [pltpu.SemaphoreType.DMA((len(given),)), pltpu.SemaphoreType.DMA((len(shapes),))],
        compiler_params=pltpu.CompilerParams(vmem_limit_bytes=60 * 2**20),
        name="update_weights",
    )(*given)


def on_device_fast(
    frames,
    span_mask,
    cotangent,
    qkv_weight,
    qkv_mean,
    qkv_square,
    out_weight,
    out_mean,
    out_square,
    up_weight,
    up_mean,
    up_square,
    down_weight,
    down_mean,
    down_square,
    head_biases,
    bias_mean,
    bias_square,
    norm_vectors,
    vector_mean,
    vector_square,
):
    share = frames.shape[0]
    act, fg, *sums, norm, vec_tiles = run_layer(
        share,
        frames,
        span_mask,
        cotangent,
        qkv_weight,
        out_weight,
        up_weight,
        down_weight.T,
        head_biases,
        norm_vectors,
    )
    down = (down_weight.T, down_mean.T, down_square.T)
    state = (qkv_weight, qkv_mean, qkv_square, out_weight, out_mean, out_square)
    state += (up_weight, up_mean, up_square, *down, head_biases, bias_mean, bias_square)
    state += (norm_vectors, vector_mean, vector_square)
    grad_norm, outputs, frame_grad, *updated = run_update(sums, norm, vec_tiles, act, fg, state)
    updated[9:12] = [value.T for value in updated[9:12]]
    return (outputs, frame_grad, grad_norm.reshape(()), *updated)


def solution(mesh):
    return jax.shard_map(
        on_device_fast if fast_fits(mesh) else on_device,
        mesh=mesh,
        in_specs=(
            P(("dp", "mp"), None),
            P("dp", None),
            P(("dp", "mp"), None),
            P("dp", "mp"),
            P("dp", "mp"),
            P("dp", "mp"),
            P("mp", "dp"),
            P("mp", "dp"),
            P("mp", "dp"),
            P("dp", "mp"),
            P("dp", "mp"),
            P("dp", "mp"),
            P("mp", "dp"),
            P("mp", "dp"),
            P("mp", "dp"),
            P("mp", "dp"),
            P("mp", "dp"),
            P("mp", "dp"),
            P(None, "dp"),
            P(None, "dp"),
            P(None, "dp"),
        ),
        out_specs=(
            P(("dp", "mp"), None),
            P(("dp", "mp"), None),
            P(),
            P("dp", "mp"),
            P("dp", "mp"),
            P("dp", "mp"),
            P("mp", "dp"),
            P("mp", "dp"),
            P("mp", "dp"),
            P("dp", "mp"),
            P("dp", "mp"),
            P("dp", "mp"),
            P("mp", "dp"),
            P("mp", "dp"),
            P("mp", "dp"),
            P("mp", "dp"),
            P("mp", "dp"),
            P("mp", "dp"),
            P(None, "dp"),
            P(None, "dp"),
            P(None, "dp"),
        ),
        check_vma=False,
    )
```

```python
import functools

import jax
import jax.numpy as jnp
from jax import lax
from jax.experimental import pallas as pl
from jax.experimental.pallas import tpu as pltpu
from jax.sharding import PartitionSpec as P

HD = 64
LEN = 688


norm_eps = 1e-05
adam_eps = 1e-08
beta_one = 0.9
beta_two = 0.999
step_count = 10.0
clip_limit = 1.0
settings = ((0.05, 0.1), (0.3, 0.1), (0.05, 0.1), (0.03, 0.1), (0.3, 0.0), (0.4, 0.0))


def norm_rows(values, norm_gain, norm_shift):
    centred = values - jnp.mean(values, axis=-1, keepdims=True)
    variance = jnp.mean(centred * centred, axis=-1, keepdims=True)
    inverse = lax.rsqrt(variance + norm_eps)
    normed = centred * inverse
    return (normed * norm_gain + norm_shift, normed, inverse)


def norm_back(upstream, normed, inverse, norm_gain):
    scaled = upstream * norm_gain
    inner_part = (
        scaled
        - jnp.mean(scaled, axis=-1, keepdims=True)
        - normed * jnp.mean(scaled * normed, axis=-1, keepdims=True)
    )
    return (inverse * inner_part, jnp.sum(upstream * normed, axis=0), jnp.sum(upstream, axis=0))


def gelu_slope(pre_act):
    cumulative = 0.5 * (1.0 + jax.scipy.special.erf(pre_act * 0.7071067811865476))
    return cumulative + pre_act * jnp.exp(-0.5 * pre_act * pre_act) * 0.3989422804014327


def attend_forward(clip_block):
    scaling = HD ** (-0.5)
    queries = clip_block[:, :, 0]
    key_rows = clip_block[:, :, 1]
    value_rows = clip_block[:, :, 2]
    scores = (
        jnp.einsum("qhe,khe->hqk", queries, key_rows, preferred_element_type=jnp.float32) * scaling
    )
    row_peak = jnp.max(scores, axis=-1, keepdims=True)
    log_total = row_peak + jnp.log(jnp.sum(jnp.exp(scores - row_peak), axis=-1, keepdims=True))
    attention = jnp.exp(scores - log_total).astype(jnp.bfloat16)
    mixed_rows = jnp.einsum(
        "hqk,khe->qhe", attention, value_rows, preferred_element_type=jnp.float32
    )
    return (mixed_rows.astype(jnp.bfloat16).reshape(clip_block.shape[0], -1), log_total)


def attend_backward(pieces):
    clip_block, log_total, grad_mixed = pieces
    scaling = HD ** (-0.5)
    queries = clip_block[:, :, 0]
    key_rows = clip_block[:, :, 1]
    value_rows = clip_block[:, :, 2]
    scores = (
        jnp.einsum("qhe,khe->hqk", queries, key_rows, preferred_element_type=jnp.float32) * scaling
    )
    attention = jnp.exp(scores - log_total)
    attention_low = attention.astype(jnp.bfloat16)
    mixed_rows = jnp.einsum(
        "hqk,khe->qhe", attention_low, value_rows, preferred_element_type=jnp.float32
    ).astype(jnp.bfloat16)
    grad_rows = grad_mixed.reshape(queries.shape)
    grad_attention = jnp.einsum(
        "qhe,khe->hqk", grad_rows, value_rows, preferred_element_type=jnp.float32
    )
    grad_values = jnp.einsum(
        "hqk,qhe->khe", attention_low, grad_rows, preferred_element_type=jnp.float32
    )
    row_inner = jnp.sum(attention * grad_attention, axis=-1, keepdims=True)
    grad_scores = (attention * (grad_attention - row_inner)).astype(jnp.bfloat16)
    grad_queries = (
        jnp.einsum("hqk,khe->qhe", grad_scores, key_rows, preferred_element_type=jnp.float32)
        * scaling
    )
    grad_keys = (
        jnp.einsum("hqk,qhe->khe", grad_scores, queries, preferred_element_type=jnp.float32)
        * scaling
    )
    grad_block = jnp.stack([grad_queries, grad_keys, grad_values], axis=2).astype(jnp.bfloat16)
    return (
        mixed_rows.reshape(clip_block.shape[0], -1),
        grad_block.reshape(clip_block.shape[0], -1),
    )


def adam_step(weight, mean_old, square_old, gradient, factor, rate, decay):
    clipped = gradient * factor
    mean_new = beta_one * mean_old + (1.0 - beta_one) * clipped
    square_new = beta_two * square_old + (1.0 - beta_two) * clipped * clipped
    mean_hat = mean_new / (1.0 - beta_one**step_count)
    square_hat = square_new / (1.0 - beta_two**step_count)
    weight_new = weight - rate * (mean_hat / (jnp.sqrt(square_hat) + adam_eps) + decay * weight)
    return (weight_new, mean_new, square_new)


def on_device(
    frames,
    span_mask,
    cotangent,
    qkv_weight,
    qkv_mean,
    qkv_square,
    out_weight,
    out_mean,
    out_square,
    up_weight,
    up_mean,
    up_square,
    down_weight,
    down_mean,
    down_square,
    head_biases,
    bias_mean,
    bias_square,
    norm_vectors,
    vector_mean,
    vector_square,
):
    masters = (qkv_weight, out_weight, up_weight, down_weight, head_biases, norm_vectors)
    lowered = tuple((weight.astype(jnp.bfloat16) for weight in masters))
    qkv_full, out_full, up_full, down_full, bias_full, vector_full = (
        lax.all_gather(lowered[0], "dp", axis=0, tiled=True),
        lax.all_gather(lowered[1], "dp", axis=1, tiled=True),
        lax.all_gather(lowered[2], "dp", axis=0, tiled=True),
        lax.all_gather(lowered[3], "dp", axis=1, tiled=True),
        lax.all_gather(lowered[4], "dp", axis=1, tiled=True),
        lax.all_gather(lowered[5], "dp", axis=1, tiled=True),
    )
    share_rows = frames.shape[0]
    start_row = lax.axis_index("mp") * share_rows
    vectors = vector_full.astype(jnp.float32)
    local_heads = bias_full.shape[0]

    def share_of(array_full):
        return lax.dynamic_slice_in_dim(array_full, start_row, share_rows, 0)

    gathered = lax.all_gather(frames, "mp", axis=0, tiled=True)
    all_rows = gathered.shape[0]
    masked = span_mask.reshape(all_rows, 1) == 1
    inputs = jnp.where(masked, vectors[0], gathered.astype(jnp.float32))
    rounded = inputs.astype(jnp.bfloat16)
    zero_bias = jnp.zeros_like(bias_full[:, :HD])
    qkv_bias = (
        jnp.stack([bias_full[:, :HD], zero_bias, bias_full[:, HD : 2 * HD]], axis=1)
        .reshape(-1)
        .astype(jnp.float32)
    )
    up_bias = bias_full[:, 2 * HD :].reshape(-1).astype(jnp.float32)
    projected = (jnp.dot(rounded, qkv_full, preferred_element_type=jnp.float32) + qkv_bias).astype(
        jnp.bfloat16
    )
    blocks = projected.reshape(-1, LEN, local_heads, 3, HD)
    mixed_rows, log_total = lax.map(attend_forward, blocks)
    mixed_rows = mixed_rows.reshape(all_rows, -1)
    attn_part = jnp.dot(mixed_rows, out_full, preferred_element_type=jnp.float32)
    attended = lax.psum(attn_part, "mp")
    first_sum = inputs + attended + vectors[5]
    hidden, normed_full, inverse_full = norm_rows(first_sum, vectors[1], vectors[2])
    normed_one = share_of(normed_full)
    inverse_one = share_of(inverse_full)
    hidden_low = hidden.astype(jnp.bfloat16)
    pre_act = jnp.dot(hidden_low, up_full, preferred_element_type=jnp.float32) + up_bias
    activated = jax.nn.gelu(pre_act, approximate=False).astype(jnp.bfloat16)
    ffn_part = jnp.dot(activated, down_full, preferred_element_type=jnp.float32)
    second_sum = hidden + lax.psum(ffn_part, "mp") + vectors[6]
    outputs_full, normed_full, inverse_full = norm_rows(second_sum, vectors[3], vectors[4])
    outputs = share_of(outputs_full)
    normed_two = share_of(normed_full)
    inverse_two = share_of(inverse_full)
    qkv_full, out_full, up_full, down_full, bias_full, vector_full = (
        lax.all_gather(lowered[0], "dp", axis=0, tiled=True),
        lax.all_gather(lowered[1], "dp", axis=1, tiled=True),
        lax.all_gather(lowered[2], "dp", axis=0, tiled=True),
        lax.all_gather(lowered[3], "dp", axis=1, tiled=True),
        lax.all_gather(lowered[4], "dp", axis=1, tiled=True),
        lax.all_gather(lowered[5], "dp", axis=1, tiled=True),
    )
    upstream = cotangent.astype(jnp.float32)
    grad_two, grad_gain_two, grad_shift_two = norm_back(
        upstream, normed_two, inverse_two, vectors[3]
    )
    grad_down_bias = jnp.sum(grad_two, axis=0)
    grad_two_full = lax.all_gather(grad_two.astype(jnp.bfloat16), "mp", axis=0, tiled=True)
    pre_again = jnp.dot(hidden_low, up_full, preferred_element_type=jnp.float32) + up_bias
    act_again = jax.nn.gelu(pre_again, approximate=False).astype(jnp.bfloat16)
    grad_down = jnp.einsum(
        "tf,td->fd", act_again, grad_two_full, preferred_element_type=jnp.float32
    )
    grad_act = jnp.einsum("td,fd->tf", grad_two_full, down_full, preferred_element_type=jnp.float32)
    grad_pre = (grad_act * gelu_slope(pre_again)).astype(jnp.bfloat16)
    grad_up = jnp.einsum("td,tf->df", hidden_low, grad_pre, preferred_element_type=jnp.float32)
    grad_up_bias = jnp.sum(grad_pre, axis=0, dtype=jnp.float32)
    hidden_part = jnp.einsum("tf,df->td", grad_pre, up_full, preferred_element_type=jnp.float32)
    grad_hidden = grad_two + lax.psum_scatter(hidden_part, "mp", scatter_dimension=0, tiled=True)
    grad_one, grad_gain_one, grad_shift_one = norm_back(
        grad_hidden, normed_one, inverse_one, vectors[1]
    )
    grad_out_bias = jnp.sum(grad_one, axis=0)
    grad_one_full = lax.all_gather(grad_one.astype(jnp.bfloat16), "mp", axis=0, tiled=True)
    grad_mixed = jnp.einsum(
        "td,cd->tc", grad_one_full, out_full, preferred_element_type=jnp.float32
    ).astype(jnp.bfloat16)
    mixed_again, grad_blocks = lax.map(
        attend_backward, (blocks, log_total, grad_mixed.reshape(-1, LEN, grad_mixed.shape[1]))
    )
    mixed_again = mixed_again.reshape(all_rows, -1)
    grad_blocks = grad_blocks.reshape(all_rows, -1)
    grad_out = jnp.einsum(
        "tc,td->cd", mixed_again, grad_one_full, preferred_element_type=jnp.float32
    )
    grad_qkv = jnp.einsum("td,tc->dc", rounded, grad_blocks, preferred_element_type=jnp.float32)
    bias_sums = jnp.sum(grad_blocks, axis=0, dtype=jnp.float32).reshape(local_heads, 3, HD)
    grad_biases = jnp.concatenate(
        [bias_sums[:, 0], bias_sums[:, 2], grad_up_bias.reshape(local_heads, -1)], axis=1
    )
    input_part = jnp.einsum("tc,dc->td", grad_blocks, qkv_full, preferred_element_type=jnp.float32)
    grad_inputs = grad_one + lax.psum_scatter(
        input_part.astype(jnp.bfloat16), "mp", scatter_dimension=0, tiled=True
    ).astype(jnp.float32)
    masked_share = share_of(masked)
    grad_embed = jnp.sum(jnp.where(masked_share, grad_inputs, 0.0), axis=0)
    frame_grad = jnp.where(masked_share, 0.0, grad_inputs)
    grad_vectors = jnp.stack(
        [
            grad_embed,
            grad_gain_one,
            grad_shift_one,
            grad_gain_two,
            grad_shift_two,
            grad_out_bias,
            grad_down_bias,
        ]
    )
    reduced = (
        lax.psum_scatter(grad_qkv, "dp", scatter_dimension=0, tiled=True),
        lax.psum_scatter(grad_out, "dp", scatter_dimension=1, tiled=True),
        lax.psum_scatter(grad_up, "dp", scatter_dimension=0, tiled=True),
        lax.psum_scatter(grad_down, "dp", scatter_dimension=1, tiled=True),
        lax.psum_scatter(grad_biases, "dp", scatter_dimension=1, tiled=True),
    )
    local_squares = jnp.float32(0.0)
    for portion in reduced:
        local_squares = local_squares + jnp.sum(portion * portion)
    total_squares, vector_total = lax.psum((local_squares, grad_vectors), ("dp", "mp"))
    grad_norm = jnp.sqrt(total_squares + jnp.sum(vector_total * vector_total))
    column_count = norm_vectors.shape[1]
    vector_grad = lax.dynamic_slice_in_dim(
        vector_total, lax.axis_index("dp") * column_count, column_count, 1
    )
    factor = jnp.minimum(1.0, clip_limit / (grad_norm + 1e-06))
    gradients = (reduced[0], reduced[1], reduced[2], reduced[3], reduced[4], vector_grad)
    means = (qkv_mean, out_mean, up_mean, down_mean, bias_mean, vector_mean)
    squares = (qkv_square, out_square, up_square, down_square, bias_square, vector_square)
    updated = []
    for index_at in range(6):
        updated.extend(
            adam_step(
                masters[index_at],
                means[index_at],
                squares[index_at],
                gradients[index_at],
                factor,
                settings[index_at][0],
                settings[index_at][1],
            )
        )
    return (
        outputs,
        frame_grad,
        grad_norm,
        updated[0],
        updated[1],
        updated[2],
        updated[3],
        updated[4],
        updated[5],
        updated[6],
        updated[7],
        updated[8],
        updated[9],
        updated[10],
        updated[11],
        updated[12],
        updated[13],
        updated[14],
        updated[15],
        updated[16],
        updated[17],
    )


MESH = pl.DeviceIdType.MESH
SMALL, MIX, UP, DOWN = range(4)
SEMS = 32
f32, bf16 = jnp.float32, jnp.bfloat16


def fast_fits(mesh):
    return mesh.shape["dp"] == 8 and mesh.shape["mp"] == 4


def flip(dp, bit):
    held = lax.rem(lax.div(dp, bit), 2)
    return dp + bit - 2 * bit * held


def dg(a, b, ca, cb):
    return lax.dot_general(a, b, (((ca,), (cb,)), ((), ())), preferred_element_type=f32)


def landed(dst, sem):
    pltpu.make_async_copy(dst, dst, sem).wait()


def layer_kernel(
    share,
    frames_in,
    mask_in,
    cot_in,
    qkv_in,
    out_in,
    up_in,
    down_in,
    bias_in,
    vec_in,
    act_out,
    fg_out,
    small_sum,
    mix_sum,
    up_sum,
    down_sum,
    norm_ref,
    vec_tiles,
    ws,
    wm,
    wu,
    wd,
    gs,
    gd,
    rcs,
    rcm,
    rcu,
    rcd,
    rds,
    rdm,
    rdu,
    rdd,
    rxs,
    rxm,
    rxu,
    rxd,
    rys,
    rym,
    ryu,
    ryd,
    rzs,
    rzm,
    rzu,
    rzd,
    fm_own,
    cot_own,
    fmx,
    cotx,
    x_low,
    q_all,
    kv_own,
    kv_far,
    mixed,
    lse,
    mix_t,
    n_one,
    r_one,
    hid_low,
    act,
    slope,
    acc,
    low,
    dm,
    dproj,
    far_pair,
    frames_at,
    cot_at,
    up_at,
    down_at,
    small_at,
    stage_act,
    stage_fg,
    fg_far,
    vec,
    bias,
    gvec,
    gbias,
    tiles,
    gather_s,
    gather_r,
    reduce_s,
    reduce_r,
    kv_s,
    kv_r,
    move_s,
    move_r,
    tile_s,
    tile_r,
    load_s,
):
    T = share
    dp, mp = lax.axis_index("dp"), lax.axis_index("mp")
    core = lax.rem(dp, 2)
    dx, dy, dc = flip(dp, 2), flip(dp, 4), flip(dp, 1)
    dd = flip(dx, 4)
    planes = (mp, flip(mp, 1), flip(mp, 2), flip(flip(mp, 1), 2))
    mover = lax.rem(core + mp, 2) == 1
    stay = lax.rem(core + mp, 2) == 0
    swap_with = (dc, planes[1])
    full = (ws, wm, wu, wd)
    local = (gs, wm, wu, gd)
    from_core = (rcs, rcm, rcu, rcd)
    from_diag = (rds, rdm, rdu, rdd)
    from_x = (rxs, rxm, rxu, rxd)
    from_y = (rys, rym, ryu, ryd)
    from_z = (rzs, rzm, rzu, rzd)
    result = (small_sum, mix_sum, up_sum, down_sum)
    heads = q_all.shape[1]
    chunks = [(r, min(88, T - r)) for r in range(0, T, 88)]

    def remote(src, dst, send_sem, recv_sem, device):
        return pltpu.make_async_remote_copy(
            src_ref=src,
            dst_ref=dst,
            send_sem=send_sem,
            recv_sem=recv_sem,
            device_id=device,
            device_id_type=MESH,
        )

    pending = {}

    def send(tag, src, dst, sems, at, device):
        copy = remote(src, dst, sems[0].at[at], sems[1].at[at], device)
        copy.start()
        pending.setdefault(tag, []).append(copy)

    def sent(tag):
        for copy in pending.pop(tag, []):
            copy.wait_send()

    def hand_over(slot, src, dst):
        @pl.when(mover)
        def _():
            remote(src, dst, move_s.at[slot], move_r.at[slot], swap_with).start()

        @pl.when(stay)
        def _():
            pltpu.make_async_copy(src, dst, move_r.at[slot]).start()

    def halves(ref):
        n = ref.shape[-2] // 2
        return ref.at[pl.ds(0, n)], ref.at[pl.ds(n, n)]

    gather = (gather_s, gather_r)

    def slot(w, k, d):
        return full[w].at[planes[k], lax.div(d, 2), lax.rem(d, 2)]

    def ag_own(w):
        for k in (1, 2, 3):
            send(("ag", w), slot(w, 0, dp), slot(w, 0, dp), gather, (w, k), (dp, planes[k]))

    def ag_a(w, k):
        ref = slot(w, k, dp)
        if k:
            landed(ref, gather_r.at[w, k])
        send(("ag", w), ref, ref, gather, (w, 4 + k), (dx, mp))
        send(("ag", w), ref, ref, gather, (w, 8 + k), (dy, mp))

    own_j, x_j, y_j, d_j = (lax.div(d, 2) for d in (dp, dx, dy, dd))
    row_j = 2 * lax.div(own_j, 2)

    def to_core(w, k, cells, at):
        ref = full[w].at[planes[k], cells, core]
        send(("ag", w), ref, ref, gather, (w, at), (dc, mp))

    def ag_b(w, k):
        at_x, at_y = slot(w, k, dx), slot(w, k, dy)
        landed(at_x, gather_r.at[w, 4 + k])
        if k == 2 or (w == SMALL and k == 0):
            send(("ag", w), at_x, at_x, gather, (w, 12 + k), (dy, mp))
        elif k == 0:
            ref = halves(at_x)[0]
            send(("ag", w), ref, ref, gather, (w, 12), (dy, mp))
        if w == DOWN:
            to_core(w, k, pl.ds(row_j, 2), 17 + k)
        landed(at_y, gather_r.at[w, 8 + k])
        if k == 3 or (w == SMALL and k == 1):
            send(("ag", w), at_y, at_y, gather, (w, 12 + k), (dx, mp))
        elif k == 0 and w != SMALL:
            ref = halves(at_y)[1]
            send(("ag", w), ref, ref, gather, (w, 13), (dx, mp))
        if w == DOWN:
            to_core(w, k, y_j, 21 + k)

    def ag_c(w, k):
        ref = slot(w, k, dd)
        if w == SMALL or k > 1:
            landed(ref, gather_r.at[w, 12 + k])
        elif k == 0:
            for i, half in enumerate(halves(ref)):
                landed(half, gather_r.at[w, 12 + i])
            send(("ag", w), ref, ref, gather, (w, 16), (dp, planes[1]))
        else:
            landed(ref, gather_r.at[w, 16])
        if w == DOWN:
            to_core(w, k, d_j, 25 + k)
        else:
            to_core(w, k, slice(None), 17 + k)

    def ag_d(w, k):
        if w == DOWN:
            for cells, at in ((pl.ds(row_j, 2), 17), (y_j, 21), (d_j, 25)):
                landed(full[w].at[planes[k], cells, 1 - core], gather_r.at[w, at + k])
        else:
            landed(full[w].at[planes[k], :, 1 - core], gather_r.at[w, 17 + k])

    squares = []
    reduce = (reduce_s, reduce_r)

    def part(w, k, d):
        return local[w].at[planes[k], lax.div(d, 2), lax.rem(d, 2)]

    def add_to(ref, arrived):
        ref[...] = ref[...] + arrived[...]

    def rs_0(w, k):
        send("rs", local[w].at[planes[k], :, 1 - core], from_core[w].at[k], reduce, (w, k), (dc, mp))

    def rs_1(w, k):
        landed(from_core[w].at[k], reduce_r.at[w, k])
        add_to(local[w].at[planes[k], :, core], from_core[w].at[k])
        at_d, at_x, at_y = part(w, k, dd), part(w, k, dx), part(w, k, dy)
        to_d, to_x, to_y = from_diag[w].at[k], from_x[w].at[k], from_y[w].at[k]
        if w == SMALL or k > 1:
            if k % 2:
                send("rs", at_d, to_d, reduce, (w, 4 + k), (dx, mp))
                send("rs", at_x, to_x, reduce, (w, 10 + k), (dx, mp))
            else:
                send("rs", at_d, to_d, reduce, (w, 4 + k), (dy, mp))
                send("rs", at_y, to_y, reduce, (w, 15 + k), (dy, mp))
        elif k == 1:
            send("rs", at_d, to_d, reduce, (w, 4), (dp, planes[1]))
            send("rs", at_x, to_x, reduce, (w, 10 + k), (dx, mp))
            send("rs", at_y, to_y, reduce, (w, 15 + k), (dy, mp))
        else:
            landed(from_diag[w].at[1], reduce_r.at[w, 4])
            add_to(at_d, from_diag[w].at[1])
            send("rs", halves(at_d)[0], halves(to_d)[0], reduce, (w, 8), (dx, mp))
            send("rs", halves(at_d)[1], halves(to_d)[1], reduce, (w, 9), (dy, mp))
            send("rs", halves(at_x)[0], halves(to_x)[0], reduce, (w, 10), (dx, mp))
            send("rs", halves(at_y)[1], halves(to_y)[1], reduce, (w, 15), (dy, mp))

    def rs_2(w, k):
        at_x, at_y = part(w, k, dx), part(w, k, dy)
        come, to_x, to_y = from_diag[w].at[k], from_x[w].at[k], from_y[w].at[k]
        if w == SMALL or k > 1:
            landed(come, reduce_r.at[w, 4 + k])
            if k % 2:
                add_to(at_y, come)
                send("rs", at_y, to_y, reduce, (w, 15 + k), (dy, mp))
            else:
                add_to(at_x, come)
                send("rs", at_x, to_x, reduce, (w, 10 + k), (dx, mp))
        else:
            first, second = halves(come)
            landed(first, reduce_r.at[w, 8])
            add_to(halves(at_y)[0], first)
            send("rs", halves(at_y)[0], halves(to_y)[0], reduce, (w, 19), (dy, mp))
            landed(second, reduce_r.at[w, 9])
            add_to(halves(at_x)[1], second)
            send("rs", halves(at_x)[1], halves(to_x)[1], reduce, (w, 14), (dx, mp))

    def rs_3(w, k):
        if w == SMALL or k:
            landed(from_x[w].at[k], reduce_r.at[w, 10 + k])
            landed(from_y[w].at[k], reduce_r.at[w, 15 + k])
        else:
            for half, at in zip(halves(from_x[w].at[0]), (10, 14)):
                landed(half, reduce_r.at[w, at])
            for half, at in zip(halves(from_y[w].at[0]), (19, 15)):
                landed(half, reduce_r.at[w, at])
        ref = part(w, k, dp)
        total = ref[...].astype(f32) + from_x[w][k].astype(f32) + from_y[w][k].astype(f32)
        if k:
            ref[...] = total.astype(ref.dtype)
            send("rs", ref, from_z[w].at[k - 1], reduce, (w, 19 + k), (dp, planes[k]))
        else:
            result[w][...] = total

    def rs_4(w):
        total = result[w][...]
        for k in (1, 2, 3):
            landed(from_z[w].at[k - 1], reduce_r.at[w, 19 + k])
            total = total + from_z[w][k - 1].astype(f32)
        result[w][...] = total
        squares.append(jnp.sum(total * total))

    loads = [
        pltpu.make_async_copy(src, dst, load_s.at[i])
        for i, (src, dst) in enumerate(
            ((up_in, up_at), (frames_in, frames_at), (down_in, down_at), (cot_in, cot_at))
        )
    ]
    for copy in loads:
        copy.start()
    cut, vec_cut = bias_in.shape[1], vec_in.shape[1]
    width, wide = frames_in.shape[1], up_in.shape[1]
    qkv_wide = 192 * heads + 64
    out_first = 192 * heads - 64
    lane = lax.broadcasted_iota(jnp.int32, (1, 128), 1)
    cells = [(j, c) for j in range(4) for c in range(2)]
    group = [dc, dx, dy, dd, flip(dx, 1), flip(dy, 1), flip(dd, 1)]
    others = [(d, mp) for d in group] + [(dp, planes[k]) for k in (1, 2, 3)] + [swap_with]
    bar = pltpu.get_barrier_semaphore()
    for device in others:
        pl.semaphore_signal(bar, inc=1, device_id=device, device_id_type=MESH)
    small_at[...] = jnp.zeros(small_at.shape, f32)
    small_at[0:heads, 0:cut] = bias_in[...]
    small_at[8:15, 0:vec_cut] = vec_in[...]
    ws[mp, own_j, core] = small_at[...].astype(bf16)

    def prep_mix():
        wm[mp, own_j, core] = jnp.concatenate([qkv_in[...], out_in[...].T], axis=1).astype(bf16)

    def prep_up():
        loads[0].wait()
        wu[mp, own_j, core] = up_at[...].astype(bf16)

    def prep_down():
        loads[2].wait()
        wd[mp, own_j, core] = down_at[...].astype(bf16)

    def prep_flags():
        flags = mask_in[...].astype(f32)
        flags = jnp.where(lax.rem(mp, 2) == 0, flags[:, 0:T], flags[:, T : 2 * T])
        flags = jnp.where(lax.div(mp, 2) == 0, flags[0:1, :], flags[1:2, :])
        loads[1].wait()
        fm_own[0:T, 0:width] = frames_at[...]
        fm_own[0:T, width:] = jnp.broadcast_to(flags, (128, T)).T.astype(bf16)

    def move_frames():
        hand_over(0, fm_own, fmx)

    def move_cot():
        loads[3].wait()
        cot_own[0:T, :] = cot_at[...]
        hand_over(1, cot_own, cotx)

    def unpack():
        for k in range(4):
            ag_d(SMALL, k)
        for z in range(4):
            held = [ws[z, j, c].astype(f32) for j, c in cells]
            bias[z] = jnp.concatenate([piece[0:8, 0:cut] for piece in held], axis=1)
            if z == 0:
                vec[...] = jnp.concatenate([piece[8:16, 0:vec_cut] for piece in held], axis=1)

    def vector(i):
        return vec[i : i + 1, :]

    embed, gain_one, shift_one, gain_two, shift_two, out_add, down_add = (
        functools.partial(vector, i) for i in range(7)
    )

    def masked_rows(r, n):
        flag = fmx[r : r + n, width:].astype(f32)
        return jnp.concatenate([flag] * (width // 128), axis=1) > 0.5

    def input_rows(r, n):
        return jnp.where(masked_rows(r, n), embed(), fmx[r : r + n, 0:width].astype(f32))

    def round_inputs():
        landed(fmx, move_r.at[0])
        for r, n in chunks:
            x_low[r : r + n, :] = input_rows(r, n).astype(bf16)

    def weight(ref, z, first, last):
        return ref[z, :, :, :, first:last].reshape(width, last - first)

    def add_up(piece, first):
        acc[...] = piece if first else acc[...] + piece

    def project(k):
        z = planes[k]
        ag_d(MIX, k)
        slab = jnp.dot(x_low[...], weight(wm, z, 0, qkv_wide), preferred_element_type=f32)
        for h in range(heads):
            both = bias[z, h : h + 1, 0:128]
            head = slab[:, 192 * h : 192 * h + 128] + both
            head = head.astype(bf16).astype(f32) * HD ** (-0.5)
            q_all[z, h] = jnp.where(lane < HD, head, 0.0).astype(bf16)
            pair = slab[:, 192 * h + 64 : 192 * h + 192] + jnp.where(lane < HD, 0.0, both)
            kv_own[z, h, 0:T, :] = pair.astype(bf16)
        send("kv", kv_own.at[z], kv_far.at[z], (kv_s, kv_r), (k,), (dc, mp))

    def stand(value):
        flat = value.reshape(heads * HD, T)
        return jnp.concatenate([jnp.zeros((HD, T), f32), flat], axis=0).T.astype(bf16)

    def attend(k, h):
        z = planes[k]
        if h == 0:
            landed(kv_far.at[z], kv_r.at[k])

        queries = q_all[z, h]
        own, far = kv_own[z, h, 0:T, :], kv_far[z, h, 0:T, :]
        s_own, s_far = dg(own, queries, 1, 1), dg(far, queries, 1, 1)
        peak = jnp.maximum(
            jnp.max(s_own, axis=0, keepdims=True), jnp.max(s_far, axis=0, keepdims=True)
        )
        e_own, e_far = jnp.exp(s_own - peak), jnp.exp(s_far - peak)
        total = jnp.sum(e_own, axis=0, keepdims=True) + jnp.sum(e_far, axis=0, keepdims=True)
        lse[z, h] = peak + jnp.log(total)
        scale = 1.0 / total
        mix = dg(own, (e_own * scale).astype(bf16), 0, 0)
        mix = mix + dg(far, (e_far * scale).astype(bf16), 0, 0)
        mix_t[h] = mix[HD:, :]

        if h == heads - 1:
            mixed[z] = stand(mix_t[...])

    def norm_one():
        for k in range(4):
            add_up(dg(mixed[planes[k]], weight(wm, planes[k], out_first, width), 1, 1), k == 0)
        for r, n in chunks:
            v = input_rows(r, n) + acc[r : r + n, :] + out_add()
            v = v - jnp.mean(v, axis=-1, keepdims=True)
            inverse = lax.rsqrt(jnp.mean(v * v, axis=-1, keepdims=True) + norm_eps)
            normed = v * inverse
            n_one[r : r + n, :] = normed
            r_one[r : r + n, :] = inverse
            hid_low[r : r + n, :] = (normed * gain_one() + shift_one()).astype(bf16)

    def rise(k):
        z = planes[k]
        ag_d(UP, k)
        for h in range(heads):
            cols = slice(256 * h, 256 * h + 256)
            u = jnp.dot(
                hid_low[...], weight(wu, z, 256 * h, 256 * h + 256), preferred_element_type=f32
            )
            u = u + bias[z, h : h + 1, 128:384]
            cumulative = 0.5 * (1.0 + lax.erf(u * 0.7071067811865476))
            act[z, 0:T, cols] = (u * cumulative).astype(bf16)
            bell = jnp.exp(-0.5 * u * u) * 0.3989422804014327
            slope[z, 0:T, cols] = (cumulative + u * bell).astype(bf16)

    def drop(k):
        ag_d(DOWN, k)
        add_up(dg(act[planes[k], 0:T, :], weight(wd, planes[k], 0, wide), 1, 1), k == 0)

    def norm_two():
        landed(cotx, move_r.at[1])
        sums = [jnp.zeros((1, width), f32) for _ in range(3)]
        for r, n in chunks:
            v = n_one[r : r + n, :] * gain_one() + shift_one() + acc[r : r + n, :] + down_add()
            v = v - jnp.mean(v, axis=-1, keepdims=True)
            inverse = lax.rsqrt(jnp.mean(v * v, axis=-1, keepdims=True) + norm_eps)
            normed = v * inverse
            stage_act[r : r + n, :] = normed * gain_two() + shift_two()
            up = cotx[r : r + n, :].astype(f32)
            scaled = up * gain_two()
            inner = jnp.mean(scaled * normed, axis=-1, keepdims=True)
            grad = inverse * (scaled - jnp.mean(scaled, axis=-1, keepdims=True) - normed * inner)
            acc[r : r + n, :] = grad
            low[r : r + n, :] = grad.astype(bf16)
            for i, term in enumerate((up * normed, up, grad)):
                sums[i] = sums[i] + jnp.sum(term, axis=0, keepdims=True)
        gvec[...] = jnp.zeros(gvec.shape, f32)
        gbias[...] = jnp.zeros(gbias.shape, f32)
        gvec[3:4, :], gvec[4:5, :], gvec[6:7, :] = sums

    pl.semaphore_wait(bar, len(others))
    for step, *given in (
        (ag_own, SMALL),
        (prep_mix,),
        (ag_own, MIX),
        (prep_up,),
        (prep_flags,),
        (ag_a, UP, 0),
        (prep_down,),
        (ag_a, SMALL, 0),
        (ag_a, SMALL, 3),
        (move_frames,),
        (ag_a, SMALL, 1),
        (ag_own, UP),
        (ag_a, MIX, 0),
        (ag_a, SMALL, 2),
        (ag_a, DOWN, 0),
        (ag_b, SMALL, 2),
        (ag_b, SMALL, 1),
        (ag_b, MIX, 0),
        (ag_a, MIX, 2),
        (ag_b, UP, 0),
        (ag_b, DOWN, 0),
        (ag_c, SMALL, 2),
        (ag_c, MIX, 0),
        (ag_b, SMALL, 3),
        (ag_b, SMALL, 0),
        (ag_a, MIX, 1),
        (ag_a, MIX, 3),
        (ag_c, SMALL, 3),
        (ag_c, SMALL, 1),
        (ag_c, SMALL, 0),
        (unpack,),
        (ag_a, UP, 1),
        (round_inputs,),
        (project, 0),
        (ag_own, DOWN),
        (attend, 0, 0),
        (ag_b, MIX, 3),
        (ag_c, UP, 0),
        (ag_b, MIX, 2),
        (ag_a, UP, 2),
        (ag_c, MIX, 2),
        (ag_a, UP, 3),
        (attend, 0, 1),
        (attend, 0, 2),
        (project, 2),
        (ag_b, MIX, 1),
        (ag_c, DOWN, 0),
        (ag_b, UP, 2),
        (ag_c, MIX, 3),
        (attend, 2, 0),
        (ag_a, DOWN, 2),
        (ag_b, UP, 3),
        (move_cot,),
        (attend, 2, 1),
        (ag_b, UP, 1),
        (ag_c, MIX, 1),
        (project, 3),
        (attend, 2, 2),
        (project, 1),
        (attend, 3, 0),
        (ag_a, DOWN, 3),
        (ag_c, UP, 2),
        (attend, 3, 1),
        (ag_c, UP, 1),
        (attend, 3, 2),
        (attend, 1, 0),
        (ag_a, DOWN, 1),
        (attend, 1, 1),
        (attend, 1, 2),
        (ag_b, DOWN, 2),
        (norm_one,),
        (ag_b, DOWN, 3),
        (rise, 1),
        (ag_c, UP, 3),
        (rise, 0),
        (drop, 0),
        (ag_b, DOWN, 1),
        (ag_c, DOWN, 1),
        (rise, 2),
        (rise, 3),
        (drop, 1),
        (ag_c, DOWN, 2),
        (ag_c, DOWN, 3),
        (drop, 2),
        (drop, 3),
        (norm_two,),
    ):
        step(*given)

    def tiled(value):
        return value.reshape(4, 2, -1, value.shape[1])

    def move_act():
        hand_over(2, stage_act, act_out)

    def gain_down(k):
        z = planes[k]
        gd[z] = tiled(dg(low[...], act[z, 0:T, :], 0, 0).astype(bf16))
        rs_0(DOWN, k)

    def fall(k):
        z = planes[k]
        grad = dg(low[...], weight(wd, z, 0, wide), 1, 0)
        grad = (grad * slope[z, 0:T, :].astype(f32)).astype(bf16)
        slope[z, 0:T, :] = grad
        total = jnp.sum(grad.astype(f32), axis=0, keepdims=True)
        for h in range(heads):
            gbias[z, h : h + 1, 128:384] = total[:, 256 * h : 256 * h + 256]

    def flow(k):
        z = planes[k]
        acc[...] = acc[...] + dg(slope[z, 0:T, :], weight(wu, z, 0, wide), 1, 1)

    def gain_up(k):
        sent(("ag", UP))
        z = planes[k]
        wu[z] = tiled(dg(hid_low[...], slope[z, 0:T, :], 0, 0).astype(bf16))
        rs_0(UP, k)

    def norm_back_one():
        sums = [jnp.zeros((1, width), f32) for _ in range(3)]
        for r, n in chunks:
            grad_in = acc[r : r + n, :]
            normed = n_one[r : r + n, :]
            scaled = grad_in * gain_one()
            inner = jnp.mean(scaled * normed, axis=-1, keepdims=True)
            grad = r_one[r : r + n, :] * (
                scaled - jnp.mean(scaled, axis=-1, keepdims=True) - normed * inner
            )
            acc[r : r + n, :] = grad
            low[r : r + n, :] = grad.astype(bf16)
            for i, term in enumerate((grad_in * normed, grad_in, grad)):
                sums[i] = sums[i] + jnp.sum(term, axis=0, keepdims=True)
        gvec[1:2, :], gvec[2:3, :], gvec[5:6, :] = sums

    def unmix():
        for z in planes:
            grad = dg(low[...], weight(wm, z, out_first, width), 1, 0).astype(bf16).astype(f32)
            for h in range(heads):
                if h % 2 == 0:
                    head = grad[:, HD * h : HD * h + 128]
                else:
                    piece = grad[:, HD * h + HD : HD * h + 2 * HD]
                    head = jnp.concatenate([piece, piece], axis=1)
                dm[z, h] = jnp.where(lane < HD, 0.0, head).astype(bf16)

    def attend_back(k, h):
        z = planes[k]

        queries, gm = q_all[z, h], dm[z, h]
        own, far = kv_own[z, h, 0:T, :], kv_far[z, h, 0:T, :]
        level = lse[z, h]
        p_own = jnp.exp(dg(own, queries, 1, 1) - level)
        p_far = jnp.exp(dg(far, queries, 1, 1) - level)
        g_own, g_far = dg(own, gm, 1, 1), dg(far, gm, 1, 1)
        inner = jnp.sum(p_own * g_own, axis=0, keepdims=True)
        inner = inner + jnp.sum(p_far * g_far, axis=0, keepdims=True)
        s_own = (p_own * (g_own - inner)).astype(bf16)
        s_far = (p_far * (g_far - inner)).astype(bf16)
        pair_far = jnp.dot(s_far, queries, preferred_element_type=f32)
        pair_far = pair_far + jnp.dot(p_far.astype(bf16), gm, preferred_element_type=f32)
        pair_own = jnp.dot(s_own, queries, preferred_element_type=f32)
        pair_own = pair_own + jnp.dot(p_own.astype(bf16), gm, preferred_element_type=f32)
        slope[z, 0:T, 128 * h : 128 * h + 128] = pair_far.astype(bf16)
        at = 128 * (heads + h)
        slope[z, 0:T, at : at + 128] = pair_own.astype(bf16)
        grad_q = dg(own, s_own, 0, 0) + dg(far, s_far, 0, 0)
        mix_t[h] = grad_q[0:HD, :] * HD ** (-0.5)

        if h < heads - 1:
            return
        act[z, 0:T, 0 : HD * heads] = mix_t[...].reshape(heads * HD, T).T.astype(bf16)
        send(
            "rs",
            slope.at[z, :, 0 : 128 * heads],
            far_pair.at[z],
            (kv_s, kv_r),
            (4 + k,),
            (dc, mp),
        )

    def project_back(k):
        sent(("ag", MIX))
        z = planes[k]
        landed(far_pair.at[z], kv_r.at[4 + k])
        pieces = []
        for h in range(heads):
            pieces.append(act[z, 0:T, HD * h : HD * h + HD].astype(f32))
            far = far_pair[z, 0:T, 128 * h : 128 * h + 128].astype(f32)
            at = 128 * (heads + h)
            pieces.append(far + slope[z, 0:T, at : at + 128].astype(f32))
        pieces.append(jnp.zeros((T, HD), f32))
        slab = jnp.concatenate(pieces, axis=1).astype(bf16)
        dproj[...] = slab
        total = jnp.sum(slab.astype(f32), axis=0, keepdims=True)
        for h in range(heads):
            gbias[z, h : h + 1, 0:128] = jnp.concatenate(
                [total[:, 192 * h : 192 * h + 64], total[:, 192 * h + 128 : 192 * h + 192]], axis=1
            )
        acc[...] = acc[...] + dg(dproj[...], weight(wm, z, 0, qkv_wide), 1, 1)
        grad_qkv = dg(x_low[...], dproj[...], 0, 0)
        grad_out = dg(low[...], mixed[z], 0, 0)
        wm[z, :, :, :, 0:out_first] = tiled(grad_qkv[:, 0:out_first].astype(bf16))
        both = grad_qkv[:, out_first:] + grad_out[:, 0:128]
        wm[z, :, :, :, out_first:qkv_wide] = tiled(both.astype(bf16))
        wm[z, :, :, :, qkv_wide:] = tiled(grad_out[:, 128:].astype(bf16))
        rs_0(MIX, k)

    def finish():
        embed_sum = jnp.zeros((1, width), f32)
        for r, n in chunks:
            hidden_rows = masked_rows(r, n)
            grad = acc[r : r + n, :]
            stage_fg[r : r + n, :] = jnp.where(hidden_rows, 0.0, grad)
            embed_sum = embed_sum + jnp.sum(
                jnp.where(hidden_rows, grad, 0.0), axis=0, keepdims=True
            )
        gvec[0:1, :] = embed_sum

        @pl.when(mover)
        def _():
            remote(cot_own, cotx, move_s.at[1], move_r.at[1], swap_with).wait_send()
            cot_own[0:T, :] = stage_fg[...].astype(bf16)
            remote(cot_own, fg_far, move_s.at[3], move_r.at[4], swap_with).start()

        @pl.when(stay)
        def _():
            pltpu.make_async_copy(stage_fg, fg_out, move_r.at[3]).start()

        gs[...] = jnp.zeros(gs.shape, f32)
        for d, (j, c) in enumerate(cells):
            vectors = gvec[:, vec_cut * d : vec_cut * (d + 1)]
            for z in range(4):
                gs[z, j, c, 0:4, 0:cut] = gbias[z, 0:4, cut * d : cut * (d + 1)]
                gs[z, j, c, 4:6, 0:vec_cut] = vectors[2 * z : 2 * z + 2, :]
        for k in (1, 2, 3, 0):
            rs_0(SMALL, k)

    def take_fg():
        @pl.when(mover)
        def _():
            landed(fg_far, move_r.at[4])
            stage_fg[...] = fg_far[0:T, :].astype(f32)
            pltpu.make_async_copy(stage_fg, fg_out, move_r.at[3]).start()

    for step, *given in (
        (move_act,),
        (gain_down, 3),
        (gain_down, 2),
        (fall, 2),
        (flow, 2),
        (rs_1, DOWN, 3),
        (gain_down, 1),
        (rs_1, DOWN, 2),
        (fall, 3),
        (flow, 3),
        (gain_up, 3),
        (fall, 0),
        (rs_1, DOWN, 1),
        (flow, 0),
        (fall, 1),
        (flow, 1),
        (gain_up, 1),
        (rs_2, DOWN, 2),
        (gain_down, 0),
        (rs_1, UP, 3),
        (norm_back_one,),
        (unmix,),
        (rs_1, UP, 1),
        (attend_back, 3, 0),
        (attend_back, 3, 1),
        (attend_back, 3, 2),
        (rs_3, DOWN, 2),
        (rs_2, DOWN, 3),
        (gain_up, 2),
        (rs_3, DOWN, 1),
        (project_back, 3),
        (rs_2, UP, 3),
        (attend_back, 1, 0),
        (attend_back, 1, 1),
        (rs_3, DOWN, 3),
        (rs_1, UP, 2),
        (rs_1, MIX, 3),
        (attend_back, 1, 2),
        (gain_up, 0),
        (rs_3, UP, 1),
        (attend_back, 2, 0),
        (rs_3, UP, 3),
        (project_back, 1),
        (rs_2, MIX, 3),
        (attend_back, 2, 1),
        (attend_back, 2, 2),
        (rs_1, MIX, 1),
        (rs_2, UP, 2),
        (rs_1, UP, 0),
        (project_back, 2),
        (rs_3, MIX, 3),
        (attend_back, 0, 0),
        (attend_back, 0, 1),
        (rs_1, MIX, 2),
        (rs_3, MIX, 1),
        (attend_back, 0, 2),
        (rs_1, DOWN, 0),
        (rs_3, UP, 2),
        (project_back, 0),
        (finish,),
        (rs_2, MIX, 2),
        (rs_1, SMALL, 1),
        (rs_1, SMALL, 3),
        (rs_1, SMALL, 0),
        (rs_1, SMALL, 2),
        (rs_1, MIX, 0),
        (rs_3, MIX, 2),
        (rs_2, SMALL, 3),
        (rs_2, SMALL, 1),
        (rs_2, SMALL, 2),
        (rs_2, UP, 0),
        (rs_2, DOWN, 0),
        (rs_2, MIX, 0),
        (rs_2, SMALL, 0),
        (rs_3, SMALL, 1),
        (rs_3, SMALL, 2),
        (rs_3, SMALL, 3),
        (rs_3, UP, 0),
        (rs_3, DOWN, 0),
        (rs_4, UP),
        (rs_4, DOWN),
        (rs_3, SMALL, 0),
        (take_fg,),
        (rs_3, MIX, 0),
        (rs_4, MIX),
        (rs_4, SMALL),
    ):
        step(*given)
    row_id = lax.broadcasted_iota(jnp.int32, (8, 128), 0)
    tiles[0] = jnp.where(row_id == 7, sum(squares), small_sum[...])
    for k in (1, 2, 3):
        send("end", tiles.at[0], tiles.at[k], (tile_s, tile_r), (k,), (dp, planes[k]))
    for k in (1, 2, 3):
        landed(tiles.at[k], tile_r.at[k])
    for k in range(4):
        vec_tiles[planes[k]] = tiles[k]
    tiles[4] = vec_tiles[0] + vec_tiles[1] + vec_tiles[2] + vec_tiles[3]
    for i, d in enumerate(group):
        send("end", tiles.at[4], tiles.at[5 + i], (tile_s, tile_r), (4 + i,), (d, mp))
    for i in range(7):
        landed(tiles.at[5 + i], tile_r.at[4 + i])
    pairs = [tiles[4] + tiles[5], tiles[6] + tiles[9], tiles[7] + tiles[10], tiles[8] + tiles[11]]
    norm_ref[...] = (pairs[0] + pairs[1]) + (pairs[2] + pairs[3])
    for tag in ("kv", "rs", "end", ("ag", SMALL), ("ag", DOWN)):
        sent(tag)
    landed(act_out, move_r.at[2])
    landed(fg_out, move_r.at[3])

    @pl.when(mover)
    def _():
        remote(fm_own, fmx, move_s.at[0], move_r.at[0], swap_with).wait_send()
        remote(stage_act, act_out, move_s.at[2], move_r.at[2], swap_with).wait_send()
        remote(cot_own, fg_far, move_s.at[3], move_r.at[4], swap_with).wait_send()


def run_layer(share, frames, mask, cot, qkv, out, up, down, biases, vectors):
    width = frames.shape[1]
    tall = share + -share % 16
    heads = biases.shape[0]
    rows = qkv.shape[0]
    wide = up.shape[1]
    columns = (128, width, wide, wide)
    types = (bf16,) * 4
    heights = (16, rows, rows, rows)
    weights = [
        pltpu.VMEM((4, 4, 2, n, c), t) for n, c, t in zip(heights, columns, types)
    ] + [pltpu.VMEM((4, 4, 2, 8, 128), f32), pltpu.VMEM((4, 4, 2, rows, wide), bf16)]
    pieces = list(zip((8, rows, rows, rows), columns, (f32, bf16, bf16, bf16)))
    arrivals = [
        pltpu.VMEM((*lead, n, c), t)
        for lead in ((4, 4), (4,), (4,), (4,), (3,))
        for n, c, t in pieces
    ]
    activations = [
        pltpu.VMEM((tall, width + 128), bf16),
        pltpu.VMEM((tall, width), bf16),
        pltpu.VMEM((tall, width + 128), bf16),
        pltpu.VMEM((tall, width), bf16),
        pltpu.VMEM((share, width), bf16),
        pltpu.VMEM((4, heads, share, 128), bf16),
        pltpu.VMEM((4, heads, tall, 128), bf16),
        pltpu.VMEM((4, heads, tall, 128), bf16),
        pltpu.VMEM((4, share, heads * HD + HD), bf16),
        pltpu.VMEM((4, heads, 1, share), f32),
        pltpu.VMEM((heads, HD, share), f32),
        pltpu.VMEM((share, width), f32),
        pltpu.VMEM((share, 1), f32),
        pltpu.VMEM((share, width), bf16),
        pltpu.VMEM((4, tall, wide), bf16),
        pltpu.VMEM((4, tall, wide), bf16),
        pltpu.VMEM((share, width), f32),
        pltpu.VMEM((share, width), bf16),
        pltpu.VMEM((4, heads, share, 128), bf16),
        pltpu.VMEM((share, qkv.shape[1] + HD), bf16),
        pltpu.VMEM((4, tall, 128 * heads), bf16),
        pltpu.VMEM((share, width), bf16),
        pltpu.VMEM((share, width), bf16),
        pltpu.VMEM((rows, wide), f32),
        pltpu.VMEM((rows, wide), f32),
        pltpu.VMEM((16, 128), f32),
        pltpu.VMEM((share, width), f32),
        pltpu.VMEM((share, width), f32),
        pltpu.VMEM((tall, width), bf16),
        pltpu.VMEM((8, width), f32),
        pltpu.VMEM((4, 8, 384), f32),
        pltpu.VMEM((8, width), f32),
        pltpu.VMEM((4, 8, 384), f32),
        pltpu.VMEM((12, 8, 128), f32),
    ]
    semaphores = [pltpu.SemaphoreType.DMA((4, SEMS)) for _ in range(4)] + [
        pltpu.SemaphoreType.DMA((n,)) for n in (8, 8, 5, 5, 12, 12, 4)
    ]
    anywhere = pl.BlockSpec(memory_space=pl.ANY)
    vmem = pl.BlockSpec(memory_space=pltpu.VMEM)
    shapes = [
        (share, width),
        (share, width),
        (8, 128),
        (rows, width),
        (rows, wide),
        (rows, wide),
        (8, 128),
        (4, 8, 128),
    ]
    return pl.pallas_call(
        functools.partial(layer_kernel, share),
        out_shape=tuple(jax.ShapeDtypeStruct(s, f32) for s in shapes),
        in_specs=[anywhere, vmem, anywhere, vmem, vmem, anywhere, anywhere, vmem, vmem],
        out_specs=(anywhere,) * 2 + (vmem,) * 6,
        scratch_shapes=weights + arrivals + activations + semaphores,
        compiler_params=pltpu.CompilerParams(
            collective_id=0, has_side_effects=True, vmem_limit_bytes=60 * 2**20
        ),
        name="encoder_layer",
    )(frames, mask, cot, qkv, out, up, down, biases, vectors)


def update_kernel(*refs):
    given, made = refs[:26], refs[26:47]
    held, ready = refs[47:73], refs[73:92]
    come, leave = refs[92:]
    arriving = [
        pltpu.make_async_copy(src, dst, come.at[i]) for i, (src, dst) in enumerate(zip(given, held))
    ]
    for copy in arriving:
        copy.start()
    leaving = []

    def out(src, i):
        copy = pltpu.make_async_copy(src, made[i], leave.at[i])
        copy.start()
        leaving.append(copy)

    for copy in arriving[:6]:
        copy.wait()
    small, mix, up, down, norm, vec_tiles = held[:6]
    state = held[8:]
    grad_norm = jnp.sqrt(norm[7:8, 0:1])
    ready[0][...] = grad_norm
    out(ready[0], 0)
    factor = jnp.minimum(1.0, clip_limit / (grad_norm + 1e-06))
    qkv_columns = state[0].shape[1]
    first = mix.shape[1] - state[3].shape[0] - HD
    heads, cut = state[12].shape
    vec_rows, vec_cut = state[15].shape
    gradients = (
        lambda: mix[:, 0:qkv_columns],
        lambda: mix[:, first:].T[HD:, :],
        lambda: up[...],
        lambda: down[...],
        lambda: small[0:heads, 0:cut],
        lambda: jnp.concatenate([vec_tiles[z, 4:6, 0:vec_cut] for z in range(4)], axis=0)[0:vec_rows, :],
    )
    for i in (2, 3, 0, 1, 4, 5):
        old = state[3 * i : 3 * i + 3]
        for copy in arriving[8 + 3 * i : 11 + 3 * i]:
            copy.wait()
        values = adam_step(*(ref[...] for ref in old), gradients[i](), factor, *settings[i])
        for at, value in enumerate(values):
            ready[1 + 3 * i + at][...] = value
            out(ready[1 + 3 * i + at], 3 + 3 * i + at)
    for at in range(2):
        arriving[6 + at].wait()
        out(held[6 + at], 1 + at)
    for copy in leaving:
        copy.wait()


def run_update(sums, norm, vec_tiles, act, fg, state):
    anywhere = pl.BlockSpec(memory_space=pl.ANY)
    given = (*sums, norm, vec_tiles, act, fg, *state)
    shapes = [(1, 1), act.shape, fg.shape] + [a.shape for a in state]
    return pl.pallas_call(
        update_kernel,
        out_shape=tuple(jax.ShapeDtypeStruct(s, f32) for s in shapes),
        in_specs=[anywhere] * len(given),
        out_specs=(anywhere,) * len(shapes),
        scratch_shapes=[pltpu.VMEM(a.shape, f32) for a in given]
        + [pltpu.VMEM(s, f32) for s in shapes[:1] + shapes[3:]]
        + [pltpu.SemaphoreType.DMA((len(given),)), pltpu.SemaphoreType.DMA((len(shapes),))],
        compiler_params=pltpu.CompilerParams(vmem_limit_bytes=60 * 2**20),
        name="update_weights",
    )(*given)


def on_device_fast(
    frames,
    span_mask,
    cotangent,
    qkv_weight,
    qkv_mean,
    qkv_square,
    out_weight,
    out_mean,
    out_square,
    up_weight,
    up_mean,
    up_square,
    down_weight,
    down_mean,
    down_square,
    head_biases,
    bias_mean,
    bias_square,
    norm_vectors,
    vector_mean,
    vector_square,
):
    share = frames.shape[0]
    act, fg, *sums, norm, vec_tiles = run_layer(
        share,
        frames,
        span_mask,
        cotangent,
        qkv_weight,
        out_weight,
        up_weight,
        down_weight.T,
        head_biases,
        norm_vectors,
    )
    down = (down_weight.T, down_mean.T, down_square.T)
    state = (qkv_weight, qkv_mean, qkv_square, out_weight, out_mean, out_square)
    state += (up_weight, up_mean, up_square, *down, head_biases, bias_mean, bias_square)
    state += (norm_vectors, vector_mean, vector_square)
    grad_norm, outputs, frame_grad, *updated = run_update(sums, norm, vec_tiles, act, fg, state)
    updated[9:12] = [value.T for value in updated[9:12]]
    return (outputs, frame_grad, grad_norm.reshape(()), *updated)


def solution(mesh):
    return jax.shard_map(
        on_device_fast if fast_fits(mesh) else on_device,
        mesh=mesh,
        in_specs=(
            P(("dp", "mp"), None),
            P("dp", None),
            P(("dp", "mp"), None),
            P("dp", "mp"),
            P("dp", "mp"),
            P("dp", "mp"),
            P("mp", "dp"),
            P("mp", "dp"),
            P("mp", "dp"),
            P("dp", "mp"),
            P("dp", "mp"),
            P("dp", "mp"),
            P("mp", "dp"),
            P("mp", "dp"),
            P("mp", "dp"),
            P("mp", "dp"),
            P("mp", "dp"),
            P("mp", "dp"),
            P(None, "dp"),
            P(None, "dp"),
            P(None, "dp"),
        ),
        out_specs=(
            P(("dp", "mp"), None),
            P(("dp", "mp"), None),
            P(),
            P("dp", "mp"),
            P("dp", "mp"),
            P("dp", "mp"),
            P("mp", "dp"),
            P("mp", "dp"),
            P("mp", "dp"),
            P("dp", "mp"),
            P("dp", "mp"),
            P("dp", "mp"),
            P("mp", "dp"),
            P("mp", "dp"),
            P("mp", "dp"),
            P("mp", "dp"),
            P("mp", "dp"),
            P("mp", "dp"),
            P(None, "dp"),
            P(None, "dp"),
            P(None, "dp"),
        ),
        check_vma=False,
    )
```

```python
import functools

import jax
import jax.numpy as jnp
from jax import lax
from jax.experimental import pallas as pl
from jax.experimental.pallas import tpu as pltpu
from jax.sharding import PartitionSpec as P

HD = 64
LEN = 688


norm_eps = 1e-05
adam_eps = 1e-08
beta_one = 0.9
beta_two = 0.999
step_count = 10.0
clip_limit = 1.0
settings = ((0.05, 0.1), (0.3, 0.1), (0.05, 0.1), (0.03, 0.1), (0.3, 0.0), (0.4, 0.0))


def norm_rows(values, norm_gain, norm_shift):
    centred = values - jnp.mean(values, axis=-1, keepdims=True)
    variance = jnp.mean(centred * centred, axis=-1, keepdims=True)
    inverse = lax.rsqrt(variance + norm_eps)
    normed = centred * inverse
    return (normed * norm_gain + norm_shift, normed, inverse)


def norm_back(upstream, normed, inverse, norm_gain):
    scaled = upstream * norm_gain
    inner_part = (
        scaled
        - jnp.mean(scaled, axis=-1, keepdims=True)
        - normed * jnp.mean(scaled * normed, axis=-1, keepdims=True)
    )
    return (inverse * inner_part, jnp.sum(upstream * normed, axis=0), jnp.sum(upstream, axis=0))


def gelu_slope(pre_act):
    cumulative = 0.5 * (1.0 + jax.scipy.special.erf(pre_act * 0.7071067811865476))
    return cumulative + pre_act * jnp.exp(-0.5 * pre_act * pre_act) * 0.3989422804014327


def attend_forward(clip_block):
    scaling = HD ** (-0.5)
    queries = clip_block[:, :, 0]
    key_rows = clip_block[:, :, 1]
    value_rows = clip_block[:, :, 2]
    scores = (
        jnp.einsum("qhe,khe->hqk", queries, key_rows, preferred_element_type=jnp.float32) * scaling
    )
    row_peak = jnp.max(scores, axis=-1, keepdims=True)
    log_total = row_peak + jnp.log(jnp.sum(jnp.exp(scores - row_peak), axis=-1, keepdims=True))
    attention = jnp.exp(scores - log_total).astype(jnp.bfloat16)
    mixed_rows = jnp.einsum(
        "hqk,khe->qhe", attention, value_rows, preferred_element_type=jnp.float32
    )
    return (mixed_rows.astype(jnp.bfloat16).reshape(clip_block.shape[0], -1), log_total)


def attend_backward(pieces):
    clip_block, log_total, grad_mixed = pieces
    scaling = HD ** (-0.5)
    queries = clip_block[:, :, 0]
    key_rows = clip_block[:, :, 1]
    value_rows = clip_block[:, :, 2]
    scores = (
        jnp.einsum("qhe,khe->hqk", queries, key_rows, preferred_element_type=jnp.float32) * scaling
    )
    attention = jnp.exp(scores - log_total)
    attention_low = attention.astype(jnp.bfloat16)
    mixed_rows = jnp.einsum(
        "hqk,khe->qhe", attention_low, value_rows, preferred_element_type=jnp.float32
    ).astype(jnp.bfloat16)
    grad_rows = grad_mixed.reshape(queries.shape)
    grad_attention = jnp.einsum(
        "qhe,khe->hqk", grad_rows, value_rows, preferred_element_type=jnp.float32
    )
    grad_values = jnp.einsum(
        "hqk,qhe->khe", attention_low, grad_rows, preferred_element_type=jnp.float32
    )
    row_inner = jnp.sum(attention * grad_attention, axis=-1, keepdims=True)
    grad_scores = (attention * (grad_attention - row_inner)).astype(jnp.bfloat16)
    grad_queries = (
        jnp.einsum("hqk,khe->qhe", grad_scores, key_rows, preferred_element_type=jnp.float32)
        * scaling
    )
    grad_keys = (
        jnp.einsum("hqk,qhe->khe", grad_scores, queries, preferred_element_type=jnp.float32)
        * scaling
    )
    grad_block = jnp.stack([grad_queries, grad_keys, grad_values], axis=2).astype(jnp.bfloat16)
    return (
        mixed_rows.reshape(clip_block.shape[0], -1),
        grad_block.reshape(clip_block.shape[0], -1),
    )


def adam_step(weight, mean_old, square_old, gradient, factor, rate, decay):
    clipped = gradient * factor
    mean_new = beta_one * mean_old + (1.0 - beta_one) * clipped
    square_new = beta_two * square_old + (1.0 - beta_two) * clipped * clipped
    mean_hat = mean_new / (1.0 - beta_one**step_count)
    square_hat = square_new / (1.0 - beta_two**step_count)
    weight_new = weight - rate * (mean_hat / (jnp.sqrt(square_hat) + adam_eps) + decay * weight)
    return (weight_new, mean_new, square_new)


def on_device(
    frames,
    span_mask,
    cotangent,
    qkv_weight,
    qkv_mean,
    qkv_square,
    out_weight,
    out_mean,
    out_square,
    up_weight,
    up_mean,
    up_square,
    down_weight,
    down_mean,
    down_square,
    head_biases,
    bias_mean,
    bias_square,
    norm_vectors,
    vector_mean,
    vector_square,
):
    masters = (qkv_weight, out_weight, up_weight, down_weight, head_biases, norm_vectors)
    lowered = tuple((weight.astype(jnp.bfloat16) for weight in masters))
    qkv_full, out_full, up_full, down_full, bias_full, vector_full = (
        lax.all_gather(lowered[0], "dp", axis=0, tiled=True),
        lax.all_gather(lowered[1], "dp", axis=1, tiled=True),
        lax.all_gather(lowered[2], "dp", axis=0, tiled=True),
        lax.all_gather(lowered[3], "dp", axis=1, tiled=True),
        lax.all_gather(lowered[4], "dp", axis=1, tiled=True),
        lax.all_gather(lowered[5], "dp", axis=1, tiled=True),
    )
    share_rows = frames.shape[0]
    start_row = lax.axis_index("mp") * share_rows
    vectors = vector_full.astype(jnp.float32)
    local_heads = bias_full.shape[0]

    def share_of(array_full):
        return lax.dynamic_slice_in_dim(array_full, start_row, share_rows, 0)

    gathered = lax.all_gather(frames, "mp", axis=0, tiled=True)
    all_rows = gathered.shape[0]
    masked = span_mask.reshape(all_rows, 1) == 1
    inputs = jnp.where(masked, vectors[0], gathered.astype(jnp.float32))
    rounded = inputs.astype(jnp.bfloat16)
    zero_bias = jnp.zeros_like(bias_full[:, :HD])
    qkv_bias = (
        jnp.stack([bias_full[:, :HD], zero_bias, bias_full[:, HD : 2 * HD]], axis=1)
        .reshape(-1)
        .astype(jnp.float32)
    )
    up_bias = bias_full[:, 2 * HD :].reshape(-1).astype(jnp.float32)
    projected = (jnp.dot(rounded, qkv_full, preferred_element_type=jnp.float32) + qkv_bias).astype(
        jnp.bfloat16
    )
    blocks = projected.reshape(-1, LEN, local_heads, 3, HD)
    mixed_rows, log_total = lax.map(attend_forward, blocks)
    mixed_rows = mixed_rows.reshape(all_rows, -1)
    attn_part = jnp.dot(mixed_rows, out_full, preferred_element_type=jnp.float32)
    attended = lax.psum(attn_part, "mp")
    first_sum = inputs + attended + vectors[5]
    hidden, normed_full, inverse_full = norm_rows(first_sum, vectors[1], vectors[2])
    normed_one = share_of(normed_full)
    inverse_one = share_of(inverse_full)
    hidden_low = hidden.astype(jnp.bfloat16)
    pre_act = jnp.dot(hidden_low, up_full, preferred_element_type=jnp.float32) + up_bias
    activated = jax.nn.gelu(pre_act, approximate=False).astype(jnp.bfloat16)
    ffn_part = jnp.dot(activated, down_full, preferred_element_type=jnp.float32)
    second_sum = hidden + lax.psum(ffn_part, "mp") + vectors[6]
    outputs_full, normed_full, inverse_full = norm_rows(second_sum, vectors[3], vectors[4])
    outputs = share_of(outputs_full)
    normed_two = share_of(normed_full)
    inverse_two = share_of(inverse_full)
    qkv_full, out_full, up_full, down_full, bias_full, vector_full = (
        lax.all_gather(lowered[0], "dp", axis=0, tiled=True),
        lax.all_gather(lowered[1], "dp", axis=1, tiled=True),
        lax.all_gather(lowered[2], "dp", axis=0, tiled=True),
        lax.all_gather(lowered[3], "dp", axis=1, tiled=True),
        lax.all_gather(lowered[4], "dp", axis=1, tiled=True),
        lax.all_gather(lowered[5], "dp", axis=1, tiled=True),
    )
    upstream = cotangent.astype(jnp.float32)
    grad_two, grad_gain_two, grad_shift_two = norm_back(
        upstream, normed_two, inverse_two, vectors[3]
    )
    grad_down_bias = jnp.sum(grad_two, axis=0)
    grad_two_full = lax.all_gather(grad_two.astype(jnp.bfloat16), "mp", axis=0, tiled=True)
    pre_again = jnp.dot(hidden_low, up_full, preferred_element_type=jnp.float32) + up_bias
    act_again = jax.nn.gelu(pre_again, approximate=False).astype(jnp.bfloat16)
    grad_down = jnp.einsum(
        "tf,td->fd", act_again, grad_two_full, preferred_element_type=jnp.float32
    )
    grad_act = jnp.einsum("td,fd->tf", grad_two_full, down_full, preferred_element_type=jnp.float32)
    grad_pre = (grad_act * gelu_slope(pre_again)).astype(jnp.bfloat16)
    grad_up = jnp.einsum("td,tf->df", hidden_low, grad_pre, preferred_element_type=jnp.float32)
    grad_up_bias = jnp.sum(grad_pre, axis=0, dtype=jnp.float32)
    hidden_part = jnp.einsum("tf,df->td", grad_pre, up_full, preferred_element_type=jnp.float32)
    grad_hidden = grad_two + lax.psum_scatter(hidden_part, "mp", scatter_dimension=0, tiled=True)
    grad_one, grad_gain_one, grad_shift_one = norm_back(
        grad_hidden, normed_one, inverse_one, vectors[1]
    )
    grad_out_bias = jnp.sum(grad_one, axis=0)
    grad_one_full = lax.all_gather(grad_one.astype(jnp.bfloat16), "mp", axis=0, tiled=True)
    grad_mixed = jnp.einsum(
        "td,cd->tc", grad_one_full, out_full, preferred_element_type=jnp.float32
    ).astype(jnp.bfloat16)
    mixed_again, grad_blocks = lax.map(
        attend_backward, (blocks, log_total, grad_mixed.reshape(-1, LEN, grad_mixed.shape[1]))
    )
    mixed_again = mixed_again.reshape(all_rows, -1)
    grad_blocks = grad_blocks.reshape(all_rows, -1)
    grad_out = jnp.einsum(
        "tc,td->cd", mixed_again, grad_one_full, preferred_element_type=jnp.float32
    )
    grad_qkv = jnp.einsum("td,tc->dc", rounded, grad_blocks, preferred_element_type=jnp.float32)
    bias_sums = jnp.sum(grad_blocks, axis=0, dtype=jnp.float32).reshape(local_heads, 3, HD)
    grad_biases = jnp.concatenate(
        [bias_sums[:, 0], bias_sums[:, 2], grad_up_bias.reshape(local_heads, -1)], axis=1
    )
    input_part = jnp.einsum("tc,dc->td", grad_blocks, qkv_full, preferred_element_type=jnp.float32)
    grad_inputs = grad_one + lax.psum_scatter(
        input_part.astype(jnp.bfloat16), "mp", scatter_dimension=0, tiled=True
    ).astype(jnp.float32)
    masked_share = share_of(masked)
    grad_embed = jnp.sum(jnp.where(masked_share, grad_inputs, 0.0), axis=0)
    frame_grad = jnp.where(masked_share, 0.0, grad_inputs)
    grad_vectors = jnp.stack(
        [
            grad_embed,
            grad_gain_one,
            grad_shift_one,
            grad_gain_two,
            grad_shift_two,
            grad_out_bias,
            grad_down_bias,
        ]
    )
    reduced = (
        lax.psum_scatter(grad_qkv, "dp", scatter_dimension=0, tiled=True),
        lax.psum_scatter(grad_out, "dp", scatter_dimension=1, tiled=True),
        lax.psum_scatter(grad_up, "dp", scatter_dimension=0, tiled=True),
        lax.psum_scatter(grad_down, "dp", scatter_dimension=1, tiled=True),
        lax.psum_scatter(grad_biases, "dp", scatter_dimension=1, tiled=True),
    )
    local_squares = jnp.float32(0.0)
    for portion in reduced:
        local_squares = local_squares + jnp.sum(portion * portion)
    total_squares, vector_total = lax.psum((local_squares, grad_vectors), ("dp", "mp"))
    grad_norm = jnp.sqrt(total_squares + jnp.sum(vector_total * vector_total))
    column_count = norm_vectors.shape[1]
    vector_grad = lax.dynamic_slice_in_dim(
        vector_total, lax.axis_index("dp") * column_count, column_count, 1
    )
    factor = jnp.minimum(1.0, clip_limit / (grad_norm + 1e-06))
    gradients = (reduced[0], reduced[1], reduced[2], reduced[3], reduced[4], vector_grad)
    means = (qkv_mean, out_mean, up_mean, down_mean, bias_mean, vector_mean)
    squares = (qkv_square, out_square, up_square, down_square, bias_square, vector_square)
    updated = []
    for index_at in range(6):
        updated.extend(
            adam_step(
                masters[index_at],
                means[index_at],
                squares[index_at],
                gradients[index_at],
                factor,
                settings[index_at][0],
                settings[index_at][1],
            )
        )
    return (
        outputs,
        frame_grad,
        grad_norm,
        updated[0],
        updated[1],
        updated[2],
        updated[3],
        updated[4],
        updated[5],
        updated[6],
        updated[7],
        updated[8],
        updated[9],
        updated[10],
        updated[11],
        updated[12],
        updated[13],
        updated[14],
        updated[15],
        updated[16],
        updated[17],
    )


MESH = pl.DeviceIdType.MESH
SMALL, MIX, UP, DOWN = range(4)
SEMS = 32
f32, bf16 = jnp.float32, jnp.bfloat16


def fast_fits(mesh):
    return mesh.shape["dp"] == 8 and mesh.shape["mp"] == 4


def flip(dp, bit):
    held = lax.rem(lax.div(dp, bit), 2)
    return dp + bit - 2 * bit * held


def dg(a, b, ca, cb):
    return lax.dot_general(a, b, (((ca,), (cb,)), ((), ())), preferred_element_type=f32)


def landed(dst, sem):
    pltpu.make_async_copy(dst, dst, sem).wait()


def layer_kernel(
    share,
    frames_in,
    mask_in,
    cot_in,
    qkv_in,
    out_in,
    up_in,
    down_in,
    bias_in,
    vec_in,
    act_out,
    fg_out,
    small_sum,
    mix_sum,
    up_sum,
    down_sum,
    norm_ref,
    vec_tiles,
    ws,
    wm,
    wu,
    wd,
    gs,
    gd,
    rcs,
    rcm,
    rcu,
    rcd,
    rds,
    rdm,
    rdu,
    rdd,
    rxs,
    rxm,
    rxu,
    rxd,
    rys,
    rym,
    ryu,
    ryd,
    rzs,
    rzm,
    rzu,
    rzd,
    fm_own,
    cot_own,
    fmx,
    cotx,
    x_low,
    q_all,
    kv_own,
    kv_far,
    mixed,
    lse,
    mix_t,
    n_one,
    r_one,
    hid_low,
    act,
    slope,
    acc,
    low,
    dm,
    dproj,
    far_pair,
    frames_at,
    cot_at,
    up_at,
    down_at,
    small_at,
    stage_act,
    stage_fg,
    fg_far,
    vec,
    bias,
    gvec,
    gbias,
    tiles,
    gather_s,
    gather_r,
    reduce_s,
    reduce_r,
    kv_s,
    kv_r,
    move_s,
    move_r,
    tile_s,
    tile_r,
    load_s,
):
    T = share
    dp, mp = lax.axis_index("dp"), lax.axis_index("mp")
    core = lax.rem(dp, 2)
    dx, dy, dc = flip(dp, 2), flip(dp, 4), flip(dp, 1)
    dd = flip(dx, 4)
    planes = (mp, flip(mp, 1), flip(mp, 2), flip(flip(mp, 1), 2))
    mover = lax.rem(core + mp, 2) == 1
    stay = lax.rem(core + mp, 2) == 0
    swap_with = (dc, planes[1])
    full = (ws, wm, wu, wd)
    local = (gs, wm, wu, gd)
    from_core = (rcs, rcm, rcu, rcd)
    from_diag = (rds, rdm, rdu, rdd)
    from_x = (rxs, rxm, rxu, rxd)
    from_y = (rys, rym, ryu, ryd)
    from_z = (rzs, rzm, rzu, rzd)
    result = (small_sum, mix_sum, up_sum, down_sum)
    heads = q_all.shape[1]
    chunks = [(r, min(88, T - r)) for r in range(0, T, 88)]

    def remote(src, dst, send_sem, recv_sem, device):
        return pltpu.make_async_remote_copy(
            src_ref=src,
            dst_ref=dst,
            send_sem=send_sem,
            recv_sem=recv_sem,
            device_id=device,
            device_id_type=MESH,
        )

    pending = {}

    def send(tag, src, dst, sems, at, device):
        copy = remote(src, dst, sems[0].at[at], sems[1].at[at], device)
        copy.start()
        pending.setdefault(tag, []).append(copy)

    def sent(tag):
        for copy in pending.pop(tag, []):
            copy.wait_send()

    def hand_over(slot, src, dst):
        @pl.when(mover)
        def _():
            remote(src, dst, move_s.at[slot], move_r.at[slot], swap_with).start()

        @pl.when(stay)
        def _():
            pltpu.make_async_copy(src, dst, move_r.at[slot]).start()

    def halves(ref):
        n = ref.shape[-2] // 2
        return ref.at[pl.ds(0, n)], ref.at[pl.ds(n, n)]

    gather = (gather_s, gather_r)

    def slot(w, k, d):
        return full[w].at[planes[k], lax.div(d, 2), lax.rem(d, 2)]

    def ag_own(w):
        for k in (1, 2, 3):
            send(("ag", w), slot(w, 0, dp), slot(w, 0, dp), gather, (w, k), (dp, planes[k]))

    def ag_a(w, k):
        ref = slot(w, k, dp)
        if k:
            landed(ref, gather_r.at[w, k])
        send(("ag", w), ref, ref, gather, (w, 4 + k), (dx, mp))
        send(("ag", w), ref, ref, gather, (w, 8 + k), (dy, mp))

    own_j, x_j, y_j, d_j = (lax.div(d, 2) for d in (dp, dx, dy, dd))
    row_j = 2 * lax.div(own_j, 2)

    def to_core(w, k, cells, at):
        ref = full[w].at[planes[k], cells, core]
        send(("ag", w), ref, ref, gather, (w, at), (dc, mp))

    def ag_b(w, k):
        at_x, at_y = slot(w, k, dx), slot(w, k, dy)
        landed(at_x, gather_r.at[w, 4 + k])
        if k == 2 or (w == SMALL and k == 0):
            send(("ag", w), at_x, at_x, gather, (w, 12 + k), (dy, mp))
        elif k == 0:
            ref = halves(at_x)[0]
            send(("ag", w), ref, ref, gather, (w, 12), (dy, mp))
        if w == DOWN:
            to_core(w, k, pl.ds(row_j, 2), 17 + k)
        landed(at_y, gather_r.at[w, 8 + k])
        if k == 3 or (w == SMALL and k == 1):
            send(("ag", w), at_y, at_y, gather, (w, 12 + k), (dx, mp))
        elif k == 0 and w != SMALL:
            ref = halves(at_y)[1]
            send(("ag", w), ref, ref, gather, (w, 13), (dx, mp))
        if w == DOWN:
            to_core(w, k, y_j, 21 + k)

    def ag_c(w, k):
        ref = slot(w, k, dd)
        if w == SMALL or k > 1:
            landed(ref, gather_r.at[w, 12 + k])
        elif k == 0:
            for i, half in enumerate(halves(ref)):
                landed(half, gather_r.at[w, 12 + i])
            send(("ag", w), ref, ref, gather, (w, 16), (dp, planes[1]))
        else:
            landed(ref, gather_r.at[w, 16])
        if w == DOWN:
            to_core(w, k, d_j, 25 + k)
        else:
            to_core(w, k, slice(None), 17 + k)

    def ag_d(w, k):
        if w == DOWN:
            for cells, at in ((pl.ds(row_j, 2), 17), (y_j, 21), (d_j, 25)):
                landed(full[w].at[planes[k], cells, 1 - core], gather_r.at[w, at + k])
        else:
            landed(full[w].at[planes[k], :, 1 - core], gather_r.at[w, 17 + k])

    squares = []
    reduce = (reduce_s, reduce_r)

    def part(w, k, d):
        return local[w].at[planes[k], lax.div(d, 2), lax.rem(d, 2)]

    def add_to(ref, arrived):
        ref[...] = ref[...] + arrived[...]

    def rs_0(w, k):
        send("rs", local[w].at[planes[k], :, 1 - core], from_core[w].at[k], reduce, (w, k), (dc, mp))

    def rs_1(w, k):
        landed(from_core[w].at[k], reduce_r.at[w, k])
        add_to(local[w].at[planes[k], :, core], from_core[w].at[k])
        at_d, at_x, at_y = part(w, k, dd), part(w, k, dx), part(w, k, dy)
        to_d, to_x, to_y = from_diag[w].at[k], from_x[w].at[k], from_y[w].at[k]
        if w == SMALL or k > 1:
            if k % 2:
                send("rs", at_d, to_d, reduce, (w, 4 + k), (dx, mp))
                send("rs", at_x, to_x, reduce, (w, 10 + k), (dx, mp))
            else:
                send("rs", at_d, to_d, reduce, (w, 4 + k), (dy, mp))
                send("rs", at_y, to_y, reduce, (w, 15 + k), (dy, mp))
        elif k == 1:
            send("rs", at_d, to_d, reduce, (w, 4), (dp, planes[1]))
            send("rs", at_x, to_x, reduce, (w, 10 + k), (dx, mp))
            send("rs", at_y, to_y, reduce, (w, 15 + k), (dy, mp))
        else:
            landed(from_diag[w].at[1], reduce_r.at[w, 4])
            add_to(at_d, from_diag[w].at[1])
            send("rs", halves(at_d)[0], halves(to_d)[0], reduce, (w, 8), (dx, mp))
            send("rs", halves(at_d)[1], halves(to_d)[1], reduce, (w, 9), (dy, mp))
            send("rs", halves(at_x)[0], halves(to_x)[0], reduce, (w, 10), (dx, mp))
            send("rs", halves(at_y)[1], halves(to_y)[1], reduce, (w, 15), (dy, mp))

    def rs_2(w, k):
        at_x, at_y = part(w, k, dx), part(w, k, dy)
        come, to_x, to_y = from_diag[w].at[k], from_x[w].at[k], from_y[w].at[k]
        if w == SMALL or k > 1:
            landed(come, reduce_r.at[w, 4 + k])
            if k % 2:
                add_to(at_y, come)
                send("rs", at_y, to_y, reduce, (w, 15 + k), (dy, mp))
            else:
                add_to(at_x, come)
                send("rs", at_x, to_x, reduce, (w, 10 + k), (dx, mp))
        else:
            first, second = halves(come)
            landed(first, reduce_r.at[w, 8])
            add_to(halves(at_y)[0], first)
            send("rs", halves(at_y)[0], halves(to_y)[0], reduce, (w, 19), (dy, mp))
            landed(second, reduce_r.at[w, 9])
            add_to(halves(at_x)[1], second)
            send("rs", halves(at_x)[1], halves(to_x)[1], reduce, (w, 14), (dx, mp))

    def rs_3(w, k):
        if w == SMALL or k:
            landed(from_x[w].at[k], reduce_r.at[w, 10 + k])
            landed(from_y[w].at[k], reduce_r.at[w, 15 + k])
        else:
            for half, at in zip(halves(from_x[w].at[0]), (10, 14)):
                landed(half, reduce_r.at[w, at])
            for half, at in zip(halves(from_y[w].at[0]), (19, 15)):
                landed(half, reduce_r.at[w, at])
        ref = part(w, k, dp)
        total = ref[...].astype(f32) + from_x[w][k].astype(f32) + from_y[w][k].astype(f32)
        if k:
            ref[...] = total.astype(ref.dtype)
            send("rs", ref, from_z[w].at[k - 1], reduce, (w, 19 + k), (dp, planes[k]))
        else:
            result[w][...] = total

    def rs_4(w):
        total = result[w][...]
        for k in (1, 2, 3):
            landed(from_z[w].at[k - 1], reduce_r.at[w, 19 + k])
            total = total + from_z[w][k - 1].astype(f32)
        result[w][...] = total
        squares.append(jnp.sum(total * total))

    loads = [
        pltpu.make_async_copy(src, dst, load_s.at[i])
        for i, (src, dst) in enumerate(
            ((up_in, up_at), (frames_in, frames_at), (down_in, down_at), (cot_in, cot_at))
        )
    ]
    for copy in loads:
        copy.start()
    cut, vec_cut = bias_in.shape[1], vec_in.shape[1]
    width, wide = frames_in.shape[1], up_in.shape[1]
    qkv_wide = 192 * heads + 64
    out_first = 192 * heads - 64
    lane = lax.broadcasted_iota(jnp.int32, (1, 128), 1)
    cells = [(j, c) for j in range(4) for c in range(2)]
    group = [dc, dx, dy, dd, flip(dx, 1), flip(dy, 1), flip(dd, 1)]
    others = [(d, mp) for d in group] + [(dp, planes[k]) for k in (1, 2, 3)] + [swap_with]
    bar = pltpu.get_barrier_semaphore()
    for device in others:
        pl.semaphore_signal(bar, inc=1, device_id=device, device_id_type=MESH)
    small_at[...] = jnp.zeros(small_at.shape, f32)
    small_at[0:heads, 0:cut] = bias_in[...]
    small_at[8:15, 0:vec_cut] = vec_in[...]
    ws[mp, own_j, core] = small_at[...].astype(bf16)

    def prep_mix():
        wm[mp, own_j, core] = jnp.concatenate([qkv_in[...], out_in[...].T], axis=1).astype(bf16)

    def prep_up():
        loads[0].wait()
        wu[mp, own_j, core] = up_at[...].astype(bf16)

    def prep_down():
        loads[2].wait()
        wd[mp, own_j, core] = down_at[...].astype(bf16)

    def prep_flags():
        flags = mask_in[...].astype(f32)
        flags = jnp.where(lax.rem(mp, 2) == 0, flags[:, 0:T], flags[:, T : 2 * T])
        flags = jnp.where(lax.div(mp, 2) == 0, flags[0:1, :], flags[1:2, :])
        loads[1].wait()
        fm_own[0:T, 0:width] = frames_at[...]
        fm_own[0:T, width:] = jnp.broadcast_to(flags, (128, T)).T.astype(bf16)

    def move_frames():
        hand_over(0, fm_own, fmx)

    def move_cot():
        loads[3].wait()
        cot_own[0:T, :] = cot_at[...]
        hand_over(1, cot_own, cotx)

    def unpack():
        for k in range(4):
            ag_d(SMALL, k)
        for z in range(4):
            held = [ws[z, j, c].astype(f32) for j, c in cells]
            bias[z] = jnp.concatenate([piece[0:8, 0:cut] for piece in held], axis=1)
            if z == 0:
                vec[...] = jnp.concatenate([piece[8:16, 0:vec_cut] for piece in held], axis=1)

    def vector(i):
        return vec[i : i + 1, :]

    embed, gain_one, shift_one, gain_two, shift_two, out_add, down_add = (
        functools.partial(vector, i) for i in range(7)
    )

    def masked_rows(r, n):
        flag = fmx[r : r + n, width:].astype(f32)
        return jnp.concatenate([flag] * (width // 128), axis=1) > 0.5

    def input_rows(r, n):
        return jnp.where(masked_rows(r, n), embed(), fmx[r : r + n, 0:width].astype(f32))

    def round_inputs():
        landed(fmx, move_r.at[0])
        for r, n in chunks:
            x_low[r : r + n, :] = input_rows(r, n).astype(bf16)

    def weight(ref, z, first, last):
        return ref[z, :, :, :, first:last].reshape(width, last - first)

    def add_up(piece, first):
        acc[...] = piece if first else acc[...] + piece

    def project(k):
        z = planes[k]
        ag_d(MIX, k)
        slab = jnp.dot(x_low[...], weight(wm, z, 0, qkv_wide), preferred_element_type=f32)
        for h in range(heads):
            both = bias[z, h : h + 1, 0:128]
            head = slab[:, 192 * h : 192 * h + 128] + both
            head = head.astype(bf16).astype(f32) * HD ** (-0.5)
            q_all[z, h] = jnp.where(lane < HD, head, 0.0).astype(bf16)
            pair = slab[:, 192 * h + 64 : 192 * h + 192] + jnp.where(lane < HD, 0.0, both)
            kv_own[z, h, 0:T, :] = pair.astype(bf16)
        send("kv", kv_own.at[z], kv_far.at[z], (kv_s, kv_r), (k,), (dc, mp))

    def stand(value):
        flat = value.reshape(heads * HD, T)
        return jnp.concatenate([jnp.zeros((HD, T), f32), flat], axis=0).T.astype(bf16)

    def attend(k, h):
        z = planes[k]
        if h == 0:
            landed(kv_far.at[z], kv_r.at[k])

        queries = q_all[z, h]
        own, far = kv_own[z, h, 0:T, :], kv_far[z, h, 0:T, :]
        s_own, s_far = dg(own, queries, 1, 1), dg(far, queries, 1, 1)
        peak = jnp.maximum(
            jnp.max(s_own, axis=0, keepdims=True), jnp.max(s_far, axis=0, keepdims=True)
        )
        e_own, e_far = jnp.exp(s_own - peak), jnp.exp(s_far - peak)
        total = jnp.sum(e_own, axis=0, keepdims=True) + jnp.sum(e_far, axis=0, keepdims=True)
        lse[z, h] = peak + jnp.log(total)
        scale = 1.0 / total
        mix = dg(own, (e_own * scale).astype(bf16), 0, 0)
        mix = mix + dg(far, (e_far * scale).astype(bf16), 0, 0)
        mix_t[h] = mix[HD:, :]

        if h == heads - 1:
            mixed[z] = stand(mix_t[...])

    def norm_one():
        for k in range(4):
            add_up(dg(mixed[planes[k]], weight(wm, planes[k], out_first, width), 1, 1), k == 0)
        for r, n in chunks:
            v = input_rows(r, n) + acc[r : r + n, :] + out_add()
            v = v - jnp.mean(v, axis=-1, keepdims=True)
            inverse = lax.rsqrt(jnp.mean(v * v, axis=-1, keepdims=True) + norm_eps)
            normed = v * inverse
            n_one[r : r + n, :] = normed
            r_one[r : r + n, :] = inverse
            hid_low[r : r + n, :] = (normed * gain_one() + shift_one()).astype(bf16)

    def rise(k):
        z = planes[k]
        ag_d(UP, k)
        for h in range(heads):
            cols = slice(256 * h, 256 * h + 256)
            u = jnp.dot(
                hid_low[...], weight(wu, z, 256 * h, 256 * h + 256), preferred_element_type=f32
            )
            u = u + bias[z, h : h + 1, 128:384]
            cumulative = 0.5 * (1.0 + lax.erf(u * 0.7071067811865476))
            act[z, 0:T, cols] = (u * cumulative).astype(bf16)
            bell = jnp.exp(-0.5 * u * u) * 0.3989422804014327
            slope[z, 0:T, cols] = (cumulative + u * bell).astype(bf16)

    def drop(k):
        ag_d(DOWN, k)
        add_up(dg(act[planes[k], 0:T, :], weight(wd, planes[k], 0, wide), 1, 1), k == 0)

    def norm_two():
        landed(cotx, move_r.at[1])
        sums = [jnp.zeros((1, width), f32) for _ in range(3)]
        for r, n in chunks:
            v = n_one[r : r + n, :] * gain_one() + shift_one() + acc[r : r + n, :] + down_add()
            v = v - jnp.mean(v, axis=-1, keepdims=True)
            inverse = lax.rsqrt(jnp.mean(v * v, axis=-1, keepdims=True) + norm_eps)
            normed = v * inverse
            stage_act[r : r + n, :] = normed * gain_two() + shift_two()
            up = cotx[r : r + n, :].astype(f32)
            scaled = up * gain_two()
            inner = jnp.mean(scaled * normed, axis=-1, keepdims=True)
            grad = inverse * (scaled - jnp.mean(scaled, axis=-1, keepdims=True) - normed * inner)
            acc[r : r + n, :] = grad
            low[r : r + n, :] = grad.astype(bf16)
            for i, term in enumerate((up * normed, up, grad)):
                sums[i] = sums[i] + jnp.sum(term, axis=0, keepdims=True)
        gvec[...] = jnp.zeros(gvec.shape, f32)
        gbias[...] = jnp.zeros(gbias.shape, f32)
        gvec[3:4, :], gvec[4:5, :], gvec[6:7, :] = sums

    pl.semaphore_wait(bar, len(others))
    for step, *given in (
        (ag_own, SMALL),
        (prep_mix,),
        (ag_own, MIX),
        (prep_up,),
        (prep_flags,),
        (ag_a, UP, 0),
        (prep_down,),
        (ag_a, SMALL, 0),
        (ag_a, SMALL, 3),
        (move_frames,),
        (ag_a, SMALL, 1),
        (ag_own, UP),
        (ag_a, MIX, 0),
        (ag_a, SMALL, 2),
        (ag_a, DOWN, 0),
        (ag_b, SMALL, 2),
        (ag_b, SMALL, 1),
        (ag_b, MIX, 0),
        (ag_a, MIX, 2),
        (ag_b, UP, 0),
        (ag_b, DOWN, 0),
        (ag_c, SMALL, 2),
        (ag_c, MIX, 0),
        (ag_b, SMALL, 3),
        (ag_b, SMALL, 0),
        (ag_a, MIX, 1),
        (ag_a, MIX, 3),
        (ag_c, SMALL, 3),
        (ag_c, SMALL, 1),
        (ag_c, SMALL, 0),
        (unpack,),
        (ag_a, UP, 1),
        (round_inputs,),
        (project, 0),
        (ag_own, DOWN),
        (attend, 0, 0),
        (ag_b, MIX, 3),
        (ag_c, UP, 0),
        (ag_b, MIX, 2),
        (ag_a, UP, 2),
        (ag_c, MIX, 2),
        (ag_a, UP, 3),
        (attend, 0, 1),
        (attend, 0, 2),
        (project, 2),
        (ag_b, MIX, 1),
        (ag_c, DOWN, 0),
        (ag_b, UP, 2),
        (ag_c, MIX, 3),
        (attend, 2, 0),
        (ag_a, DOWN, 2),
        (ag_b, UP, 3),
        (move_cot,),
        (attend, 2, 1),
        (ag_b, UP, 1),
        (ag_c, MIX, 1),
        (project, 3),
        (attend, 2, 2),
        (project, 1),
        (attend, 3, 0),
        (ag_a, DOWN, 3),
        (ag_c, UP, 2),
        (attend, 3, 1),
        (ag_c, UP, 1),
        (attend, 3, 2),
        (attend, 1, 0),
        (ag_a, DOWN, 1),
        (attend, 1, 1),
        (attend, 1, 2),
        (ag_b, DOWN, 2),
        (norm_one,),
        (ag_b, DOWN, 3),
        (rise, 1),
        (ag_c, UP, 3),
        (rise, 0),
        (drop, 0),
        (ag_b, DOWN, 1),
        (ag_c, DOWN, 1),
        (rise, 2),
        (rise, 3),
        (drop, 1),
        (ag_c, DOWN, 2),
        (ag_c, DOWN, 3),
        (drop, 2),
        (drop, 3),
        (norm_two,),
    ):
        step(*given)

    def tiled(value):
        return value.reshape(4, 2, -1, value.shape[1])

    def move_act():
        hand_over(2, stage_act, act_out)

    def gain_down(k):
        z = planes[k]
        gd[z] = tiled(dg(low[...], act[z, 0:T, :], 0, 0).astype(bf16))
        rs_0(DOWN, k)

    def fall(k):
        z = planes[k]
        grad = dg(low[...], weight(wd, z, 0, wide), 1, 0)
        grad = (grad * slope[z, 0:T, :].astype(f32)).astype(bf16)
        slope[z, 0:T, :] = grad
        total = jnp.sum(grad.astype(f32), axis=0, keepdims=True)
        for h in range(heads):
            gbias[z, h : h + 1, 128:384] = total[:, 256 * h : 256 * h + 256]

    def flow(k):
        z = planes[k]
        acc[...] = acc[...] + dg(slope[z, 0:T, :], weight(wu, z, 0, wide), 1, 1)

    def gain_up(k):
        sent(("ag", UP))
        z = planes[k]
        wu[z] = tiled(dg(hid_low[...], slope[z, 0:T, :], 0, 0).astype(bf16))
        rs_0(UP, k)

    def norm_back_one():
        sums = [jnp.zeros((1, width), f32) for _ in range(3)]
        for r, n in chunks:
            grad_in = acc[r : r + n, :]
            normed = n_one[r : r + n, :]
            scaled = grad_in * gain_one()
            inner = jnp.mean(scaled * normed, axis=-1, keepdims=True)
            grad = r_one[r : r + n, :] * (
                scaled - jnp.mean(scaled, axis=-1, keepdims=True) - normed * inner
            )
            acc[r : r + n, :] = grad
            low[r : r + n, :] = grad.astype(bf16)
            for i, term in enumerate((grad_in * normed, grad_in, grad)):
                sums[i] = sums[i] + jnp.sum(term, axis=0, keepdims=True)
        gvec[1:2, :], gvec[2:3, :], gvec[5:6, :] = sums

    def unmix():
        for z in planes:
            grad = dg(low[...], weight(wm, z, out_first, width), 1, 0).astype(bf16).astype(f32)
            for h in range(heads):
                if h % 2 == 0:
                    head = grad[:, HD * h : HD * h + 128]
                else:
                    piece = grad[:, HD * h + HD : HD * h + 2 * HD]
                    head = jnp.concatenate([piece, piece], axis=1)
                dm[z, h] = jnp.where(lane < HD, 0.0, head).astype(bf16)

    def attend_back(k, h):
        z = planes[k]

        queries, gm = q_all[z, h], dm[z, h]
        own, far = kv_own[z, h, 0:T, :], kv_far[z, h, 0:T, :]
        level = lse[z, h]
        p_own = jnp.exp(dg(own, queries, 1, 1) - level)
        p_far = jnp.exp(dg(far, queries, 1, 1) - level)
        g_own, g_far = dg(own, gm, 1, 1), dg(far, gm, 1, 1)
        inner = jnp.sum(p_own * g_own, axis=0, keepdims=True)
        inner = inner + jnp.sum(p_far * g_far, axis=0, keepdims=True)
        s_own = (p_own * (g_own - inner)).astype(bf16)
        s_far = (p_far * (g_far - inner)).astype(bf16)
        pair_far = jnp.dot(s_far, queries, preferred_element_type=f32)
        pair_far = pair_far + jnp.dot(p_far.astype(bf16), gm, preferred_element_type=f32)
        pair_own = jnp.dot(s_own, queries, preferred_element_type=f32)
        pair_own = pair_own + jnp.dot(p_own.astype(bf16), gm, preferred_element_type=f32)
        slope[z, 0:T, 128 * h : 128 * h + 128] = pair_far.astype(bf16)
        at = 128 * (heads + h)
        slope[z, 0:T, at : at + 128] = pair_own.astype(bf16)
        grad_q = dg(own, s_own, 0, 0) + dg(far, s_far, 0, 0)
        mix_t[h] = grad_q[0:HD, :] * HD ** (-0.5)

        if h < heads - 1:
            return
        act[z, 0:T, 0 : HD * heads] = mix_t[...].reshape(heads * HD, T).T.astype(bf16)
        send(
            "rs",
            slope.at[z, :, 0 : 128 * heads],
            far_pair.at[z],
            (kv_s, kv_r),
            (4 + k,),
            (dc, mp),
        )

    def project_back(k):
        sent(("ag", MIX))
        z = planes[k]
        landed(far_pair.at[z], kv_r.at[4 + k])
        pieces = []
        for h in range(heads):
            pieces.append(act[z, 0:T, HD * h : HD * h + HD].astype(f32))
            far = far_pair[z, 0:T, 128 * h : 128 * h + 128].astype(f32)
            at = 128 * (heads + h)
            pieces.append(far + slope[z, 0:T, at : at + 128].astype(f32))
        pieces.append(jnp.zeros((T, HD), f32))
        slab = jnp.concatenate(pieces, axis=1).astype(bf16)
        dproj[...] = slab
        total = jnp.sum(slab.astype(f32), axis=0, keepdims=True)
        for h in range(heads):
            gbias[z, h : h + 1, 0:128] = jnp.concatenate(
                [total[:, 192 * h : 192 * h + 64], total[:, 192 * h + 128 : 192 * h + 192]], axis=1
            )
        acc[...] = acc[...] + dg(dproj[...], weight(wm, z, 0, qkv_wide), 1, 1)
        grad_qkv = dg(x_low[...], dproj[...], 0, 0)
        grad_out = dg(low[...], mixed[z], 0, 0)
        wm[z, :, :, :, 0:out_first] = tiled(grad_qkv[:, 0:out_first].astype(bf16))
        both = grad_qkv[:, out_first:] + grad_out[:, 0:128]
        wm[z, :, :, :, out_first:qkv_wide] = tiled(both.astype(bf16))
        wm[z, :, :, :, qkv_wide:] = tiled(grad_out[:, 128:].astype(bf16))
        rs_0(MIX, k)

    def finish():
        embed_sum = jnp.zeros((1, width), f32)
        for r, n in chunks:
            hidden_rows = masked_rows(r, n)
            grad = acc[r : r + n, :]
            stage_fg[r : r + n, :] = jnp.where(hidden_rows, 0.0, grad)
            embed_sum = embed_sum + jnp.sum(
                jnp.where(hidden_rows, grad, 0.0), axis=0, keepdims=True
            )
        gvec[0:1, :] = embed_sum

        @pl.when(mover)
        def _():
            remote(cot_own, cotx, move_s.at[1], move_r.at[1], swap_with).wait_send()
            cot_own[0:T, :] = stage_fg[...].astype(bf16)
            remote(cot_own, fg_far, move_s.at[3], move_r.at[4], swap_with).start()

        @pl.when(stay)
        def _():
            pltpu.make_async_copy(stage_fg, fg_out, move_r.at[3]).start()

        gs[...] = jnp.zeros(gs.shape, f32)
        for d, (j, c) in enumerate(cells):
            vectors = gvec[:, vec_cut * d : vec_cut * (d + 1)]
            for z in range(4):
                gs[z, j, c, 0:4, 0:cut] = gbias[z, 0:4, cut * d : cut * (d + 1)]
                gs[z, j, c, 4:6, 0:vec_cut] = vectors[2 * z : 2 * z + 2, :]
        for k in (1, 2, 3, 0):
            rs_0(SMALL, k)

    def take_fg():
        @pl.when(mover)
        def _():
            landed(fg_far, move_r.at[4])
            stage_fg[...] = fg_far[0:T, :].astype(f32)
            pltpu.make_async_copy(stage_fg, fg_out, move_r.at[3]).start()

    for step, *given in (
        (move_act,),
        (gain_down, 3),
        (gain_down, 2),
        (fall, 2),
        (flow, 2),
        (rs_1, DOWN, 3),
        (gain_down, 1),
        (rs_1, DOWN, 2),
        (fall, 3),
        (flow, 3),
        (gain_up, 3),
        (fall, 0),
        (rs_1, DOWN, 1),
        (flow, 0),
        (fall, 1),
        (flow, 1),
        (gain_up, 1),
        (rs_2, DOWN, 2),
        (gain_down, 0),
        (rs_1, UP, 3),
        (norm_back_one,),
        (unmix,),
        (rs_1, UP, 1),
        (attend_back, 3, 0),
        (attend_back, 3, 1),
        (attend_back, 3, 2),
        (rs_3, DOWN, 2),
        (rs_2, DOWN, 3),
        (gain_up, 2),
        (rs_3, DOWN, 1),
        (project_back, 3),
        (rs_2, UP, 3),
        (attend_back, 1, 0),
        (attend_back, 1, 1),
        (rs_3, DOWN, 3),
        (rs_1, UP, 2),
        (rs_1, MIX, 3),
        (attend_back, 1, 2),
        (gain_up, 0),
        (rs_3, UP, 1),
        (attend_back, 2, 0),
        (rs_3, UP, 3),
        (project_back, 1),
        (rs_2, MIX, 3),
        (attend_back, 2, 1),
        (attend_back, 2, 2),
        (rs_1, MIX, 1),
        (rs_2, UP, 2),
        (rs_1, UP, 0),
        (project_back, 2),
        (rs_3, MIX, 3),
        (attend_back, 0, 0),
        (attend_back, 0, 1),
        (rs_1, MIX, 2),
        (rs_3, MIX, 1),
        (attend_back, 0, 2),
        (rs_1, DOWN, 0),
        (rs_3, UP, 2),
        (project_back, 0),
        (finish,),
        (rs_2, MIX, 2),
        (rs_1, SMALL, 1),
        (rs_1, SMALL, 3),
        (rs_1, SMALL, 0),
        (rs_1, SMALL, 2),
        (rs_1, MIX, 0),
        (rs_3, MIX, 2),
        (rs_2, SMALL, 3),
        (rs_2, SMALL, 1),
        (rs_2, SMALL, 2),
        (rs_2, UP, 0),
        (rs_2, DOWN, 0),
        (rs_2, MIX, 0),
        (rs_2, SMALL, 0),
        (rs_3, SMALL, 1),
        (rs_3, SMALL, 2),
        (rs_3, SMALL, 3),
        (rs_3, UP, 0),
        (rs_3, DOWN, 0),
        (rs_4, UP),
        (rs_4, DOWN),
        (rs_3, SMALL, 0),
        (take_fg,),
        (rs_3, MIX, 0),
        (rs_4, MIX),
        (rs_4, SMALL),
    ):
        step(*given)
    row_id = lax.broadcasted_iota(jnp.int32, (8, 128), 0)
    tiles[0] = jnp.where(row_id == 7, sum(squares), small_sum[...])
    for k in (1, 2, 3):
        send("end", tiles.at[0], tiles.at[k], (tile_s, tile_r), (k,), (dp, planes[k]))
    for k in (1, 2, 3):
        landed(tiles.at[k], tile_r.at[k])
    for k in range(4):
        vec_tiles[planes[k]] = tiles[k]
    tiles[4] = vec_tiles[0] + vec_tiles[1] + vec_tiles[2] + vec_tiles[3]
    for i, d in enumerate(group):
        send("end", tiles.at[4], tiles.at[5 + i], (tile_s, tile_r), (4 + i,), (d, mp))
    for i in range(7):
        landed(tiles.at[5 + i], tile_r.at[4 + i])
    pairs = [tiles[4] + tiles[5], tiles[6] + tiles[9], tiles[7] + tiles[10], tiles[8] + tiles[11]]
    norm_ref[...] = (pairs[0] + pairs[1]) + (pairs[2] + pairs[3])
    for tag in ("kv", "rs", "end", ("ag", SMALL), ("ag", DOWN)):
        sent(tag)
    landed(act_out, move_r.at[2])
    landed(fg_out, move_r.at[3])

    @pl.when(mover)
    def _():
        remote(fm_own, fmx, move_s.at[0], move_r.at[0], swap_with).wait_send()
        remote(stage_act, act_out, move_s.at[2], move_r.at[2], swap_with).wait_send()
        remote(cot_own, fg_far, move_s.at[3], move_r.at[4], swap_with).wait_send()


def run_layer(share, frames, mask, cot, qkv, out, up, down, biases, vectors):
    width = frames.shape[1]
    tall = share + -share % 16
    heads = biases.shape[0]
    rows = qkv.shape[0]
    wide = up.shape[1]
    columns = (128, width, wide, wide)
    types = (bf16,) * 4
    heights = (16, rows, rows, rows)
    weights = [
        pltpu.VMEM((4, 4, 2, n, c), t) for n, c, t in zip(heights, columns, types)
    ] + [pltpu.VMEM((4, 4, 2, 8, 128), f32), pltpu.VMEM((4, 4, 2, rows, wide), bf16)]
    pieces = list(zip((8, rows, rows, rows), columns, (f32, bf16, bf16, bf16)))
    arrivals = [
        pltpu.VMEM((*lead, n, c), t)
        for lead in ((4, 4), (4,), (4,), (4,), (3,))
        for n, c, t in pieces
    ]
    activations = [
        pltpu.VMEM((tall, width + 128), bf16),
        pltpu.VMEM((tall, width), bf16),
        pltpu.VMEM((tall, width + 128), bf16),
        pltpu.VMEM((tall, width), bf16),
        pltpu.VMEM((share, width), bf16),
        pltpu.VMEM((4, heads, share, 128), bf16),
        pltpu.VMEM((4, heads, tall, 128), bf16),
        pltpu.VMEM((4, heads, tall, 128), bf16),
        pltpu.VMEM((4, share, heads * HD + HD), bf16),
        pltpu.VMEM((4, heads, 1, share), f32),
        pltpu.VMEM((heads, HD, share), f32),
        pltpu.VMEM((share, width), f32),
        pltpu.VMEM((share, 1), f32),
        pltpu.VMEM((share, width), bf16),
        pltpu.VMEM((4, tall, wide), bf16),
        pltpu.VMEM((4, tall, wide), bf16),
        pltpu.VMEM((share, width), f32),
        pltpu.VMEM((share, width), bf16),
        pltpu.VMEM((4, heads, share, 128), bf16),
        pltpu.VMEM((share, qkv.shape[1] + HD), bf16),
        pltpu.VMEM((4, tall, 128 * heads), bf16),
        pltpu.VMEM((share, width), bf16),
        pltpu.VMEM((share, width), bf16),
        pltpu.VMEM((rows, wide), f32),
        pltpu.VMEM((rows, wide), f32),
        pltpu.VMEM((16, 128), f32),
        pltpu.VMEM((share, width), f32),
        pltpu.VMEM((share, width), f32),
        pltpu.VMEM((tall, width), bf16),
        pltpu.VMEM((8, width), f32),
        pltpu.VMEM((4, 8, 384), f32),
        pltpu.VMEM((8, width), f32),
        pltpu.VMEM((4, 8, 384), f32),
        pltpu.VMEM((12, 8, 128), f32),
    ]
    semaphores = [pltpu.SemaphoreType.DMA((4, SEMS)) for _ in range(4)] + [
        pltpu.SemaphoreType.DMA((n,)) for n in (8, 8, 5, 5, 12, 12, 4)
    ]
    anywhere = pl.BlockSpec(memory_space=pl.ANY)
    vmem = pl.BlockSpec(memory_space=pltpu.VMEM)
    shapes = [
        (share, width),
        (share, width),
        (8, 128),
        (rows, width),
        (rows, wide),
        (rows, wide),
        (8, 128),
        (4, 8, 128),
    ]
    return pl.pallas_call(
        functools.partial(layer_kernel, share),
        out_shape=tuple(jax.ShapeDtypeStruct(s, f32) for s in shapes),
        in_specs=[anywhere, vmem, anywhere, vmem, vmem, anywhere, anywhere, vmem, vmem],
        out_specs=(anywhere,) * 2 + (vmem,) * 6,
        scratch_shapes=weights + arrivals + activations + semaphores,
        compiler_params=pltpu.CompilerParams(
            collective_id=0, has_side_effects=True, vmem_limit_bytes=60 * 2**20
        ),
        name="encoder_layer",
    )(frames, mask, cot, qkv, out, up, down, biases, vectors)


def update_kernel(*refs):
    given, made = refs[:26], refs[26:47]
    held, ready = refs[47:73], refs[73:92]
    come, leave = refs[92:]
    arriving = [
        pltpu.make_async_copy(src, dst, come.at[i]) for i, (src, dst) in enumerate(zip(given, held))
    ]
    first_used = arriving[:6] + arriving[14:17] + arriving[6:8]
    for copy in first_used + arriving[17:20] + arriving[8:14] + arriving[20:]:
        copy.start()
    leaving = []

    def out(src, i):
        copy = pltpu.make_async_copy(src, made[i], leave.at[i])
        copy.start()
        leaving.append(copy)

    for copy in arriving[:6]:
        copy.wait()
    small, mix, up, down, norm, vec_tiles = held[:6]
    state = held[8:]
    grad_norm = jnp.sqrt(norm[7:8, 0:1])
    ready[0][...] = grad_norm
    out(ready[0], 0)
    factor = jnp.minimum(1.0, clip_limit / (grad_norm + 1e-06))
    qkv_columns = state[0].shape[1]
    first = mix.shape[1] - state[3].shape[0] - HD
    heads, cut = state[12].shape
    vec_rows, vec_cut = state[15].shape
    gradients = (
        lambda: mix[:, 0:qkv_columns],
        lambda: mix[:, first:].T[HD:, :],
        lambda: up[...],
        lambda: down[...],
        lambda: small[0:heads, 0:cut],
        lambda: jnp.concatenate([vec_tiles[z, 4:6, 0:vec_cut] for z in range(4)], axis=0)[0:vec_rows, :],
    )
    for i in (2, 3, 0, 1, 4, 5):
        old = state[3 * i : 3 * i + 3]
        for copy in arriving[8 + 3 * i : 11 + 3 * i]:
            copy.wait()
        values = adam_step(*(ref[...] for ref in old), gradients[i](), factor, *settings[i])
        for at, value in enumerate(values):
            ready[1 + 3 * i + at][...] = value
            out(ready[1 + 3 * i + at], 3 + 3 * i + at)
        if i == 2:
            for at in range(2):
                arriving[6 + at].wait()
                out(held[6 + at], 1 + at)
    for copy in leaving:
        copy.wait()


def run_update(sums, norm, vec_tiles, act, fg, state):
    anywhere = pl.BlockSpec(memory_space=pl.ANY)
    given = (*sums, norm, vec_tiles, act, fg, *state)
    shapes = [(1, 1), act.shape, fg.shape] + [a.shape for a in state]
    return pl.pallas_call(
        update_kernel,
        out_shape=tuple(jax.ShapeDtypeStruct(s, f32) for s in shapes),
        in_specs=[anywhere] * len(given),
        out_specs=(anywhere,) * len(shapes),
        scratch_shapes=[pltpu.VMEM(a.shape, f32) for a in given]
        + [pltpu.VMEM(s, f32) for s in shapes[:1] + shapes[3:]]
        + [pltpu.SemaphoreType.DMA((len(given),)), pltpu.SemaphoreType.DMA((len(shapes),))],
        compiler_params=pltpu.CompilerParams(vmem_limit_bytes=60 * 2**20),
        name="update_weights",
    )(*given)


def on_device_fast(
    frames,
    span_mask,
    cotangent,
    qkv_weight,
    qkv_mean,
    qkv_square,
    out_weight,
    out_mean,
    out_square,
    up_weight,
    up_mean,
    up_square,
    down_weight,
    down_mean,
    down_square,
    head_biases,
    bias_mean,
    bias_square,
    norm_vectors,
    vector_mean,
    vector_square,
):
    share = frames.shape[0]
    act, fg, *sums, norm, vec_tiles = run_layer(
        share,
        frames,
        span_mask,
        cotangent,
        qkv_weight,
        out_weight,
        up_weight,
        down_weight.T,
        head_biases,
        norm_vectors,
    )
    down = (down_weight.T, down_mean.T, down_square.T)
    state = (qkv_weight, qkv_mean, qkv_square, out_weight, out_mean, out_square)
    state += (up_weight, up_mean, up_square, *down, head_biases, bias_mean, bias_square)
    state += (norm_vectors, vector_mean, vector_square)
    grad_norm, outputs, frame_grad, *updated = run_update(sums, norm, vec_tiles, act, fg, state)
    updated[9:12] = [value.T for value in updated[9:12]]
    return (outputs, frame_grad, grad_norm.reshape(()), *updated)


def solution(mesh):
    return jax.shard_map(
        on_device_fast if fast_fits(mesh) else on_device,
        mesh=mesh,
        in_specs=(
            P(("dp", "mp"), None),
            P("dp", None),
            P(("dp", "mp"), None),
            P("dp", "mp"),
            P("dp", "mp"),
            P("dp", "mp"),
            P("mp", "dp"),
            P("mp", "dp"),
            P("mp", "dp"),
            P("dp", "mp"),
            P("dp", "mp"),
            P("dp", "mp"),
            P("mp", "dp"),
            P("mp", "dp"),
            P("mp", "dp"),
            P("mp", "dp"),
            P("mp", "dp"),
            P("mp", "dp"),
            P(None, "dp"),
            P(None, "dp"),
            P(None, "dp"),
        ),
        out_specs=(
            P(("dp", "mp"), None),
            P(("dp", "mp"), None),
            P(),
            P("dp", "mp"),
            P("dp", "mp"),
            P("dp", "mp"),
            P("mp", "dp"),
            P("mp", "dp"),
            P("mp", "dp"),
            P("dp", "mp"),
            P("dp", "mp"),
            P("dp", "mp"),
            P("mp", "dp"),
            P("mp", "dp"),
            P("mp", "dp"),
            P("mp", "dp"),
            P("mp", "dp"),
            P("mp", "dp"),
            P(None, "dp"),
            P(None, "dp"),
            P(None, "dp"),
        ),
        check_vma=False,
    )
```
